32 devices in a mesh: tile: 8 (over z, y), grp: 4 (over x, core).
Axes of the slice: x: 2, y: 2, z: 4, core: 2. Of those that a mesh axis runs over, the one named last changes fastest.
Arguments:
- amplitudes: bfloat16 [256, 4096], P('grp', 'tile'), may hold values from -6 to 6
- driver: float32 [256, 4096], P('grp', 'tile'), may hold values from -6 to 6
- pair_energy: float32 [256], P('grp'), may hold values from -3 to -0.5
- virt_energy: float32 [4096], P('tile'), may hold values from 1 to 4
- integrals: bfloat16 [7680, 128, 128], P(('tile', 'grp')), may hold values from -0.03125 to 0.03125
- src_block: int32 [7680], P('tile'), may hold values from 0 to 31
- dst_block: int32 [7680], P('tile'), may hold values from 0 to 3
Outputs:
- new_amplitudes: bfloat16 [256, 4096], P('grp', 'tile')
The draws below stay inside these ranges and needn't reach their ends.
All inputs are finite; a program needn't handle non-finite values.
Results may differ from the reference program's by a relative error of at most 0.0027.
Values may be sent and summed in bfloat16 or wider, within the bound.
No kernel may reach another device: no remote copies, remote signals or barrier semaphores. Data moves between devices by JAX's collectives and lax.ppermute only.
A program may use at most 192 MiB of HBM per device.

```python
import jax
import jax.numpy as jnp
from jax import lax

TB = 128
BLK_DEV = 4
ITERS = 2
NB = 32
P_SIZE = 256
NNZ_TILE = 960
N_TILE = 8


def plant(array, own_key, least, high):
    longest = array.shape.index(max(array.shape))
    spots = []
    for shift in (0, 1):
        where = [jax.random.randint(jax.random.fold_in(own_key, axis), (), 0, length) for axis, length in enumerate(array.shape)]
        where[longest] = (where[longest] + shift) % array.shape[longest]
        spots.append(tuple(where))
    return array.at[spots[0]].set(least).at[spots[1]].set(high)


def steps_of(rng, dims, split, low, top_value):
    def one(position, shards_of):
        heights = jax.random.uniform(jax.random.fold_in(jax.random.fold_in(rng, 6), position), (shards_of,), jnp.float32, low / len(split), top_value / len(split))
        return jnp.repeat(jnp.exp(heights), dims[position] // shards_of).reshape((-1,) + (1,) * (len(dims) - position - 1))

    level = one(*split[0])
    for cut in split[1:]:
        level = level * one(*cut)
    return level


def centred(key, shape, deviation, most, shards=(), kind=jnp.bfloat16):
    gain = steps_of(key, shape, shards, -0.22, 0.18) if shards else 1.0
    result = jax.random.normal(key, shape, jnp.float32) * deviation * gain
    return jnp.minimum(jnp.maximum(result, -most), most).astype(kind)


def setup_inputs(seed: int = 0) -> dict:
    seeds = jax.random.split(jax.random.key(seed), 8)
    return {
        "amplitudes": centred(seeds[0], (P_SIZE, NB * TB), 1.0, 6.0, ((0, 4), (1, 8))),
        "driver": centred(seeds[1], (P_SIZE, NB * TB), 1.0, 6.0, ((0, 4), (1, 8)), jnp.float32),
        "pair_energy": jnp.clip(-3.0 + 2.5 * jax.random.uniform(seeds[2], (P_SIZE,), jnp.float32) ** steps_of(seeds[2], (P_SIZE,), ((0, 4),), -0.2, 0.2), -3.0, -0.5),
        "virt_energy": jnp.clip(1.0 + 3.0 * jax.random.uniform(seeds[3], (NB * TB,), jnp.float32) ** steps_of(seeds[3], (NB * TB,), ((0, 8),), -0.2, 0.2), 1.0, 4.0),
        "integrals": centred(seeds[4], (N_TILE * NNZ_TILE, TB, TB), (TB * NNZ_TILE // BLK_DEV) ** -0.5, 0.03125, ((0, 32),)),
        "src_block": plant(jax.random.randint(seeds[5], (N_TILE * NNZ_TILE,), 0, NB), jax.random.fold_in(seeds[5], 1), 0, NB - 1).astype(jnp.int32),
        "dst_block": plant(jax.random.randint(seeds[6], (N_TILE * NNZ_TILE,), 0, BLK_DEV), jax.random.fold_in(seeds[6], 1), 0, BLK_DEV - 1).astype(jnp.int32),
    }


def contract(amp_rows, tile_set, source, target, local_blocks):
    row_count = amp_rows.shape[0]
    tile_width = tile_set.shape[1]
    blocks = amp_rows.reshape(row_count, -1, tile_width)
    picked = jnp.take(blocks, source, axis=1).astype(jnp.float32)
    partial_value = jnp.einsum("rgc,gcd->rgd", picked, tile_set.astype(jnp.float32))
    onehot = (target[:, None] == jnp.arange(local_blocks, dtype=jnp.int32)[None, :]).astype(jnp.float32)
    return jnp.einsum("rgd,gb->rbd", partial_value, onehot, precision=lax.Precision.HIGHEST)


def ladder_term(amp_rows, integrals, src_block, dst_block):
    tile_groups = integrals.reshape(N_TILE, NNZ_TILE, TB, TB)
    source_groups = src_block.reshape(N_TILE, NNZ_TILE)
    target_groups = dst_block.reshape(N_TILE, NNZ_TILE)

    def per_device(packed):
        return contract(amp_rows, packed[0], packed[1], packed[2], BLK_DEV)

    stacked = lax.map(per_device, (tile_groups, source_groups, target_groups))
    return jnp.transpose(stacked, (1, 0, 2, 3)).reshape(amp_rows.shape[0], NB * TB)


def reference(amplitudes, driver, pair_energy, virt_energy, integrals, src_block, dst_block):
    denominator = virt_energy[None, :] - pair_energy[:, None]
    current = amplitudes
    for iteration in range(ITERS):
        ladder = ladder_term(current, integrals, src_block, dst_block)
        current = ((driver + ladder) / denominator).astype(jnp.bfloat16)
    return current
```

```python
import functools
import math

import jax
import jax.numpy as jnp
from jax import lax
from jax.experimental import pallas as pl
from jax.experimental.pallas import tpu as pltpu
from jax.sharding import PartitionSpec as P

ITERS = 2
MIB = 1024 * 1024


def contract_blocks(amp_rows, tile_set, source, target, local_blocks):
    row_count = amp_rows.shape[0]
    tile_width = tile_set.shape[1]
    tile_count = tile_set.shape[0]
    group_size = math.gcd(tile_count, 48)
    turns = tile_count // group_size
    blocks = amp_rows.reshape(row_count, -1, tile_width)
    packed_tiles = tile_set.reshape(turns, group_size, tile_width, tile_width)
    packed_source = source.reshape(turns, group_size)
    packed_target = target.reshape(turns, group_size)

    def advance(total_sum, packed):
        picked = jnp.take(blocks, packed[1], axis=1)
        partial_value = jnp.einsum(
            "rgc,gcd->rgd", picked, packed[0], preferred_element_type=jnp.float32
        )
        pieces = []
        for block in range(local_blocks):
            chosen = (packed[2] == block)[None, :, None]
            pieces.append(jnp.sum(jnp.where(chosen, partial_value, 0.0), axis=1))
        return (total_sum + jnp.stack(pieces, axis=1), None)

    initial = jnp.zeros((row_count, local_blocks, tile_width), jnp.float32)
    total_sum, unused = lax.scan(advance, initial, (packed_tiles, packed_source, packed_target))
    return total_sum.reshape(row_count, local_blocks * tile_width)


def general_form(amplitudes, driver, pair_energy, virt_energy, integrals, src_block, dst_block):
    tile_width = integrals.shape[1]
    local_blocks = virt_energy.shape[0] // tile_width
    denominator = virt_energy[None, :] - pair_energy[:, None]
    current = amplitudes
    first_tile = lax.axis_index("grp") * integrals.shape[0]
    my_source = lax.dynamic_slice_in_dim(src_block, first_tile, integrals.shape[0])
    my_target = lax.dynamic_slice_in_dim(dst_block, first_tile, integrals.shape[0])
    for iteration in range(ITERS):
        all_pairs = lax.all_gather(current, "grp", axis=0, tiled=True)
        whole_panel = lax.all_gather(all_pairs, "tile", axis=1, tiled=True)
        partial_value = contract_blocks(whole_panel, integrals, my_source, my_target, local_blocks)
        ladder = lax.psum_scatter(partial_value, "grp", scatter_dimension=0, tiled=True)
        current = ((driver + ladder) / denominator).astype(jnp.bfloat16)
    return current


NZ, NY, NX, NC = 4, 2, 2, 2


def z_shift(steps):
    return [(z * NY + y, (z + steps) % NZ * NY + y) for z in range(NZ) for y in range(NY)]


Y_SWAP = [(t, t ^ 1) for t in range(NZ * NY)]
X_SWAP = [(g, g ^ 2) for g in range(NX * NC)]
CORE_SWAP = [(g, g ^ 1) for g in range(NX * NC)]


def gather_panel(shard):
    rows, columns = shard.shape
    by_z = jnp.stack([shard] + [lax.ppermute(shard, "tile", z_shift(s)) for s in range(1, NZ)])
    by_y = jnp.concatenate([by_z, lax.ppermute(by_z, "tile", Y_SWAP)])
    by_x = jnp.stack([by_y, lax.ppermute(by_y, "grp", X_SWAP)])
    return by_x, lax.ppermute(by_x, "grp", CORE_SWAP)


def densify_kernel(chunk, local_blocks, src, dst, place, tiles, high, low, total):
    step = pl.program_id(0)
    blocks = total.shape[0] // local_blocks

    @pl.when(step == 0)
    def _():
        total[...] = jnp.zeros_like(total)

    tile, grp = place[0], place[1]
    z, y = tile // NY, lax.rem(tile, NY)
    first = grp * (chunk * pl.num_programs(0)) + step * chunk

    def add(k, carry):
        source = src[first + k]
        owner = source // local_blocks
        away_z = lax.rem(z - owner // NY + NZ, NZ)
        away_y = lax.rem(y + owner, NY)
        block = (away_y * NZ + away_z) * local_blocks + lax.rem(source, local_blocks)
        slot = block * local_blocks + dst[first + k]
        total[slot] += tiles[k].astype(jnp.float32)
        return carry

    lax.fori_loop(0, chunk, add, 0, unroll=4)

    @pl.when(step == pl.num_programs(0) - 1)
    def _():
        width = total.shape[-1]

        def split(block, carry):
            for d in range(local_blocks):
                value = total[block * local_blocks + d]
                top = value.astype(jnp.bfloat16)
                rest = value - top.astype(jnp.float32)
                high[block, :, d * width : (d + 1) * width] = top
                low[block, :, d * width : (d + 1) * width] = rest.astype(jnp.bfloat16)
            return carry

        lax.fori_loop(0, blocks, split, 0)


def densify(integrals, src_block, dst_block, local_blocks, blocks):
    count, width, _ = integrals.shape
    chunk = math.gcd(count, 24)
    place = jnp.stack([lax.axis_index("tile"), lax.axis_index("grp")]).astype(jnp.int32)
    shape = jax.ShapeDtypeStruct((blocks, width, local_blocks * width), jnp.bfloat16)
    whole = pl.BlockSpec(shape.shape, lambda i, *_: (0, 0, 0))
    high, low = pl.pallas_call(
        functools.partial(densify_kernel, chunk, local_blocks),
        grid_spec=pltpu.PrefetchScalarGridSpec(
            num_scalar_prefetch=3,
            grid=(count // chunk,),
            in_specs=[pl.BlockSpec((chunk, width, width), lambda i, *_: (i, 0, 0))],
            out_specs=[whole, whole],
            scratch_shapes=[pltpu.VMEM((blocks * local_blocks, width, width), jnp.float32)],
        ),
        out_shape=[shape, shape],
        compiler_params=pltpu.CompilerParams(vmem_limit_bytes=40 * MIB),
        cost_estimate=pl.CostEstimate(
            flops=count * width * width, bytes_accessed=2 * count * width * width + 8 * blocks * local_blocks * width * width, transcendentals=0
        ),
        name="densify",
    )(src_block, dst_block, place, integrals)
    return high.reshape(-1, local_blocks * width), low.reshape(-1, local_blocks * width)


def contract_kernel(mine, other, high, low, keep, send):
    @pl.when(pl.program_id(0) == 0)
    def _():
        keep[...] = jnp.zeros_like(keep)
        send[...] = jnp.zeros_like(send)

    depth = mine.shape[-1]
    half = keep.shape[0]
    rows = jnp.concatenate([mine[...].reshape(half, depth), other[...].reshape(half, depth)], axis=0)
    part = jnp.dot(rows, high[...], preferred_element_type=jnp.float32)
    part += jnp.dot(rows, low[...], preferred_element_type=jnp.float32)
    keep[...] += part[:half]
    send[...] += part[half:]


def contract(mine, other, high, low):
    across, steps, rows, depth = mine.shape
    columns = high.shape[1]
    amp = pl.BlockSpec((across, 1, rows, depth), lambda i: (0, i, 0, 0))
    matrix = pl.BlockSpec((depth, columns), lambda i: (i, 0))
    out = pl.BlockSpec((across * rows, columns), lambda i: (0, 0))
    shape = jax.ShapeDtypeStruct((across * rows, columns), jnp.float32)
    return pl.pallas_call(
        contract_kernel,
        grid=(steps,),
        in_specs=[amp, amp, matrix, matrix],
        out_specs=[out, out],
        out_shape=[shape, shape],
        compiler_params=pltpu.CompilerParams(vmem_limit_bytes=40 * MIB),
        cost_estimate=pl.CostEstimate(
            flops=8 * across * rows * steps * depth * columns,
            bytes_accessed=4 * steps * depth * columns + 4 * across * rows * steps * depth + 8 * across * rows * columns,
            transcendentals=0,
        ),
        name="contract",
    )(mine, other, high, low)


def on_device(amplitudes, driver, pair_energy, virt_energy, integrals, src_block, dst_block):
    tile_width = integrals.shape[1]
    local_blocks = virt_energy.shape[0] // tile_width
    rows = amplitudes.shape[0]
    denominator = virt_energy[None, :] - pair_energy[:, None]
    high, low = densify(integrals, src_block, dst_block, local_blocks, NZ * NY * local_blocks)
    current = amplitudes
    for iteration in range(ITERS):
        mine, other = gather_panel(current)
        keep, send = contract(mine, other, high, low)
        got = lax.ppermute(send, "grp", CORE_SWAP)
        away = lax.ppermute(keep[rows:] + got[rows:], "grp", X_SWAP)
        ladder = keep[:rows] + got[:rows] + away
        current = ((driver + ladder) / denominator).astype(jnp.bfloat16)
    return current


def solution(mesh):
    form = on_device if (mesh.shape["tile"], mesh.shape["grp"]) == (NZ * NY, NX * NC) else general_form
    return jax.shard_map(
        form,
        mesh=mesh,
        in_specs=(
            P("grp", "tile"),
            P("grp", "tile"),
            P("grp"),
            P("tile"),
            P(("tile", "grp"), None, None),
            P("tile"),
            P("tile"),
        ),
        out_specs=P("grp", "tile"),
        check_vma=False,
    )
```

```python
import functools
import math

import jax
import jax.numpy as jnp
from jax import lax
from jax.experimental import pallas as pl
from jax.experimental.pallas import tpu as pltpu
from jax.sharding import PartitionSpec as P

ITERS = 2
MIB = 1024 * 1024


def contract_blocks(amp_rows, tile_set, source, target, local_blocks):
    row_count = amp_rows.shape[0]
    tile_width = tile_set.shape[1]
    tile_count = tile_set.shape[0]
    group_size = math.gcd(tile_count, 48)
    turns = tile_count // group_size
    blocks = amp_rows.reshape(row_count, -1, tile_width)
    packed_tiles = tile_set.reshape(turns, group_size, tile_width, tile_width)
    packed_source = source.reshape(turns, group_size)
    packed_target = target.reshape(turns, group_size)

    def advance(total_sum, packed):
        picked = jnp.take(blocks, packed[1], axis=1)
        partial_value = jnp.einsum(
            "rgc,gcd->rgd", picked, packed[0], preferred_element_type=jnp.float32
        )
        pieces = []
        for block in range(local_blocks):
            chosen = (packed[2] == block)[None, :, None]
            pieces.append(jnp.sum(jnp.where(chosen, partial_value, 0.0), axis=1))
        return (total_sum + jnp.stack(pieces, axis=1), None)

    initial = jnp.zeros((row_count, local_blocks, tile_width), jnp.float32)
    total_sum, unused = lax.scan(advance, initial, (packed_tiles, packed_source, packed_target))
    return total_sum.reshape(row_count, local_blocks * tile_width)


def general_form(amplitudes, driver, pair_energy, virt_energy, integrals, src_block, dst_block):
    tile_width = integrals.shape[1]
    local_blocks = virt_energy.shape[0] // tile_width
    denominator = virt_energy[None, :] - pair_energy[:, None]
    current = amplitudes
    first_tile = lax.axis_index("grp") * integrals.shape[0]
    my_source = lax.dynamic_slice_in_dim(src_block, first_tile, integrals.shape[0])
    my_target = lax.dynamic_slice_in_dim(dst_block, first_tile, integrals.shape[0])
    for iteration in range(ITERS):
        all_pairs = lax.all_gather(current, "grp", axis=0, tiled=True)
        whole_panel = lax.all_gather(all_pairs, "tile", axis=1, tiled=True)
        partial_value = contract_blocks(whole_panel, integrals, my_source, my_target, local_blocks)
        ladder = lax.psum_scatter(partial_value, "grp", scatter_dimension=0, tiled=True)
        current = ((driver + ladder) / denominator).astype(jnp.bfloat16)
    return current


NZ, NY, NX, NC = 4, 2, 2, 2
PARTS = 2


def z_shift(steps):
    return [(z * NY + y, (z + steps) % NZ * NY + y) for z in range(NZ) for y in range(NY)]


Y_SWAP = [(t, t ^ 1) for t in range(NZ * NY)]
X_SWAP = [(g, g ^ 2) for g in range(NX * NC)]
CORE_SWAP = [(g, g ^ 1) for g in range(NX * NC)]


def over_z(shard):
    return jnp.stack([shard] + [lax.ppermute(shard, "tile", z_shift(s)) for s in range(1, NZ)])


def block_order(tile, source, local_blocks):
    z, y = tile // NY, lax.rem(tile, NY)
    owner, inner = source // local_blocks, lax.rem(source, local_blocks)
    away_z = lax.rem(z - owner // NY + NZ, NZ)
    away_y = lax.rem(y + owner, NY)
    each = local_blocks // PARTS
    return ((inner // each * NY + away_y) * NZ + away_z) * each + lax.rem(inner, each)


def sum_kernel(chunk, local_blocks, src_any, dst_any, tiles_any, total, tiles, src, dst, list_sem, tile_sem):
    steps = tiles.shape[0] // chunk
    lists = [pltpu.make_async_copy(a, b, list_sem.at[i]) for i, (a, b) in enumerate(((src_any, src), (dst_any, dst)))]
    for copy in lists:
        copy.start()

    def tile_copy(step):
        part = pl.ds(step * chunk, chunk)
        return pltpu.make_async_copy(tiles_any.at[part], tiles.at[part], tile_sem.at[step])

    for step in range(steps):
        tile_copy(step).start()

    def clear(block, carry):
        total[block] = jnp.zeros(total.shape[1:], jnp.float32)
        return carry

    lax.fori_loop(0, total.shape[0], clear, 0, unroll=4)
    for copy in lists:
        copy.wait()
    tile, first = lax.axis_index("tile"), lax.axis_index("grp") * tiles.shape[0]

    def run(step, carry):
        tile_copy(step).wait()

        def add(j, carry):
            k = step * chunk + j
            slot = block_order(tile, src[first + k], local_blocks) * local_blocks + dst[first + k]
            total[slot] += tiles[k].astype(jnp.float32)
            return carry

        lax.fori_loop(0, chunk, add, 0, unroll=4)
        return carry

    lax.fori_loop(0, steps, run, 0)


def sum_tiles(integrals, src_block, dst_block, local_blocks, blocks):
    count, width, _ = integrals.shape
    chunk = math.gcd(count, 24)
    outside = pl.BlockSpec(memory_space=pl.ANY)
    return pl.pallas_call(
        functools.partial(sum_kernel, chunk, local_blocks),
        in_specs=[outside] * 3,
        out_specs=pl.BlockSpec(memory_space=pltpu.VMEM),
        out_shape=jax.ShapeDtypeStruct((blocks * local_blocks, width, width), jnp.float32),
        scratch_shapes=[
            pltpu.VMEM(integrals.shape, jnp.bfloat16),
            pltpu.SMEM(src_block.shape, jnp.int32),
            pltpu.SMEM(dst_block.shape, jnp.int32),
            pltpu.SemaphoreType.DMA((2,)),
            pltpu.SemaphoreType.DMA((count // chunk,)),
        ],
        compiler_params=pltpu.CompilerParams(vmem_limit_bytes=24 * MIB),
        cost_estimate=pl.CostEstimate(
            flops=count * width * width, bytes_accessed=2 * count * width * width + 4 * blocks * local_blocks * width * width, transcendentals=0
        ),
        name="sum_tiles",
    )(*(pltpu.with_memory_space_constraint(a, pltpu.HBM) for a in (src_block, dst_block, integrals)))


def split_kernel(local_blocks, total, high, low):
    width = total.shape[-1]

    def split(block, carry):
        for d in range(local_blocks):
            value = total[block * local_blocks + d]
            top = value.astype(jnp.bfloat16)
            rest = value - top.astype(jnp.float32)
            high[block, :, d * width : (d + 1) * width] = top
            low[block, :, d * width : (d + 1) * width] = rest.astype(jnp.bfloat16)
        return carry

    lax.fori_loop(0, total.shape[0] // local_blocks, split, 0)


def split_parts(total, local_blocks):
    slots, width, _ = total.shape
    shape = jax.ShapeDtypeStruct((slots // local_blocks, width, local_blocks * width), jnp.bfloat16)
    local = pl.BlockSpec(memory_space=pltpu.VMEM)
    high, low = pl.pallas_call(
        functools.partial(split_kernel, local_blocks),
        in_specs=[local],
        out_specs=[local, local],
        out_shape=[shape, shape],
        compiler_params=pltpu.CompilerParams(vmem_limit_bytes=24 * MIB),
        cost_estimate=pl.CostEstimate(flops=2 * total.size, bytes_accessed=8 * total.size, transcendentals=0),
        name="split_parts",
    )(total)
    return high.reshape(-1, local_blocks * width), low.reshape(-1, local_blocks * width)


def contract_kernel(a_mine, a_other, b_mine, b_other, high, low, keep, send, rows):
    half = keep.shape[0]
    column = 0
    for part, (mine, other) in enumerate(((a_mine, a_other), (b_mine, b_other))):
        height, depth = mine.shape[-2:]
        for y in range(NY):
            for z in range(NZ):
                for core, ref in enumerate((mine, other)):
                    for x in range(NX):
                        value = ref[x, y, z] if part == 0 else ref[y, x, z]
                        start = core * half + x * height
                        rows[start : start + height, column : column + depth] = value
                column += depth
    part = jnp.dot(rows[...], high[...], preferred_element_type=jnp.float32)
    part += jnp.dot(rows[...], low[...], preferred_element_type=jnp.float32)
    keep[...] = part[:half]
    send[...] = part[half:]


def contract(a_mine, a_other, b_mine, b_other, high, low):
    height = a_mine.shape[-2]
    depth, columns = high.shape
    half = NX * height
    local = pl.BlockSpec(memory_space=pltpu.VMEM)
    shape = jax.ShapeDtypeStruct((half, columns), jnp.float32)
    return pl.pallas_call(
        contract_kernel,
        in_specs=[local] * 6,
        out_specs=[local, local],
        out_shape=[shape, shape],
        scratch_shapes=[pltpu.VMEM((NC * half, depth), jnp.bfloat16)],
        compiler_params=pltpu.CompilerParams(vmem_limit_bytes=24 * MIB),
        cost_estimate=pl.CostEstimate(
            flops=8 * half * depth * columns, bytes_accessed=4 * depth * columns + 4 * half * depth + 8 * half * columns, transcendentals=0
        ),
        name="contract",
    )(a_mine, a_other, b_mine, b_other, high, low)


def on_device(amplitudes, driver, pair_energy, virt_energy, integrals, src_block, dst_block):
    tile_width = integrals.shape[1]
    local_blocks = virt_energy.shape[0] // tile_width
    rows = amplitudes.shape[0]
    cut = local_blocks // PARTS * tile_width
    denominator = virt_energy[None, :] - pair_energy[:, None]
    total = sum_tiles(integrals, src_block, dst_block, local_blocks, NZ * NY * local_blocks)
    high = low = None
    current = amplitudes
    for iteration in range(ITERS):
        near = over_z(current)
        if iteration == 0:
            near, total = lax.optimization_barrier((near, total))
        near_a, near_b = near[..., :cut], near[..., cut:]
        two_a = jnp.stack([near_a, lax.ppermute(near_a, "tile", Y_SWAP)])
        two_b = jnp.stack([near_b, lax.ppermute(near_b, "grp", X_SWAP)])
        a_mine = jnp.stack([two_a, lax.ppermute(two_a, "grp", X_SWAP)])
        b_mine = jnp.stack([two_b, lax.ppermute(two_b, "tile", Y_SWAP)])
        if iteration == 0:
            high, low = split_parts(total, local_blocks)
            a_mine, b_mine, high, low = lax.optimization_barrier((a_mine, b_mine, high, low))
        a_other = lax.ppermute(a_mine, "grp", CORE_SWAP)
        b_other = lax.ppermute(b_mine, "grp", CORE_SWAP)
        keep, send = contract(a_mine, a_other, b_mine, b_other, high, low)
        got = lax.ppermute(send, "grp", CORE_SWAP)
        away = lax.ppermute(keep[rows:] + got[rows:], "grp", X_SWAP)
        ladder = keep[:rows] + got[:rows] + away
        current = ((driver + ladder) / denominator).astype(jnp.bfloat16)
    return current


def solution(mesh):
    form = on_device if (mesh.shape["tile"], mesh.shape["grp"]) == (NZ * NY, NX * NC) else general_form
    return jax.shard_map(
        form,
        mesh=mesh,
        in_specs=(
            P("grp", "tile"),
            P("grp", "tile"),
            P("grp"),
            P("tile"),
            P(("tile", "grp"), None, None),
            P("tile"),
            P("tile"),
        ),
        out_specs=P("grp", "tile"),
        check_vma=False,
    )
```

```python
import functools
import math

import jax
import jax.numpy as jnp
from jax import lax
from jax.experimental import pallas as pl
from jax.experimental.pallas import tpu as pltpu
from jax.sharding import PartitionSpec as P

ITERS = 2
MIB = 1024 * 1024


def contract_blocks(amp_rows, tile_set, source, target, local_blocks):
    row_count = amp_rows.shape[0]
    tile_width = tile_set.shape[1]
    tile_count = tile_set.shape[0]
    group_size = math.gcd(tile_count, 48)
    turns = tile_count // group_size
    blocks = amp_rows.reshape(row_count, -1, tile_width)
    packed_tiles = tile_set.reshape(turns, group_size, tile_width, tile_width)
    packed_source = source.reshape(turns, group_size)
    packed_target = target.reshape(turns, group_size)

    def advance(total_sum, packed):
        picked = jnp.take(blocks, packed[1], axis=1)
        partial_value = jnp.einsum(
            "rgc,gcd->rgd", picked, packed[0], preferred_element_type=jnp.float32
        )
        pieces = []
        for block in range(local_blocks):
            chosen = (packed[2] == block)[None, :, None]
            pieces.append(jnp.sum(jnp.where(chosen, partial_value, 0.0), axis=1))
        return (total_sum + jnp.stack(pieces, axis=1), None)

    initial = jnp.zeros((row_count, local_blocks, tile_width), jnp.float32)
    total_sum, unused = lax.scan(advance, initial, (packed_tiles, packed_source, packed_target))
    return total_sum.reshape(row_count, local_blocks * tile_width)


def general_form(amplitudes, driver, pair_energy, virt_energy, integrals, src_block, dst_block):
    tile_width = integrals.shape[1]
    local_blocks = virt_energy.shape[0] // tile_width
    denominator = virt_energy[None, :] - pair_energy[:, None]
    current = amplitudes
    first_tile = lax.axis_index("grp") * integrals.shape[0]
    my_source = lax.dynamic_slice_in_dim(src_block, first_tile, integrals.shape[0])
    my_target = lax.dynamic_slice_in_dim(dst_block, first_tile, integrals.shape[0])
    for iteration in range(ITERS):
        all_pairs = lax.all_gather(current, "grp", axis=0, tiled=True)
        whole_panel = lax.all_gather(all_pairs, "tile", axis=1, tiled=True)
        partial_value = contract_blocks(whole_panel, integrals, my_source, my_target, local_blocks)
        ladder = lax.psum_scatter(partial_value, "grp", scatter_dimension=0, tiled=True)
        current = ((driver + ladder) / denominator).astype(jnp.bfloat16)
    return current


NZ, NY, NX, NC = 4, 2, 2, 2
PARTS = 2


def z_shift(steps):
    return [(z * NY + y, (z + steps) % NZ * NY + y) for z in range(NZ) for y in range(NY)]


Y_SWAP = [(t, t ^ 1) for t in range(NZ * NY)]
X_SWAP = [(g, g ^ 2) for g in range(NX * NC)]
CORE_SWAP = [(g, g ^ 1) for g in range(NX * NC)]


def over_y(value):
    return lax.ppermute(value, "tile", Y_SWAP)


def over_x(value):
    return lax.ppermute(value, "grp", X_SWAP)


def over_core(value):
    return lax.ppermute(value, "grp", CORE_SWAP)


def parts_of(rows):
    return jnp.stack(jnp.split(rows, PARTS, axis=1))


def over_z(value):
    return [value] + [lax.ppermute(value, "tile", z_shift(s)) for s in range(1, NZ)]


def gather_panel(near):
    first, second = near
    first_y, second_x = over_y(first), over_x(second)
    first_x, second_y = over_x(first), over_y(second)
    first_xy, second_xy = over_x(first_y), over_y(second_x)
    return jnp.stack([first_y, second_x]), jnp.stack([first_x, second_y]), jnp.stack([first_xy, second_xy])


def sum_kernel(chunk, local_blocks, own, src_any, dst_any, tiles_any, total, tiles, src, dst, list_sem, tile_sem):
    steps = tiles.shape[0] // chunk
    half = local_blocks // NC
    lists = [pltpu.make_async_copy(a, b, list_sem.at[i]) for i, (a, b) in enumerate(((src_any, src), (dst_any, dst)))]
    for copy in lists:
        copy.start()

    def tile_copy(step):
        part = pl.ds(step * chunk, chunk)
        return pltpu.make_async_copy(tiles_any.at[part], tiles.at[part], tile_sem.at[step])

    for step in range(steps):
        tile_copy(step).start()

    def clear(block, carry):
        total[block] = jnp.zeros(total.shape[1:], jnp.float32)
        return carry

    lax.fori_loop(0, total.shape[0], clear, 0, unroll=4)
    for copy in lists:
        copy.wait()
    tile, grp = lax.axis_index("tile"), lax.axis_index("grp")
    z, y, core = tile // NY, lax.rem(tile, NY), lax.rem(grp, NC)
    wanted = core if own else 1 - core
    first = grp * tiles.shape[0]

    def run(step, carry):
        tile_copy(step).wait()

        def add(j, carry):
            k = step * chunk + j
            target = dst[first + k]

            @pl.when(target // half == wanted)
            def _():
                source = src[first + k]
                owner = source // local_blocks
                away = lax.rem(y + owner, NY) * NZ + lax.rem(z - owner // NY + NZ, NZ)
                slot = (away * local_blocks + lax.rem(source, local_blocks)) * half + lax.rem(target, half)
                total[slot] += tiles[k].astype(jnp.float32)

            return carry

        lax.fori_loop(0, chunk, add, 0)
        return carry

    lax.fori_loop(0, steps, run, 0)


def sum_tiles(integrals, src_block, dst_block, local_blocks, blocks, own):
    count, width, _ = integrals.shape
    slots = blocks * local_blocks // NC
    chunk = math.gcd(count, 24)
    outside = pl.BlockSpec(memory_space=pl.ANY)
    return pl.pallas_call(
        functools.partial(sum_kernel, chunk, local_blocks, own),
        in_specs=[outside] * 3,
        out_specs=pl.BlockSpec(memory_space=pltpu.VMEM),
        out_shape=jax.ShapeDtypeStruct((slots, width, width), jnp.float32),
        scratch_shapes=[
            pltpu.VMEM(integrals.shape, jnp.bfloat16),
            pltpu.SMEM(src_block.shape, jnp.int32),
            pltpu.SMEM(dst_block.shape, jnp.int32),
            pltpu.SemaphoreType.DMA((2,)),
            pltpu.SemaphoreType.DMA((count // chunk,)),
        ],
        compiler_params=pltpu.CompilerParams(vmem_limit_bytes=20 * MIB),
        cost_estimate=pl.CostEstimate(
            flops=count * width * width, bytes_accessed=2 * count * width * width + 4 * slots * width * width, transcendentals=0
        ),
        name="sum_own" if own else "sum_given",
    )(*(pltpu.with_memory_space_constraint(a, pltpu.HBM) for a in (src_block, dst_block, integrals)))


def split_kernel(half, mine, got, high, low):
    width = mine.shape[-1]

    def split(block, carry):
        for d in range(half):
            value = mine[block * half + d] + got[block * half + d]
            top = value.astype(jnp.bfloat16)
            rest = value - top.astype(jnp.float32)
            high[block, :, d * width : (d + 1) * width] = top
            low[block, :, d * width : (d + 1) * width] = rest.astype(jnp.bfloat16)
        return carry

    lax.fori_loop(0, mine.shape[0] // half, split, 0)


def split_parts(mine, got, half):
    slots, width, _ = mine.shape
    shape = jax.ShapeDtypeStruct((slots // half, width, half * width), jnp.bfloat16)
    local = pl.BlockSpec(memory_space=pltpu.VMEM)
    high, low = pl.pallas_call(
        functools.partial(split_kernel, half),
        in_specs=[local, local],
        out_specs=[local, local],
        out_shape=[shape, shape],
        compiler_params=pltpu.CompilerParams(vmem_limit_bytes=20 * MIB),
        cost_estimate=pl.CostEstimate(flops=3 * mine.size, bytes_accessed=12 * mine.size, transcendentals=0),
        name="split_parts",
    )(mine, got)
    return high.reshape(-1, half * width), low.reshape(-1, half * width)


def contract_kernel(by_core, *refs):
    mine, other, (high, low, keep, send, rows) = refs[:4], refs[4:8], refs[8:]
    height, depth = mine[0].shape[-2:]
    core = lax.rem(lax.axis_index("grp"), NC)
    for away, pieces in enumerate((mine, other)):
        for part in range(PARTS):
            row_core = away if by_core else part ^ away
            half = part if by_core else (core if away == 0 else 1 - core)
            for y in range(NY):
                for x in range(NX):
                    for z in range(NZ):
                        if x == 0 and y == 0:
                            value = pieces[0][part, z]
                        elif x and y:
                            value = pieces[3][part, z]
                        else:
                            value = pieces[1 if (part == 0) == (y == 1) else 2][part, z]
                        row = (x * NC + row_core) * height
                        column = (y * NZ + z) * PARTS * depth + half * depth
                        if not by_core:
                            column = pl.multiple_of(column, depth)
                        rows[row : row + height, pl.ds(column, depth)] = value
    part = jnp.dot(rows[...], high[...], preferred_element_type=jnp.float32)
    part += jnp.dot(rows[...], low[...], preferred_element_type=jnp.float32)
    near = keep.shape[0]
    keep[...] = part[:near]
    send[...] = part[near:]


def contract(mine, other, high, low, by_core):
    height = mine[0].shape[-2]
    depth, columns = high.shape
    near = NC * height
    local = pl.BlockSpec(memory_space=pltpu.VMEM)
    shape = jax.ShapeDtypeStruct((near, columns), jnp.float32)
    return pl.pallas_call(
        functools.partial(contract_kernel, by_core),
        in_specs=[local] * 10,
        out_specs=[local, local],
        out_shape=[shape, shape],
        scratch_shapes=[pltpu.VMEM((NX * near, depth), jnp.bfloat16)],
        compiler_params=pltpu.CompilerParams(vmem_limit_bytes=20 * MIB),
        cost_estimate=pl.CostEstimate(
            flops=8 * near * depth * columns, bytes_accessed=4 * depth * columns + 4 * near * depth + 8 * near * columns, transcendentals=0
        ),
        name="contract_rows" if by_core else "contract_columns",
    )(*mine, *other, high, low)


def on_device(amplitudes, driver, pair_energy, virt_energy, integrals, src_block, dst_block):
    tile_width = integrals.shape[1]
    local_blocks = virt_energy.shape[0] // tile_width
    blocks, half = NZ * NY * local_blocks, local_blocks // NC
    cut = half * tile_width
    lower = lax.rem(lax.axis_index("grp"), NC) == 0

    given = sum_tiles(integrals, src_block, dst_block, local_blocks, blocks, False)
    terms = jnp.stack([driver, virt_energy[None, :] - pair_energy[:, None]])
    kept_terms = jnp.where(lower, terms[..., :cut], terms[..., cut:])
    given_terms = jnp.where(lower, terms[..., cut:], terms[..., :cut])

    near = jnp.stack([parts_of(value) for value in over_z(amplitudes)], axis=1)
    near, given = lax.optimization_barrier((near, given))
    got = over_core(given)
    for iteration in range(ITERS):
        if iteration > 0:
            near = jnp.stack(over_z(shard), axis=1)
        direct, crossed, diagonal = gather_panel(near)
        if iteration == 0:
            own = sum_tiles(integrals, src_block, dst_block, local_blocks, blocks, True)
            diagonal, own = lax.optimization_barrier((diagonal, own))
            high, low = split_parts(own, got, half)
            both_terms = jnp.stack([kept_terms, over_core(given_terms)], axis=1)
        mine = (near, direct, crossed, diagonal)
        other = tuple(over_core(piece) for piece in mine)
        keep, send = contract(mine, other, high, low, iteration == 0)
        ladder = (keep + over_x(send)).reshape(PARTS, -1, cut)
        shard = ((both_terms[0] + ladder) / both_terms[1]).astype(jnp.bfloat16)
    sides = [shard[0], over_core(shard[1])]
    return jnp.where(lower, jnp.concatenate(sides, axis=1), jnp.concatenate(sides[::-1], axis=1))


def solution(mesh):
    form = on_device if (mesh.shape["tile"], mesh.shape["grp"]) == (NZ * NY, NX * NC) else general_form
    return jax.shard_map(
        form,
        mesh=mesh,
        in_specs=(
            P("grp", "tile"),
            P("grp", "tile"),
            P("grp"),
            P("tile"),
            P(("tile", "grp"), None, None),
            P("tile"),
            P("tile"),
        ),
        out_specs=P("grp", "tile"),
        check_vma=False,
    )
```

```python
import functools
import math

import jax
import jax.numpy as jnp
from jax import lax
from jax.experimental import pallas as pl
from jax.experimental.pallas import tpu as pltpu
from jax.sharding import PartitionSpec as P

ITERS = 2
MIB = 1024 * 1024


def contract_blocks(amp_rows, tile_set, source, target, local_blocks):
    row_count = amp_rows.shape[0]
    tile_width = tile_set.shape[1]
    tile_count = tile_set.shape[0]
    group_size = math.gcd(tile_count, 48)
    turns = tile_count // group_size
    blocks = amp_rows.reshape(row_count, -1, tile_width)
    packed_tiles = tile_set.reshape(turns, group_size, tile_width, tile_width)
    packed_source = source.reshape(turns, group_size)
    packed_target = target.reshape(turns, group_size)

    def advance(total_sum, packed):
        picked = jnp.take(blocks, packed[1], axis=1)
        partial_value = jnp.einsum(
            "rgc,gcd->rgd", picked, packed[0], preferred_element_type=jnp.float32
        )
        pieces = []
        for block in range(local_blocks):
            chosen = (packed[2] == block)[None, :, None]
            pieces.append(jnp.sum(jnp.where(chosen, partial_value, 0.0), axis=1))
        return (total_sum + jnp.stack(pieces, axis=1), None)

    initial = jnp.zeros((row_count, local_blocks, tile_width), jnp.float32)
    total_sum, unused = lax.scan(advance, initial, (packed_tiles, packed_source, packed_target))
    return total_sum.reshape(row_count, local_blocks * tile_width)


def general_form(amplitudes, driver, pair_energy, virt_energy, integrals, src_block, dst_block):
    tile_width = integrals.shape[1]
    local_blocks = virt_energy.shape[0] // tile_width
    denominator = virt_energy[None, :] - pair_energy[:, None]
    current = amplitudes
    first_tile = lax.axis_index("grp") * integrals.shape[0]
    my_source = lax.dynamic_slice_in_dim(src_block, first_tile, integrals.shape[0])
    my_target = lax.dynamic_slice_in_dim(dst_block, first_tile, integrals.shape[0])
    for iteration in range(ITERS):
        all_pairs = lax.all_gather(current, "grp", axis=0, tiled=True)
        whole_panel = lax.all_gather(all_pairs, "tile", axis=1, tiled=True)
        partial_value = contract_blocks(whole_panel, integrals, my_source, my_target, local_blocks)
        ladder = lax.psum_scatter(partial_value, "grp", scatter_dimension=0, tiled=True)
        current = ((driver + ladder) / denominator).astype(jnp.bfloat16)
    return current


NZ, NY, NX, NC = 4, 2, 2, 2
PARTS = 2


def z_swap(away):
    return [(t, t ^ (away * NY)) for t in range(NZ * NY)]


Y_SWAP = [(t, t ^ 1) for t in range(NZ * NY)]
X_SWAP = [(g, g ^ 2) for g in range(NX * NC)]
CORE_SWAP = [(g, g ^ 1) for g in range(NX * NC)]


def over_y(value):
    return lax.ppermute(value, "tile", Y_SWAP)


def over_x(value):
    return lax.ppermute(value, "grp", X_SWAP)


def over_core(value):
    return lax.ppermute(value, "grp", CORE_SWAP)


def parts_of(rows):
    return jnp.stack(jnp.split(rows, PARTS, axis=1))


def over_z(value):
    return [value] + [lax.ppermute(value, "tile", z_swap(s)) for s in range(1, NZ)]


def gather_panel(near):
    first, second = near
    first_y, second_x = over_y(first), over_x(second)
    first_x, second_y = over_x(first), over_y(second)
    first_xy, second_xy = over_x(first_y), over_y(second_x)
    return jnp.stack([first_y, second_x]), jnp.stack([first_x, second_y]), jnp.stack([first_xy, second_xy])


def sum_kernel(chunk, local_blocks, src_any, dst_any, tiles_any, total, given, tiles, src, dst, list_sem, tile_sem):
    steps = tiles.shape[0] // chunk
    half = local_blocks // NC
    shift = half.bit_length() - 1
    slots = given.shape[0]
    lists = [pltpu.make_async_copy(a, b, list_sem.at[i]) for i, (a, b) in enumerate(((src_any, src), (dst_any, dst)))]
    for copy in lists:
        copy.start()

    def tile_copy(step):
        part = pl.ds(step * chunk, chunk)
        return pltpu.make_async_copy(tiles_any.at[part], tiles.at[part], tile_sem.at[step])

    for step in range(steps):
        tile_copy(step).start()

    def clear(slot, carry):
        total[slot] = jnp.zeros(total.shape[1:], jnp.float32)
        return carry

    lax.fori_loop(0, total.shape[0], clear, 0, unroll=4)
    for copy in lists:
        copy.wait()
    grp = lax.axis_index("grp")
    here = lax.axis_index("tile") * local_blocks
    kept = lax.rem(grp, NC) * half
    first = grp * tiles.shape[0]

    def run(step, carry):
        tile_copy(step).wait()

        def add(j, carry):
            k = step * chunk + j
            target = dst[first + k] ^ kept
            slot = (target >> shift) * slots + ((src[first + k] ^ here) << shift) + (target & (half - 1))
            total[slot] += tiles[k].astype(jnp.float32)
            return carry

        lax.fori_loop(0, chunk, add, 0, unroll=8)
        return carry

    lax.fori_loop(0, steps, run, 0)

    def give(slot, carry):
        given[slot] = total[slots + slot]
        return carry

    lax.fori_loop(0, slots, give, 0, unroll=4)


def sum_tiles(integrals, src_block, dst_block, local_blocks, blocks):
    count, width, _ = integrals.shape
    slots = blocks * local_blocks // NC
    chunk = math.gcd(count, 24)
    outside = pl.BlockSpec(memory_space=pl.ANY)
    local = pl.BlockSpec(memory_space=pltpu.VMEM)
    return pl.pallas_call(
        functools.partial(sum_kernel, chunk, local_blocks),
        in_specs=[outside] * 3,
        out_specs=[local, local],
        out_shape=[pltpu.VMEM((NC * slots, width, width), jnp.float32), pltpu.VMEM((slots, width, width), jnp.float32)],
        scratch_shapes=[
            pltpu.VMEM(integrals.shape, jnp.bfloat16),
            pltpu.SMEM(src_block.shape, jnp.int32),
            pltpu.SMEM(dst_block.shape, jnp.int32),
            pltpu.SemaphoreType.DMA((2,)),
            pltpu.SemaphoreType.DMA((count // chunk,)),
        ],
        compiler_params=pltpu.CompilerParams(vmem_limit_bytes=24 * MIB),
        cost_estimate=pl.CostEstimate(
            flops=count * width * width, bytes_accessed=2 * count * width * width + 4 * slots * width * width, transcendentals=0
        ),
        name="sum_tiles",
    )(*(pltpu.with_memory_space_constraint(a, pltpu.HBM) for a in (src_block, dst_block, integrals)))


def split_kernel(half, mine, got, high, low):
    width = mine.shape[-1]

    def split(block, carry):
        for d in range(half):
            value = mine[block * half + d] + got[block * half + d]
            top = value.astype(jnp.bfloat16)
            rest = value - top.astype(jnp.float32)
            high[block, :, d * width : (d + 1) * width] = top
            low[block, :, d * width : (d + 1) * width] = rest.astype(jnp.bfloat16)
        return carry

    lax.fori_loop(0, got.shape[0] // half, split, 0)


def split_parts(mine, got, half):
    slots, width, _ = got.shape
    shape = pltpu.VMEM((slots // half, width, half * width), jnp.bfloat16)
    local = pl.BlockSpec(memory_space=pltpu.VMEM)
    high, low = pl.pallas_call(
        functools.partial(split_kernel, half),
        in_specs=[local, local],
        out_specs=[local, local],
        out_shape=[shape, shape],
        compiler_params=pltpu.CompilerParams(vmem_limit_bytes=24 * MIB),
        cost_estimate=pl.CostEstimate(flops=3 * got.size, bytes_accessed=12 * got.size, transcendentals=0),
        name="split_parts",
    )(*(pltpu.with_memory_space_constraint(a, pltpu.VMEM) for a in (mine, got)))
    return high.reshape(-1, half * width), low.reshape(-1, half * width)


def contract_kernel(by_core, *refs):
    mine, other, (high, low, keep, send, rows) = refs[:4], refs[4:8], refs[8:]
    height, depth = mine[0].shape[-2:]
    core = lax.rem(lax.axis_index("grp"), NC)
    for away, pieces in enumerate((mine, other)):
        for part in range(PARTS):
            row_core = away if by_core else part ^ away
            half = part if by_core else (core if away == 0 else 1 - core)
            for y in range(NY):
                for x in range(NX):
                    for z in range(NZ):
                        if x == 0 and y == 0:
                            value = pieces[0][part, z]
                        elif x and y:
                            value = pieces[3][part, z]
                        else:
                            value = pieces[1 if (part == 0) == (y == 1) else 2][part, z]
                        row = (x * NC + row_core) * height
                        column = (z * NY + y) * PARTS * depth + half * depth
                        if not by_core:
                            column = pl.multiple_of(column, depth)
                        rows[row : row + height, pl.ds(column, depth)] = value
    part = jnp.dot(rows[...], high[...], preferred_element_type=jnp.float32)
    part += jnp.dot(rows[...], low[...], preferred_element_type=jnp.float32)
    near = keep.shape[0]
    keep[...] = part[:near]
    send[...] = part[near:]


def contract(mine, other, high, low, by_core):
    height = mine[0].shape[-2]
    depth, columns = high.shape
    near = NC * height
    local = pl.BlockSpec(memory_space=pltpu.VMEM)
    shape = jax.ShapeDtypeStruct((near, columns), jnp.float32)
    return pl.pallas_call(
        functools.partial(contract_kernel, by_core),
        in_specs=[local] * 10,
        out_specs=[local, local],
        out_shape=[shape, shape],
        scratch_shapes=[pltpu.VMEM((NX * near, depth), jnp.bfloat16)],
        compiler_params=pltpu.CompilerParams(vmem_limit_bytes=24 * MIB),
        cost_estimate=pl.CostEstimate(
            flops=8 * near * depth * columns, bytes_accessed=4 * depth * columns + 4 * near * depth + 8 * near * columns, transcendentals=0
        ),
        name="contract_rows" if by_core else "contract_columns",
    )(*mine, *other, high, low)


def on_device(amplitudes, driver, pair_energy, virt_energy, integrals, src_block, dst_block):
    tile_width = integrals.shape[1]
    local_blocks = virt_energy.shape[0] // tile_width
    blocks, half = NZ * NY * local_blocks, local_blocks // NC
    cut = half * tile_width
    lower = lax.rem(lax.axis_index("grp"), NC) == 0

    total, given = sum_tiles(integrals, src_block, dst_block, local_blocks, blocks)
    terms = jnp.stack([driver, virt_energy[None, :] - pair_energy[:, None]])
    kept_terms = jnp.where(lower, terms[..., :cut], terms[..., cut:])
    given_terms = jnp.where(lower, terms[..., cut:], terms[..., :cut])

    near = jnp.stack([parts_of(value) for value in over_z(amplitudes)], axis=1)
    near, given = lax.optimization_barrier((near, given))
    got = over_core(given)
    for iteration in range(ITERS):
        if iteration > 0:
            near = jnp.stack(over_z(shard), axis=1)
        direct, crossed, diagonal = gather_panel(near)
        if iteration == 0:
            high, low = split_parts(total, got, half)
            both_terms = jnp.stack([kept_terms, over_core(given_terms)], axis=1)
        mine = (near, direct, crossed, diagonal)
        other = tuple(over_core(piece) for piece in mine)
        keep, send = contract(mine, other, high, low, iteration == 0)
        ladder = (keep + over_x(send)).reshape(PARTS, -1, cut)
        shard = ((both_terms[0] + ladder) / both_terms[1]).astype(jnp.bfloat16)
    sides = [shard[0], over_core(shard[1])]
    return jnp.where(lower, jnp.concatenate(sides, axis=1), jnp.concatenate(sides[::-1], axis=1))


def solution(mesh):
    form = on_device if (mesh.shape["tile"], mesh.shape["grp"]) == (NZ * NY, NX * NC) else general_form
    return jax.shard_map(
        form,
        mesh=mesh,
        in_specs=(
            P("grp", "tile"),
            P("grp", "tile"),
            P("grp"),
            P("tile"),
            P(("tile", "grp"), None, None),
            P("tile"),
            P("tile"),
        ),
        out_specs=P("grp", "tile"),
        check_vma=False,
    )
```

```python
import functools
import math

import jax
import jax.numpy as jnp
from jax import lax
from jax.experimental import pallas as pl
from jax.experimental.pallas import tpu as pltpu
from jax.sharding import PartitionSpec as P

ITERS = 2
MIB = 1024 * 1024


def contract_blocks(amp_rows, tile_set, source, target, local_blocks):
    row_count = amp_rows.shape[0]
    tile_width = tile_set.shape[1]
    tile_count = tile_set.shape[0]
    group_size = math.gcd(tile_count, 48)
    turns = tile_count // group_size
    blocks = amp_rows.reshape(row_count, -1, tile_width)
    packed_tiles = tile_set.reshape(turns, group_size, tile_width, tile_width)
    packed_source = source.reshape(turns, group_size)
    packed_target = target.reshape(turns, group_size)

    def advance(total_sum, packed):
        picked = jnp.take(blocks, packed[1], axis=1)
        partial_value = jnp.einsum(
            "rgc,gcd->rgd", picked, packed[0], preferred_element_type=jnp.float32
        )
        pieces = []
        for block in range(local_blocks):
            chosen = (packed[2] == block)[None, :, None]
            pieces.append(jnp.sum(jnp.where(chosen, partial_value, 0.0), axis=1))
        return (total_sum + jnp.stack(pieces, axis=1), None)

    initial = jnp.zeros((row_count, local_blocks, tile_width), jnp.float32)
    total_sum, unused = lax.scan(advance, initial, (packed_tiles, packed_source, packed_target))
    return total_sum.reshape(row_count, local_blocks * tile_width)


def general_form(amplitudes, driver, pair_energy, virt_energy, integrals, src_block, dst_block):
    tile_width = integrals.shape[1]
    local_blocks = virt_energy.shape[0] // tile_width
    denominator = virt_energy[None, :] - pair_energy[:, None]
    current = amplitudes
    first_tile = lax.axis_index("grp") * integrals.shape[0]
    my_source = lax.dynamic_slice_in_dim(src_block, first_tile, integrals.shape[0])
    my_target = lax.dynamic_slice_in_dim(dst_block, first_tile, integrals.shape[0])
    for iteration in range(ITERS):
        all_pairs = lax.all_gather(current, "grp", axis=0, tiled=True)
        whole_panel = lax.all_gather(all_pairs, "tile", axis=1, tiled=True)
        partial_value = contract_blocks(whole_panel, integrals, my_source, my_target, local_blocks)
        ladder = lax.psum_scatter(partial_value, "grp", scatter_dimension=0, tiled=True)
        current = ((driver + ladder) / denominator).astype(jnp.bfloat16)
    return current


NZ, NY, NX, NC = 4, 2, 2, 2
PARTS = 2


def z_swap(away):
    return [(t, t ^ (away * NY)) for t in range(NZ * NY)]


Y_SWAP = [(t, t ^ 1) for t in range(NZ * NY)]
X_SWAP = [(g, g ^ 2) for g in range(NX * NC)]
CORE_SWAP = [(g, g ^ 1) for g in range(NX * NC)]


def over_y(value):
    return lax.ppermute(value, "tile", Y_SWAP)


def over_x(value):
    return lax.ppermute(value, "grp", X_SWAP)


def over_core(value):
    return lax.ppermute(value, "grp", CORE_SWAP)


def parts_of(rows):
    return jnp.stack(jnp.split(rows, PARTS, axis=1))


def over_z(value):
    return [value] + [lax.ppermute(value, "tile", z_swap(s)) for s in range(1, NZ)]


def gather_panel(near):
    first, second = near
    first_y, second_x = over_y(first), over_x(second)
    first_x, second_y = over_x(first), over_y(second)
    first_xy, second_xy = over_x(first_y), over_y(second_x)
    return jnp.stack([first_y, second_x]), jnp.stack([first_x, second_y]), jnp.stack([first_xy, second_xy])


def sum_kernel(chunk, local_blocks, src_any, dst_any, tiles_any, total, given, which, tiles, src, dst, list_sem, tile_sem):
    steps = tiles.shape[0] // chunk
    half = local_blocks // NC
    shift = half.bit_length() - 1
    slots = given.shape[0]
    lists = [pltpu.make_async_copy(a, b, list_sem.at[i]) for i, (a, b) in enumerate(((src_any, src), (dst_any, dst)))]
    for copy in lists:
        copy.start()

    def tile_copy(step):
        part = pl.ds(step * chunk, chunk)
        return pltpu.make_async_copy(tiles_any.at[part], tiles.at[part], tile_sem.at[step])

    for step in range(steps):
        tile_copy(step).start()

    def clear(slot, carry):
        total[slot] = jnp.zeros(total.shape[1:], jnp.float32)
        return carry

    lax.fori_loop(0, total.shape[0], clear, 0, unroll=4)
    for copy in lists:
        copy.wait()
    grp = lax.axis_index("grp")
    here = lax.axis_index("tile") * local_blocks
    core = lax.rem(grp, NC)
    which[...] = jnp.full(which.shape, core, jnp.int32)
    kept = core * half
    first = grp * tiles.shape[0]

    def run(step, carry):
        tile_copy(step).wait()

        def add(j, carry):
            k = step * chunk + j
            target = dst[first + k] ^ kept
            slot = (target >> shift) * slots + ((src[first + k] ^ here) << shift) + (target & (half - 1))
            total[slot] += tiles[k].astype(jnp.float32)
            return carry

        lax.fori_loop(0, chunk, add, 0, unroll=8)
        return carry

    lax.fori_loop(0, steps, run, 0)

    def give(slot, carry):
        given[slot] = total[slots + slot]
        return carry

    lax.fori_loop(0, slots, give, 0, unroll=4)


def sum_tiles(integrals, src_block, dst_block, local_blocks, blocks, rows):
    count, width, _ = integrals.shape
    slots = blocks * local_blocks // NC
    chunk = math.gcd(count, 24)
    outside = pl.BlockSpec(memory_space=pl.ANY)
    local = pl.BlockSpec(memory_space=pltpu.VMEM)
    return pl.pallas_call(
        functools.partial(sum_kernel, chunk, local_blocks),
        in_specs=[outside] * 3,
        out_specs=[local] * 3,
        out_shape=[
            pltpu.VMEM((NC * slots, width, width), jnp.float32),
            pltpu.VMEM((slots, width, width), jnp.float32),
            pltpu.VMEM((rows, local_blocks // NC * width), jnp.int32),
        ],
        scratch_shapes=[
            pltpu.VMEM(integrals.shape, jnp.bfloat16),
            pltpu.SMEM(src_block.shape, jnp.int32),
            pltpu.SMEM(dst_block.shape, jnp.int32),
            pltpu.SemaphoreType.DMA((2,)),
            pltpu.SemaphoreType.DMA((count // chunk,)),
        ],
        compiler_params=pltpu.CompilerParams(vmem_limit_bytes=24 * MIB),
        cost_estimate=pl.CostEstimate(
            flops=count * width * width, bytes_accessed=2 * count * width * width + 4 * slots * width * width, transcendentals=0
        ),
        name="sum_tiles",
    )(*(pltpu.with_memory_space_constraint(a, pltpu.HBM) for a in (src_block, dst_block, integrals)))


def split_kernel(half, mine, got, high, low):
    width = mine.shape[-1]

    def split(block, carry):
        for d in range(half):
            value = mine[block * half + d] + got[block * half + d]
            top = value.astype(jnp.bfloat16)
            rest = value - top.astype(jnp.float32)
            high[block, :, d * width : (d + 1) * width] = top
            low[block, :, d * width : (d + 1) * width] = rest.astype(jnp.bfloat16)
        return carry

    lax.fori_loop(0, got.shape[0] // half, split, 0)


def split_parts(mine, got, half):
    slots, width, _ = got.shape
    shape = pltpu.VMEM((slots // half, width, half * width), jnp.bfloat16)
    local = pl.BlockSpec(memory_space=pltpu.VMEM)
    high, low = pl.pallas_call(
        functools.partial(split_kernel, half),
        in_specs=[local, local],
        out_specs=[local, local],
        out_shape=[shape, shape],
        compiler_params=pltpu.CompilerParams(vmem_limit_bytes=24 * MIB),
        cost_estimate=pl.CostEstimate(flops=3 * got.size, bytes_accessed=12 * got.size, transcendentals=0),
        name="split_parts",
    )(*(pltpu.with_memory_space_constraint(a, pltpu.VMEM) for a in (mine, got)))
    return high.reshape(-1, half * width), low.reshape(-1, half * width)


def contract_kernel(by_core, *refs):
    mine, other, (high, low, keep, send, rows) = refs[:4], refs[4:8], refs[8:]
    height, depth = mine[0].shape[-2:]
    core = lax.rem(lax.axis_index("grp"), NC)
    for away, pieces in enumerate((mine, other)):
        for part in range(PARTS):
            row_core = away if by_core else part ^ away
            half = part if by_core else (core if away == 0 else 1 - core)
            for y in range(NY):
                for x in range(NX):
                    for z in range(NZ):
                        if x == 0 and y == 0:
                            value = pieces[0][part, z]
                        elif x and y:
                            value = pieces[3][part, z]
                        else:
                            value = pieces[1 if (part == 0) == (y == 1) else 2][part, z]
                        row = (x * NC + row_core) * height
                        column = (z * NY + y) * PARTS * depth + half * depth
                        if not by_core:
                            column = pl.multiple_of(column, depth)
                        rows[row : row + height, pl.ds(column, depth)] = value
    part = jnp.dot(rows[...], high[...], preferred_element_type=jnp.float32)
    part += jnp.dot(rows[...], low[...], preferred_element_type=jnp.float32)
    near = keep.shape[0]
    keep[...] = part[:near]
    send[...] = part[near:]


def contract(mine, other, high, low, by_core):
    height = mine[0].shape[-2]
    depth, columns = high.shape
    near = NC * height
    local = pl.BlockSpec(memory_space=pltpu.VMEM)
    shape = jax.ShapeDtypeStruct((near, columns), jnp.float32)
    return pl.pallas_call(
        functools.partial(contract_kernel, by_core),
        in_specs=[local] * 10,
        out_specs=[local, local],
        out_shape=[shape, shape],
        scratch_shapes=[pltpu.VMEM((NX * near, depth), jnp.bfloat16)],
        compiler_params=pltpu.CompilerParams(vmem_limit_bytes=24 * MIB),
        cost_estimate=pl.CostEstimate(
            flops=8 * near * depth * columns, bytes_accessed=4 * depth * columns + 4 * near * depth + 8 * near * columns, transcendentals=0
        ),
        name="contract_rows" if by_core else "contract_columns",
    )(*mine, *other, high, low)


def on_device(amplitudes, driver, pair_energy, virt_energy, integrals, src_block, dst_block):
    tile_width = integrals.shape[1]
    local_blocks = virt_energy.shape[0] // tile_width
    blocks, half = NZ * NY * local_blocks, local_blocks // NC
    cut = half * tile_width

    total, given, which = sum_tiles(integrals, src_block, dst_block, local_blocks, blocks, amplitudes.shape[0])
    lower = which == 0
    terms = jnp.stack([driver, virt_energy[None, :] - pair_energy[:, None]])
    kept_terms = jnp.where(lower, terms[..., :cut], terms[..., cut:])
    given_terms = jnp.where(lower, terms[..., cut:], terms[..., :cut])

    near = jnp.stack([parts_of(value) for value in over_z(amplitudes)], axis=1)
    near, given = lax.optimization_barrier((near, given))
    got = over_core(given)
    for iteration in range(ITERS):
        if iteration > 0:
            near = jnp.stack(over_z(shard), axis=1)
        direct, crossed, diagonal = gather_panel(near)
        if iteration == 0:
            high, low = split_parts(total, got, half)
            both_terms = jnp.stack([kept_terms, over_core(given_terms)], axis=1)
        mine = (near, direct, crossed, diagonal)
        other = tuple(over_core(piece) for piece in mine)
        keep, send = contract(mine, other, high, low, iteration == 0)
        ladder = (keep + over_x(send)).reshape(PARTS, -1, cut)
        shard = ((both_terms[0] + ladder) / both_terms[1]).astype(jnp.bfloat16)
    here, there = shard[0], over_core(shard[1])
    return jnp.concatenate([jnp.where(lower, here, there), jnp.where(lower, there, here)], axis=1)


def solution(mesh):
    form = on_device if (mesh.shape["tile"], mesh.shape["grp"]) == (NZ * NY, NX * NC) else general_form
    return jax.shard_map(
        form,
        mesh=mesh,
        in_specs=(
            P("grp", "tile"),
            P("grp", "tile"),
            P("grp"),
            P("tile"),
            P(("tile", "grp"), None, None),
            P("tile"),
            P("tile"),
        ),
        out_specs=P("grp", "tile"),
        check_vma=False,
    )
```

```python
import functools
import math

import jax
import jax.numpy as jnp
from jax import lax
from jax.experimental import pallas as pl
from jax.experimental.pallas import tpu as pltpu
from jax.sharding import PartitionSpec as P

ITERS = 2
MIB = 1024 * 1024


def contract_blocks(amp_rows, tile_set, source, target, local_blocks):
    row_count = amp_rows.shape[0]
    tile_width = tile_set.shape[1]
    tile_count = tile_set.shape[0]
    group_size = math.gcd(tile_count, 48)
    turns = tile_count // group_size
    blocks = amp_rows.reshape(row_count, -1, tile_width)
    packed_tiles = tile_set.reshape(turns, group_size, tile_width, tile_width)
    packed_source = source.reshape(turns, group_size)
    packed_target = target.reshape(turns, group_size)

    def advance(total_sum, packed):
        picked = jnp.take(blocks, packed[1], axis=1)
        partial_value = jnp.einsum(
            "rgc,gcd->rgd", picked, packed[0], preferred_element_type=jnp.float32
        )
        pieces = []
        for block in range(local_blocks):
            chosen = (packed[2] == block)[None, :, None]
            pieces.append(jnp.sum(jnp.where(chosen, partial_value, 0.0), axis=1))
        return (total_sum + jnp.stack(pieces, axis=1), None)

    initial = jnp.zeros((row_count, local_blocks, tile_width), jnp.float32)
    total_sum, unused = lax.scan(advance, initial, (packed_tiles, packed_source, packed_target))
    return total_sum.reshape(row_count, local_blocks * tile_width)


def general_form(amplitudes, driver, pair_energy, virt_energy, integrals, src_block, dst_block):
    tile_width = integrals.shape[1]
    local_blocks = virt_energy.shape[0] // tile_width
    denominator = virt_energy[None, :] - pair_energy[:, None]
    current = amplitudes
    first_tile = lax.axis_index("grp") * integrals.shape[0]
    my_source = lax.dynamic_slice_in_dim(src_block, first_tile, integrals.shape[0])
    my_target = lax.dynamic_slice_in_dim(dst_block, first_tile, integrals.shape[0])
    for iteration in range(ITERS):
        all_pairs = lax.all_gather(current, "grp", axis=0, tiled=True)
        whole_panel = lax.all_gather(all_pairs, "tile", axis=1, tiled=True)
        partial_value = contract_blocks(whole_panel, integrals, my_source, my_target, local_blocks)
        ladder = lax.psum_scatter(partial_value, "grp", scatter_dimension=0, tiled=True)
        current = ((driver + ladder) / denominator).astype(jnp.bfloat16)
    return current


NZ, NY, NX, NC = 4, 2, 2, 2
PARTS = 2


def z_swap(away):
    return [(t, t ^ (away * NY)) for t in range(NZ * NY)]


Y_SWAP = [(t, t ^ 1) for t in range(NZ * NY)]
X_SWAP = [(g, g ^ 2) for g in range(NX * NC)]
CORE_SWAP = [(g, g ^ 1) for g in range(NX * NC)]


def over_y(value):
    return lax.ppermute(value, "tile", Y_SWAP)


def over_x(value):
    return lax.ppermute(value, "grp", X_SWAP)


def over_core(value):
    return lax.ppermute(value, "grp", CORE_SWAP)


def parts_of(rows):
    return jnp.stack(jnp.split(rows, PARTS, axis=1))


def over_z(value):
    far = [lax.ppermute(value, "tile", z_swap(away)) for away in range(NZ // 2, NZ)]
    return [value] + [lax.ppermute(value, "tile", z_swap(away)) for away in range(1, NZ // 2)] + far


def gather_panel(shards, parts, build=None):
    a = jnp.stack([parts(shard) for shard in shards[: NZ // 2]])
    far, built = shards[NZ // 2 :], ()
    a_y, a_x = over_y(a), over_x(a)
    if build is not None:
        far[0], built = build(far[0])
        far[1], a_y, a_x, built = lax.optimization_barrier((far[1], a_y, a_x, built))
    b = jnp.stack([parts(shard) for shard in far])
    b, a_y, a_x, built = lax.optimization_barrier((b, a_y, a_x, built))
    b_x, a_xy, b_y = over_x(b), over_x(a_y), over_y(b)
    a_xy, b_xy = lax.optimization_barrier((a_xy, over_y(b_x)))
    return (jnp.stack([a, a_y, a_x]), jnp.stack([b, b_y, b_x]), jnp.stack([a_xy, b_xy])), built


PLACE = {(h, y, x): (2, h) if y and x else (h, y + 2 * x) for h in range(2) for y in range(NY) for x in range(NX)}


def sum_kernel(chunk, local_blocks, src_any, dst_any, tiles_any, total, given, which, tiles, src, dst, list_sem, tile_sem):
    steps = tiles.shape[0] // chunk
    half = local_blocks // NC
    shift = half.bit_length() - 1
    slots = given.shape[0]
    lists = [pltpu.make_async_copy(a, b, list_sem.at[i]) for i, (a, b) in enumerate(((src_any, src), (dst_any, dst)))]
    for copy in lists:
        copy.start()

    def tile_copy(step):
        part = pl.ds(step * chunk, chunk)
        return pltpu.make_async_copy(tiles_any.at[part], tiles.at[part], tile_sem.at[step])

    for step in range(steps):
        tile_copy(step).start()

    def clear(slot, carry):
        total[slot] = jnp.zeros(total.shape[1:], jnp.float32)
        return carry

    lax.fori_loop(0, total.shape[0], clear, 0, unroll=4)
    for copy in lists:
        copy.wait()
    grp = lax.axis_index("grp")
    here = lax.axis_index("tile") * local_blocks
    core = lax.rem(grp, NC)
    which[...] = jnp.full(which.shape, core, jnp.int32)
    kept = core * half
    first = grp * tiles.shape[0]

    def run(step, carry):
        tile_copy(step).wait()

        def add(j, carry):
            k = step * chunk + j
            target = dst[first + k] ^ kept
            slot = (target >> shift) * slots + ((src[first + k] ^ here) << shift) + (target & (half - 1))
            total[slot] += tiles[k].astype(jnp.float32)
            return carry

        lax.fori_loop(0, chunk, add, 0, unroll=8)
        return carry

    lax.fori_loop(0, steps, run, 0)

    def give(slot, carry):
        given[slot] = total[slots + slot]
        return carry

    lax.fori_loop(0, slots, give, 0, unroll=4)


def sum_tiles(integrals, src_block, dst_block, local_blocks, blocks, rows):
    count, width, _ = integrals.shape
    slots = blocks * local_blocks // NC
    chunk = math.gcd(count, 24)
    outside = pl.BlockSpec(memory_space=pl.ANY)
    local = pl.BlockSpec(memory_space=pltpu.VMEM)
    return pl.pallas_call(
        functools.partial(sum_kernel, chunk, local_blocks),
        in_specs=[outside] * 3,
        out_specs=[local] * 3,
        out_shape=[
            pltpu.VMEM((NC * slots, width, width), jnp.float32),
            pltpu.VMEM((slots, width, width), jnp.float32),
            pltpu.VMEM((rows, local_blocks // NC * width), jnp.int32),
        ],
        scratch_shapes=[
            pltpu.VMEM(integrals.shape, jnp.bfloat16),
            pltpu.SMEM(src_block.shape, jnp.int32),
            pltpu.SMEM(dst_block.shape, jnp.int32),
            pltpu.SemaphoreType.DMA((2,)),
            pltpu.SemaphoreType.DMA((count // chunk,)),
        ],
        compiler_params=pltpu.CompilerParams(vmem_limit_bytes=24 * MIB),
        cost_estimate=pl.CostEstimate(
            flops=count * width * width, bytes_accessed=2 * count * width * width + 4 * slots * width * width, transcendentals=0
        ),
        name="sum_tiles",
    )(*(pltpu.with_memory_space_constraint(a, pltpu.HBM) for a in (src_block, dst_block, integrals)))


def split_kernel(half, mine, got, high, low):
    width = mine.shape[-1]

    def split(block, carry):
        for d in range(half):
            value = mine[block * half + d] + got[block * half + d]
            top = value.astype(jnp.bfloat16)
            rest = value - top.astype(jnp.float32)
            high[block, :, d * width : (d + 1) * width] = top
            low[block, :, d * width : (d + 1) * width] = rest.astype(jnp.bfloat16)
        return carry

    lax.fori_loop(0, got.shape[0] // half, split, 0)


def split_parts(mine, got, half):
    slots, width, _ = got.shape
    shape = pltpu.VMEM((slots // half, width, half * width), jnp.bfloat16)
    local = pl.BlockSpec(memory_space=pltpu.VMEM)
    high, low = pl.pallas_call(
        functools.partial(split_kernel, half),
        in_specs=[local, local],
        out_specs=[local, local],
        out_shape=[shape, shape],
        compiler_params=pltpu.CompilerParams(vmem_limit_bytes=24 * MIB),
        cost_estimate=pl.CostEstimate(flops=3 * got.size, bytes_accessed=12 * got.size, transcendentals=0),
        name="split_parts",
    )(*(pltpu.with_memory_space_constraint(a, pltpu.VMEM) for a in (mine, got)))
    return high.reshape(-1, half * width), low.reshape(-1, half * width)


def contract_kernel(by_core, *refs):
    mine, other, (high, low, keep, send, rows) = refs[:3], refs[3:6], refs[6:]
    height, depth = mine[0].shape[-2:]
    core = lax.rem(lax.axis_index("grp"), NC)
    for away, pieces in enumerate((mine, other)):
        for part in range(PARTS):
            row_core = away if by_core else part ^ away
            half = part if by_core else (core if away == 0 else 1 - core)
            for (far, y, x), (piece, index) in PLACE.items():
                for near_z in range(NZ // 2):
                    z = far * (NZ // 2) + near_z
                    row = (x * NC + row_core) * height
                    column = (z * NY + y) * PARTS * depth + half * depth
                    if not by_core:
                        column = pl.multiple_of(column, depth)
                    rows[row : row + height, pl.ds(column, depth)] = pieces[piece][index, near_z, part]
    part = jnp.dot(rows[...], high[...], preferred_element_type=jnp.float32)
    part += jnp.dot(rows[...], low[...], preferred_element_type=jnp.float32)
    near = keep.shape[0]
    keep[...] = part[:near]
    send[...] = part[near:]


def contract(mine, other, high, low, by_core):
    height = mine[0].shape[-2]
    depth, columns = high.shape
    near = NC * height
    local = pl.BlockSpec(memory_space=pltpu.VMEM)
    shape = jax.ShapeDtypeStruct((near, columns), jnp.float32)
    return pl.pallas_call(
        functools.partial(contract_kernel, by_core),
        in_specs=[local] * 8,
        out_specs=[local, local],
        out_shape=[shape, shape],
        scratch_shapes=[pltpu.VMEM((NX * near, depth), jnp.bfloat16)],
        compiler_params=pltpu.CompilerParams(vmem_limit_bytes=24 * MIB),
        cost_estimate=pl.CostEstimate(
            flops=8 * near * depth * columns, bytes_accessed=4 * depth * columns + 4 * near * depth + 8 * near * columns, transcendentals=0
        ),
        name="contract_rows" if by_core else "contract_columns",
    )(*mine, *other, high, low)


def on_device(amplitudes, driver, pair_energy, virt_energy, integrals, src_block, dst_block):
    tile_width = integrals.shape[1]
    local_blocks = virt_energy.shape[0] // tile_width
    blocks, half = NZ * NY * local_blocks, local_blocks // NC
    cut = half * tile_width

    def build(ready):
        ready, src = lax.optimization_barrier((ready, src_block))
        return ready, sum_tiles(integrals, src, dst_block, local_blocks, blocks, amplitudes.shape[0])

    for iteration in range(ITERS):
        if iteration == 0:
            mine, (total, given, which) = gather_panel(over_z(amplitudes), parts_of, build)
            high, low = split_parts(total, over_core(given), half)
            lower = which == 0
            terms = jnp.stack([driver, virt_energy[None, :] - pair_energy[:, None]])
            kept_terms = jnp.where(lower, terms[..., :cut], terms[..., cut:])
            given_terms = jnp.where(lower, terms[..., cut:], terms[..., :cut])
            both_terms = jnp.stack([kept_terms, over_core(given_terms)], axis=1)
        else:
            mine, _ = gather_panel(over_z(shard), lambda parts: parts)
        other = tuple(over_core(piece) for piece in mine)
        keep, send = contract(mine, other, high, low, iteration == 0)
        ladder = (keep + over_x(send)).reshape(PARTS, -1, cut)
        shard = ((both_terms[0] + ladder) / both_terms[1]).astype(jnp.bfloat16)
    here, there = shard[0], over_core(shard[1])
    return jnp.concatenate([jnp.where(lower, here, there), jnp.where(lower, there, here)], axis=1)


def solution(mesh):
    form = on_device if (mesh.shape["tile"], mesh.shape["grp"]) == (NZ * NY, NX * NC) else general_form
    return jax.shard_map(
        form,
        mesh=mesh,
        in_specs=(
            P("grp", "tile"),
            P("grp", "tile"),
            P("grp"),
            P("tile"),
            P(("tile", "grp"), None, None),
            P("tile"),
            P("tile"),
        ),
        out_specs=P("grp", "tile"),
        check_vma=False,
    )
```

```python
import functools
import math

import jax
import jax.numpy as jnp
from jax import lax
from jax.experimental import pallas as pl
from jax.experimental.pallas import tpu as pltpu
from jax.sharding import PartitionSpec as P

ITERS = 2
MIB = 1024 * 1024


def contract_blocks(amp_rows, tile_set, source, target, local_blocks):
    row_count = amp_rows.shape[0]
    tile_width = tile_set.shape[1]
    tile_count = tile_set.shape[0]
    group_size = math.gcd(tile_count, 48)
    turns = tile_count // group_size
    blocks = amp_rows.reshape(row_count, -1, tile_width)
    packed_tiles = tile_set.reshape(turns, group_size, tile_width, tile_width)
    packed_source = source.reshape(turns, group_size)
    packed_target = target.reshape(turns, group_size)

    def advance(total_sum, packed):
        picked = jnp.take(blocks, packed[1], axis=1)
        partial_value = jnp.einsum(
            "rgc,gcd->rgd", picked, packed[0], preferred_element_type=jnp.float32
        )
        pieces = []
        for block in range(local_blocks):
            chosen = (packed[2] == block)[None, :, None]
            pieces.append(jnp.sum(jnp.where(chosen, partial_value, 0.0), axis=1))
        return (total_sum + jnp.stack(pieces, axis=1), None)

    initial = jnp.zeros((row_count, local_blocks, tile_width), jnp.float32)
    total_sum, unused = lax.scan(advance, initial, (packed_tiles, packed_source, packed_target))
    return total_sum.reshape(row_count, local_blocks * tile_width)


def general_form(amplitudes, driver, pair_energy, virt_energy, integrals, src_block, dst_block):
    tile_width = integrals.shape[1]
    local_blocks = virt_energy.shape[0] // tile_width
    denominator = virt_energy[None, :] - pair_energy[:, None]
    current = amplitudes
    first_tile = lax.axis_index("grp") * integrals.shape[0]
    my_source = lax.dynamic_slice_in_dim(src_block, first_tile, integrals.shape[0])
    my_target = lax.dynamic_slice_in_dim(dst_block, first_tile, integrals.shape[0])
    for iteration in range(ITERS):
        all_pairs = lax.all_gather(current, "grp", axis=0, tiled=True)
        whole_panel = lax.all_gather(all_pairs, "tile", axis=1, tiled=True)
        partial_value = contract_blocks(whole_panel, integrals, my_source, my_target, local_blocks)
        ladder = lax.psum_scatter(partial_value, "grp", scatter_dimension=0, tiled=True)
        current = ((driver + ladder) / denominator).astype(jnp.bfloat16)
    return current


NZ, NY, NX, NC = 4, 2, 2, 2
PARTS = 2


def z_swap(away):
    return [(t, t ^ (away * NY)) for t in range(NZ * NY)]


Y_SWAP = [(t, t ^ 1) for t in range(NZ * NY)]
X_SWAP = [(g, g ^ 2) for g in range(NX * NC)]
CORE_SWAP = [(g, g ^ 1) for g in range(NX * NC)]
DIAGONAL_SWAP = [(g, g ^ 3) for g in range(NX * NC)]


def over_y(value):
    return lax.ppermute(value, "tile", Y_SWAP)


def over_x(value):
    return lax.ppermute(value, "grp", X_SWAP)


def over_core(value):
    return lax.ppermute(value, "grp", CORE_SWAP)


def over_diagonal(value):
    return lax.ppermute(value, "grp", DIAGONAL_SWAP)


def parts_of(rows):
    return jnp.stack(jnp.split(rows, PARTS, axis=1))


def over_z(value):
    far = [lax.ppermute(value, "tile", z_swap(away)) for away in range(NZ // 2, NZ)]
    return [value] + [lax.ppermute(value, "tile", z_swap(away)) for away in range(1, NZ // 2)] + far


def gather_panel(shards, parts, build=None):
    built = build() if build is not None else ()
    if build is not None:
        shards, built = lax.optimization_barrier((shards, built))
    a = jnp.stack([parts(shard) for shard in shards[: NZ // 2]])
    a_y, a_x = over_y(a), over_x(a)
    b = jnp.stack([parts(shard) for shard in shards[NZ // 2 :]])
    if build is None:
        b, a_y = lax.optimization_barrier((b, a_y))
    b_x, b_y = over_x(b), over_y(b)
    a_y, a_x, b_x = lax.optimization_barrier((a_y, a_x, b_x))
    a_xy, b_xy = lax.optimization_barrier((over_x(a_y), over_y(b_x)))
    return (jnp.stack([a, a_y, a_x]), jnp.stack([b, b_y, b_x]), jnp.stack([a_xy, b_xy])), built


PLACE = {(h, y, x): (2, h) if y and x else (h, y + 2 * x) for h in range(2) for y in range(NY) for x in range(NX)}


def sum_kernel(chunk, local_blocks, src_any, dst_any, tiles_any, total, given, which, tiles, src, dst, list_sem, tile_sem):
    steps = tiles.shape[0] // chunk
    half = local_blocks // NC
    shift = half.bit_length() - 1
    slots = given.shape[0]
    lists = [pltpu.make_async_copy(a, b, list_sem.at[i]) for i, (a, b) in enumerate(((src_any, src), (dst_any, dst)))]
    for copy in lists:
        copy.start()

    def tile_copy(step):
        part = pl.ds(step * chunk, chunk)
        return pltpu.make_async_copy(tiles_any.at[part], tiles.at[part], tile_sem.at[step])

    for step in range(steps):
        tile_copy(step).start()

    def clear(slot, carry):
        total[slot] = jnp.zeros(total.shape[1:], jnp.float32)
        return carry

    lax.fori_loop(0, total.shape[0], clear, 0, unroll=4)
    for copy in lists:
        copy.wait()
    grp = lax.axis_index("grp")
    here = lax.axis_index("tile") * local_blocks
    core = lax.rem(grp, NC)
    which[...] = jnp.full(which.shape, core, jnp.int32)
    kept = core * half
    first = grp * tiles.shape[0]

    def run(step, carry):
        tile_copy(step).wait()

        def add(j, carry):
            k = step * chunk + j
            target = dst[first + k] ^ kept
            slot = (target >> shift) * slots + ((src[first + k] ^ here) << shift) + (target & (half - 1))
            total[slot] += tiles[k].astype(jnp.float32)
            return carry

        lax.fori_loop(0, chunk, add, 0, unroll=8)
        return carry

    lax.fori_loop(0, steps, run, 0)

    def give(slot, carry):
        given[slot] = total[slots + slot]
        return carry

    lax.fori_loop(0, slots, give, 0, unroll=4)


def sum_tiles(integrals, src_block, dst_block, local_blocks, blocks, rows):
    count, width, _ = integrals.shape
    slots = blocks * local_blocks // NC
    chunk = math.gcd(count, 24)
    outside = pl.BlockSpec(memory_space=pl.ANY)
    local = pl.BlockSpec(memory_space=pltpu.VMEM)
    return pl.pallas_call(
        functools.partial(sum_kernel, chunk, local_blocks),
        in_specs=[outside] * 3,
        out_specs=[local] * 3,
        out_shape=[
            pltpu.VMEM((NC * slots, width, width), jnp.float32),
            pltpu.VMEM((slots, width, width), jnp.float32),
            pltpu.VMEM((rows, local_blocks // NC * width), jnp.int32),
        ],
        scratch_shapes=[
            pltpu.VMEM(integrals.shape, jnp.bfloat16),
            pltpu.SMEM(src_block.shape, jnp.int32),
            pltpu.SMEM(dst_block.shape, jnp.int32),
            pltpu.SemaphoreType.DMA((2,)),
            pltpu.SemaphoreType.DMA((count // chunk,)),
        ],
        compiler_params=pltpu.CompilerParams(vmem_limit_bytes=24 * MIB),
        cost_estimate=pl.CostEstimate(
            flops=count * width * width, bytes_accessed=2 * count * width * width + 4 * slots * width * width, transcendentals=0
        ),
        name="sum_tiles",
    )(*(pltpu.with_memory_space_constraint(a, pltpu.HBM) for a in (src_block, dst_block, integrals)))


def split_kernel(half, mine, got, high, low):
    width = mine.shape[-1]

    def split(block, carry):
        for d in range(half):
            value = mine[block * half + d] + got[block * half + d]
            top = value.astype(jnp.bfloat16)
            rest = value - top.astype(jnp.float32)
            high[block, :, d * width : (d + 1) * width] = top
            low[block, :, d * width : (d + 1) * width] = rest.astype(jnp.bfloat16)
        return carry

    lax.fori_loop(0, got.shape[0] // half, split, 0)


def split_parts(mine, got, half):
    slots, width, _ = got.shape
    shape = pltpu.VMEM((slots // half, width, half * width), jnp.bfloat16)
    local = pl.BlockSpec(memory_space=pltpu.VMEM)
    high, low = pl.pallas_call(
        functools.partial(split_kernel, half),
        in_specs=[local, local],
        out_specs=[local, local],
        out_shape=[shape, shape],
        compiler_params=pltpu.CompilerParams(vmem_limit_bytes=24 * MIB),
        cost_estimate=pl.CostEstimate(flops=3 * got.size, bytes_accessed=12 * got.size, transcendentals=0),
        name="split_parts",
    )(*(pltpu.with_memory_space_constraint(a, pltpu.VMEM) for a in (mine, got)))
    return high.reshape(-1, half * width), low.reshape(-1, half * width)


def contract_kernel(by_core, across, *refs):
    mine, other, (high, low, out, rows) = refs[:3], refs[3:6], refs[6:]
    height, depth = mine[0].shape[-2:]
    core = lax.rem(lax.axis_index("grp"), NC)
    for away, pieces in enumerate((mine, other)):
        for part in range(PARTS):
            row_core = away if by_core else part ^ away
            half = part if by_core else (core if away == 0 else 1 - core)
            for (far, y, x), (piece, index) in PLACE.items():
                if x != across:
                    continue
                for near_z in range(NZ // 2):
                    z = far * (NZ // 2) + near_z
                    row = row_core * height
                    column = (z * NY + y) * PARTS * depth + half * depth
                    if not by_core:
                        column = pl.multiple_of(column, depth)
                    rows[row : row + height, pl.ds(column, depth)] = pieces[piece][index, near_z, part]
    total = jnp.dot(rows[...], high[...], preferred_element_type=jnp.float32)
    total += jnp.dot(rows[...], low[...], preferred_element_type=jnp.float32)
    for core in range(NC):
        out[core] = total[core * height : (core + 1) * height]


def contract(mine, other, high, low, by_core, across):
    height = mine[0].shape[-2]
    depth, columns = high.shape
    local = pl.BlockSpec(memory_space=pltpu.VMEM)
    return pl.pallas_call(
        functools.partial(contract_kernel, by_core, across),
        in_specs=[local] * 8,
        out_specs=local,
        out_shape=jax.ShapeDtypeStruct((NC, height, columns), jnp.float32),
        scratch_shapes=[pltpu.VMEM((NC * height, depth), jnp.bfloat16)],
        compiler_params=pltpu.CompilerParams(vmem_limit_bytes=24 * MIB),
        cost_estimate=pl.CostEstimate(
            flops=4 * NC * height * depth * columns, bytes_accessed=4 * depth * columns + 2 * NC * height * depth + 4 * NC * height * columns, transcendentals=0
        ),
        name="contract_sent" if across else "contract_kept",
    )(*mine, *other, high, low)


def on_device(amplitudes, driver, pair_energy, virt_energy, integrals, src_block, dst_block):
    tile_width = integrals.shape[1]
    local_blocks = virt_energy.shape[0] // tile_width
    blocks, half = NZ * NY * local_blocks, local_blocks // NC
    cut = half * tile_width

    def build():
        return sum_tiles(integrals, src_block, dst_block, local_blocks, blocks, amplitudes.shape[0])

    for iteration in range(ITERS):
        if iteration == 0:
            mine, (total, given, which) = gather_panel(over_z(amplitudes), parts_of, build)
            high, low = split_parts(total, over_core(given), half)
            lower = which == 0
            terms = jnp.stack([driver, virt_energy[None, :] - pair_energy[:, None]])
            kept_terms = jnp.where(lower, terms[..., :cut], terms[..., cut:])
            given_terms = jnp.where(lower, terms[..., cut:], terms[..., :cut])
            both_terms = jnp.stack([kept_terms, over_core(given_terms)], axis=1)
        else:
            mine, _ = gather_panel(over_z(shard), lambda parts: parts)
        other = tuple(over_core(piece) for piece in mine)
        sent = contract(mine, other, high, low, iteration == 0, 1)
        kept = contract(mine, other, high, low, iteration == 0, 0)
        if iteration < ITERS - 1:
            shard = ((both_terms[0] + (kept + over_x(sent))) / both_terms[1]).astype(jnp.bfloat16)
    here = kept[0] + over_x(sent[0])
    there = over_core(kept[1]) + over_diagonal(sent[1])
    ladder = jnp.concatenate([jnp.where(lower, here, there), jnp.where(lower, there, here)], axis=1)
    return ((driver + ladder) / (virt_energy[None, :] - pair_energy[:, None])).astype(jnp.bfloat16)


def solution(mesh):
    form = on_device if (mesh.shape["tile"], mesh.shape["grp"]) == (NZ * NY, NX * NC) else general_form
    return jax.shard_map(
        form,
        mesh=mesh,
        in_specs=(
            P("grp", "tile"),
            P("grp", "tile"),
            P("grp"),
            P("tile"),
            P(("tile", "grp"), None, None),
            P("tile"),
            P("tile"),
        ),
        out_specs=P("grp", "tile"),
        check_vma=False,
    )
```

```python
import functools
import math

import jax
import jax.numpy as jnp
from jax import lax
from jax.experimental import pallas as pl
from jax.experimental.pallas import tpu as pltpu
from jax.sharding import PartitionSpec as P

ITERS = 2
MIB = 1024 * 1024


def contract_blocks(amp_rows, tile_set, source, target, local_blocks):
    row_count = amp_rows.shape[0]
    tile_width = tile_set.shape[1]
    tile_count = tile_set.shape[0]
    group_size = math.gcd(tile_count, 48)
    turns = tile_count // group_size
    blocks = amp_rows.reshape(row_count, -1, tile_width)
    packed_tiles = tile_set.reshape(turns, group_size, tile_width, tile_width)
    packed_source = source.reshape(turns, group_size)
    packed_target = target.reshape(turns, group_size)

    def advance(total_sum, packed):
        picked = jnp.take(blocks, packed[1], axis=1)
        partial_value = jnp.einsum(
            "rgc,gcd->rgd", picked, packed[0], preferred_element_type=jnp.float32
        )
        pieces = []
        for block in range(local_blocks):
            chosen = (packed[2] == block)[None, :, None]
            pieces.append(jnp.sum(jnp.where(chosen, partial_value, 0.0), axis=1))
        return (total_sum + jnp.stack(pieces, axis=1), None)

    initial = jnp.zeros((row_count, local_blocks, tile_width), jnp.float32)
    total_sum, unused = lax.scan(advance, initial, (packed_tiles, packed_source, packed_target))
    return total_sum.reshape(row_count, local_blocks * tile_width)


def general_form(amplitudes, driver, pair_energy, virt_energy, integrals, src_block, dst_block):
    tile_width = integrals.shape[1]
    local_blocks = virt_energy.shape[0] // tile_width
    denominator = virt_energy[None, :] - pair_energy[:, None]
    current = amplitudes
    first_tile = lax.axis_index("grp") * integrals.shape[0]
    my_source = lax.dynamic_slice_in_dim(src_block, first_tile, integrals.shape[0])
    my_target = lax.dynamic_slice_in_dim(dst_block, first_tile, integrals.shape[0])
    for iteration in range(ITERS):
        all_pairs = lax.all_gather(current, "grp", axis=0, tiled=True)
        whole_panel = lax.all_gather(all_pairs, "tile", axis=1, tiled=True)
        partial_value = contract_blocks(whole_panel, integrals, my_source, my_target, local_blocks)
        ladder = lax.psum_scatter(partial_value, "grp", scatter_dimension=0, tiled=True)
        current = ((driver + ladder) / denominator).astype(jnp.bfloat16)
    return current


NZ, NY, NX, NC = 4, 2, 2, 2
PARTS = 2


def z_swap(away):
    return [(t, t ^ (away * NY)) for t in range(NZ * NY)]


Y_SWAP = [(t, t ^ 1) for t in range(NZ * NY)]
X_SWAP = [(g, g ^ 2) for g in range(NX * NC)]
CORE_SWAP = [(g, g ^ 1) for g in range(NX * NC)]
DIAGONAL_SWAP = [(g, g ^ 3) for g in range(NX * NC)]


def over_y(value):
    return lax.ppermute(value, "tile", Y_SWAP)


def over_x(value):
    return lax.ppermute(value, "grp", X_SWAP)


def over_core(value):
    return lax.ppermute(value, "grp", CORE_SWAP)


def over_diagonal(value):
    return lax.ppermute(value, "grp", DIAGONAL_SWAP)


def parts_of(rows):
    return jnp.stack(jnp.split(rows, PARTS, axis=1))


def over_z(value):
    return [lax.ppermute(value, "tile", z_swap(away)) for away in range(NZ - 1, 0, -1)] + [value]


def gather_panel(near):
    first, second = near
    first_y, second_x = over_y(first), over_x(second)
    first_x, second_y = over_x(first), over_y(second)
    first_xy, second_xy = over_x(first_y), over_y(second_x)
    return near, jnp.stack([first_y, second_x]), jnp.stack([first_x, second_y]), jnp.stack([first_xy, second_xy])


def place_of(part, y, x):
    if y and x:
        return 3
    if y or x:
        return 1 if (part == 0) == (y == 1) else 2
    return 0


def sum_kernel(chunk, local_blocks, src_any, dst_any, tiles_any, total, given, which, tiles, src, dst, list_sem, tile_sem):
    steps = tiles.shape[0] // chunk
    half = local_blocks // NC
    shift = half.bit_length() - 1
    slots = given.shape[0]
    lists = [pltpu.make_async_copy(a, b, list_sem.at[i]) for i, (a, b) in enumerate(((src_any, src), (dst_any, dst)))]
    for copy in lists:
        copy.start()

    def tile_copy(step):
        part = pl.ds(step * chunk, chunk)
        return pltpu.make_async_copy(tiles_any.at[part], tiles.at[part], tile_sem.at[step])

    for step in range(steps):
        tile_copy(step).start()

    def clear(slot, carry):
        total[slot] = jnp.zeros(total.shape[1:], jnp.float32)
        return carry

    lax.fori_loop(0, total.shape[0], clear, 0, unroll=4)
    for copy in lists:
        copy.wait()
    grp = lax.axis_index("grp")
    here = (lax.axis_index("tile") ^ (NZ - 1) * NY) * local_blocks
    core = lax.rem(grp, NC)
    which[...] = jnp.full(which.shape, core, jnp.int32)
    kept = core * half
    first = grp * tiles.shape[0]

    def run(step, carry):
        tile_copy(step).wait()

        def add(j, carry):
            k = step * chunk + j
            target = dst[first + k] ^ kept
            slot = (target >> shift) * slots + ((src[first + k] ^ here) << shift) + (target & (half - 1))
            total[slot] += tiles[k].astype(jnp.float32)
            return carry

        lax.fori_loop(0, chunk, add, 0, unroll=8)
        return carry

    lax.fori_loop(0, steps, run, 0)

    def give(slot, carry):
        given[slot] = total[slots + slot]
        return carry

    lax.fori_loop(0, slots, give, 0, unroll=4)


def sum_tiles(integrals, src_block, dst_block, local_blocks, blocks, rows):
    count, width, _ = integrals.shape
    slots = blocks * local_blocks // NC
    chunk = math.gcd(count, 24)
    outside = pl.BlockSpec(memory_space=pl.ANY)
    local = pl.BlockSpec(memory_space=pltpu.VMEM)
    return pl.pallas_call(
        functools.partial(sum_kernel, chunk, local_blocks),
        in_specs=[outside] * 3,
        out_specs=[local] * 3,
        out_shape=[
            pltpu.VMEM((NC * slots, width, width), jnp.float32),
            pltpu.VMEM((slots, width, width), jnp.float32),
            pltpu.VMEM((rows, local_blocks // NC * width), jnp.int32),
        ],
        scratch_shapes=[
            pltpu.VMEM(integrals.shape, jnp.bfloat16),
            pltpu.SMEM(src_block.shape, jnp.int32),
            pltpu.SMEM(dst_block.shape, jnp.int32),
            pltpu.SemaphoreType.DMA((2,)),
            pltpu.SemaphoreType.DMA((count // chunk,)),
        ],
        compiler_params=pltpu.CompilerParams(vmem_limit_bytes=24 * MIB),
        cost_estimate=pl.CostEstimate(
            flops=count * width * width, bytes_accessed=2 * count * width * width + 4 * slots * width * width, transcendentals=0
        ),
        name="sum_tiles",
    )(*(pltpu.with_memory_space_constraint(a, pltpu.HBM) for a in (src_block, dst_block, integrals)))


def split_kernel(half, mine, got, high, low):
    width = mine.shape[-1]

    def split(block, carry):
        for d in range(half):
            value = mine[block * half + d] + got[block * half + d]
            top = value.astype(jnp.bfloat16)
            rest = value - top.astype(jnp.float32)
            high[block, :, d * width : (d + 1) * width] = top
            low[block, :, d * width : (d + 1) * width] = rest.astype(jnp.bfloat16)
        return carry

    lax.fori_loop(0, got.shape[0] // half, split, 0)


def split_parts(mine, got, half):
    slots, width, _ = got.shape
    shape = pltpu.VMEM((slots // half, width, half * width), jnp.bfloat16)
    local = pl.BlockSpec(memory_space=pltpu.VMEM)
    high, low = pl.pallas_call(
        functools.partial(split_kernel, half),
        in_specs=[local, local],
        out_specs=[local, local],
        out_shape=[shape, shape],
        compiler_params=pltpu.CompilerParams(vmem_limit_bytes=24 * MIB),
        cost_estimate=pl.CostEstimate(flops=3 * got.size, bytes_accessed=12 * got.size, transcendentals=0),
        name="split_parts",
    )(*(pltpu.with_memory_space_constraint(a, pltpu.VMEM) for a in (mine, got)))
    return high.reshape(-1, half * width), low.reshape(-1, half * width)


def contract_kernel(by_core, across, *refs):
    mine, other, (high, low, out, rows) = refs[:4], refs[4:8], refs[8:]
    height, depth = mine[0].shape[-2:]
    core = lax.rem(lax.axis_index("grp"), NC)
    for away, pieces in enumerate((mine, other)):
        for part in range(PARTS):
            row_core = away if by_core else part ^ away
            half = part if by_core else (core if away == 0 else 1 - core)
            for y in range(NY):
                piece = pieces[place_of(part, y, across)]
                for z in range(NZ):
                    row = row_core * height
                    column = (z * NY + y) * PARTS * depth + half * depth
                    if not by_core:
                        column = pl.multiple_of(column, depth)
                    rows[row : row + height, pl.ds(column, depth)] = piece[part, z]
    total = jnp.dot(rows[...], high[...], preferred_element_type=jnp.float32)
    total += jnp.dot(rows[...], low[...], preferred_element_type=jnp.float32)
    for core in range(NC):
        out[core] = total[core * height : (core + 1) * height]


def contract(mine, other, high, low, by_core, across):
    height = mine[0].shape[-2]
    depth, columns = high.shape
    local = pl.BlockSpec(memory_space=pltpu.VMEM)
    return pl.pallas_call(
        functools.partial(contract_kernel, by_core, across),
        in_specs=[local] * 10,
        out_specs=local,
        out_shape=jax.ShapeDtypeStruct((NC, height, columns), jnp.float32),
        scratch_shapes=[pltpu.VMEM((NC * height, depth), jnp.bfloat16)],
        compiler_params=pltpu.CompilerParams(vmem_limit_bytes=24 * MIB),
        cost_estimate=pl.CostEstimate(
            flops=4 * NC * height * depth * columns, bytes_accessed=4 * depth * columns + 2 * NC * height * depth + 4 * NC * height * columns, transcendentals=0
        ),
        name="contract_sent" if across else "contract_kept",
    )(*mine, *other, high, low)


def on_device(amplitudes, driver, pair_energy, virt_energy, integrals, src_block, dst_block):
    tile_width = integrals.shape[1]
    local_blocks = virt_energy.shape[0] // tile_width
    blocks, half = NZ * NY * local_blocks, local_blocks // NC
    cut = half * tile_width

    total, given, which = sum_tiles(integrals, src_block, dst_block, local_blocks, blocks, amplitudes.shape[0])
    for iteration in range(ITERS):
        if iteration == 0:
            *far, own = over_z(amplitudes)
            own, given = lax.optimization_barrier((own, given))
            near = jnp.stack([parts_of(value) for value in (*far, own)], axis=1)
            high, low = split_parts(total, over_core(given), half)
            lower = which == 0
            terms = jnp.stack([driver, virt_energy[None, :] - pair_energy[:, None]])
            kept_terms = jnp.where(lower, terms[..., :cut], terms[..., cut:])
            given_terms = jnp.where(lower, terms[..., cut:], terms[..., :cut])
            both_terms = jnp.stack([kept_terms, over_core(given_terms)], axis=1)
        else:
            near = jnp.stack(over_z(shard), axis=1)
        mine = gather_panel(near)
        other = tuple(over_core(piece) for piece in mine)
        sent = contract(mine, other, high, low, iteration == 0, 1)
        kept = contract(mine, other, high, low, iteration == 0, 0)
        if iteration < ITERS - 1:
            shard = ((both_terms[0] + (kept + over_x(sent))) / both_terms[1]).astype(jnp.bfloat16)
    here = kept[0] + over_x(sent[0])
    there = over_core(kept[1]) + over_diagonal(sent[1])
    ladder = jnp.concatenate([jnp.where(lower, here, there), jnp.where(lower, there, here)], axis=1)
    return ((driver + ladder) / (virt_energy[None, :] - pair_energy[:, None])).astype(jnp.bfloat16)


def solution(mesh):
    form = on_device if (mesh.shape["tile"], mesh.shape["grp"]) == (NZ * NY, NX * NC) else general_form
    return jax.shard_map(
        form,
        mesh=mesh,
        in_specs=(
            P("grp", "tile"),
            P("grp", "tile"),
            P("grp"),
            P("tile"),
            P(("tile", "grp"), None, None),
            P("tile"),
            P("tile"),
        ),
        out_specs=P("grp", "tile"),
        check_vma=False,
    )
```

```python
import functools
import math

import jax
import jax.numpy as jnp
from jax import lax
from jax.experimental import pallas as pl
from jax.experimental.pallas import tpu as pltpu
from jax.sharding import PartitionSpec as P

ITERS = 2
MIB = 1024 * 1024


def contract_blocks(amp_rows, tile_set, source, target, local_blocks):
    row_count = amp_rows.shape[0]
    tile_width = tile_set.shape[1]
    tile_count = tile_set.shape[0]
    group_size = math.gcd(tile_count, 48)
    turns = tile_count // group_size
    blocks = amp_rows.reshape(row_count, -1, tile_width)
    packed_tiles = tile_set.reshape(turns, group_size, tile_width, tile_width)
    packed_source = source.reshape(turns, group_size)
    packed_target = target.reshape(turns, group_size)

    def advance(total_sum, packed):
        picked = jnp.take(blocks, packed[1], axis=1)
        partial_value = jnp.einsum(
            "rgc,gcd->rgd", picked, packed[0], preferred_element_type=jnp.float32
        )
        pieces = []
        for block in range(local_blocks):
            chosen = (packed[2] == block)[None, :, None]
            pieces.append(jnp.sum(jnp.where(chosen, partial_value, 0.0), axis=1))
        return (total_sum + jnp.stack(pieces, axis=1), None)

    initial = jnp.zeros((row_count, local_blocks, tile_width), jnp.float32)
    total_sum, unused = lax.scan(advance, initial, (packed_tiles, packed_source, packed_target))
    return total_sum.reshape(row_count, local_blocks * tile_width)


def general_form(amplitudes, driver, pair_energy, virt_energy, integrals, src_block, dst_block):
    tile_width = integrals.shape[1]
    local_blocks = virt_energy.shape[0] // tile_width
    denominator = virt_energy[None, :] - pair_energy[:, None]
    current = amplitudes
    first_tile = lax.axis_index("grp") * integrals.shape[0]
    my_source = lax.dynamic_slice_in_dim(src_block, first_tile, integrals.shape[0])
    my_target = lax.dynamic_slice_in_dim(dst_block, first_tile, integrals.shape[0])
    for iteration in range(ITERS):
        all_pairs = lax.all_gather(current, "grp", axis=0, tiled=True)
        whole_panel = lax.all_gather(all_pairs, "tile", axis=1, tiled=True)
        partial_value = contract_blocks(whole_panel, integrals, my_source, my_target, local_blocks)
        ladder = lax.psum_scatter(partial_value, "grp", scatter_dimension=0, tiled=True)
        current = ((driver + ladder) / denominator).astype(jnp.bfloat16)
    return current


NZ, NY, NX, NC = 4, 2, 2, 2
PARTS = 2


def z_swap(away):
    return [(t, t ^ (away * NY)) for t in range(NZ * NY)]


Y_SWAP = [(t, t ^ 1) for t in range(NZ * NY)]
X_SWAP = [(g, g ^ 2) for g in range(NX * NC)]
CORE_SWAP = [(g, g ^ 1) for g in range(NX * NC)]
DIAGONAL_SWAP = [(g, g ^ 3) for g in range(NX * NC)]


def over_y(value):
    return lax.ppermute(value, "tile", Y_SWAP)


def over_x(value):
    return lax.ppermute(value, "grp", X_SWAP)


def over_core(value):
    return lax.ppermute(value, "grp", CORE_SWAP)


def over_diagonal(value):
    return lax.ppermute(value, "grp", DIAGONAL_SWAP)


def parts_of(rows):
    return jnp.stack(jnp.split(rows, PARTS, axis=1))


def over_z(value):
    far = [lax.ppermute(value, "tile", z_swap(away)) for away in range(NZ // 2, NZ)]
    return [value] + [lax.ppermute(value, "tile", z_swap(away)) for away in range(1, NZ // 2)] + far


def gather_panel(shards, parts, build=None):
    built = () if build is None else build()
    if build is not None:
        shards, built = lax.optimization_barrier((shards, built))
    a = jnp.stack([parts(shard) for shard in shards[: NZ // 2]])
    b = jnp.stack([parts(shard) for shard in shards[NZ // 2 :]])
    a_y, a_x = over_y(a), over_x(a)
    if build is None:
        b, a_y = lax.optimization_barrier((b, a_y))
    b_x, b_y = over_x(b), over_y(b)
    if build is None:
        b_x, a_x = lax.optimization_barrier((b_x, a_x))
    a_xy, b_xy = over_x(a_y), over_y(b_x)
    if build is None:
        a_xy, b_xy = lax.optimization_barrier((a_xy, b_xy))
    else:
        a_x, a_xy = lax.optimization_barrier((a_x, a_xy))
    return tuple(jnp.stack(pair) for pair in ((a, b), (a_y, b_x), (a_x, b_y), (a_xy, b_xy))), built


PLACE = {(h, y, x): (3 * y * x or (y + x) * (1 + (x ^ h)), h) for h in range(2) for y in range(NY) for x in range(NX)}


def sum_kernel(chunk, local_blocks, src_any, dst_any, tiles_any, total, given, which, tiles, src, dst, list_sem, tile_sem):
    steps = tiles.shape[0] // chunk
    half = local_blocks // NC
    shift = half.bit_length() - 1
    slots = given.shape[0]
    lists = [pltpu.make_async_copy(a, b, list_sem.at[i]) for i, (a, b) in enumerate(((src_any, src), (dst_any, dst)))]
    for copy in lists:
        copy.start()

    def tile_copy(step):
        part = pl.ds(step * chunk, chunk)
        return pltpu.make_async_copy(tiles_any.at[part], tiles.at[part], tile_sem.at[step])

    for step in range(steps):
        tile_copy(step).start()

    def clear(slot, carry):
        total[slot] = jnp.zeros(total.shape[1:], jnp.float32)
        return carry

    lax.fori_loop(0, total.shape[0], clear, 0, unroll=4)
    for copy in lists:
        copy.wait()
    grp = lax.axis_index("grp")
    here = lax.axis_index("tile") * local_blocks
    core = lax.rem(grp, NC)
    which[...] = jnp.full(which.shape, core, jnp.int32)
    kept = core * half
    first = grp * tiles.shape[0]

    def run(step, carry):
        tile_copy(step).wait()

        def add(j, carry):
            k = step * chunk + j
            target = dst[first + k] ^ kept
            slot = (target >> shift) * slots + ((src[first + k] ^ here) << shift) + (target & (half - 1))
            total[slot] += tiles[k].astype(jnp.float32)
            return carry

        lax.fori_loop(0, chunk, add, 0, unroll=8)
        return carry

    lax.fori_loop(0, steps, run, 0)

    def give(slot, carry):
        given[slot] = total[slots + slot]
        return carry

    lax.fori_loop(0, slots, give, 0, unroll=4)


def sum_tiles(integrals, src_block, dst_block, local_blocks, blocks, rows):
    count, width, _ = integrals.shape
    slots = blocks * local_blocks // NC
    chunk = math.gcd(count, 24)
    outside = pl.BlockSpec(memory_space=pl.ANY)
    local = pl.BlockSpec(memory_space=pltpu.VMEM)
    return pl.pallas_call(
        functools.partial(sum_kernel, chunk, local_blocks),
        in_specs=[outside] * 3,
        out_specs=[local] * 3,
        out_shape=[
            pltpu.VMEM((NC * slots, width, width), jnp.float32),
            pltpu.VMEM((slots, width, width), jnp.float32),
            pltpu.VMEM((rows, local_blocks // NC * width), jnp.int32),
        ],
        scratch_shapes=[
            pltpu.VMEM(integrals.shape, jnp.bfloat16),
            pltpu.SMEM(src_block.shape, jnp.int32),
            pltpu.SMEM(dst_block.shape, jnp.int32),
            pltpu.SemaphoreType.DMA((2,)),
            pltpu.SemaphoreType.DMA((count // chunk,)),
        ],
        compiler_params=pltpu.CompilerParams(vmem_limit_bytes=24 * MIB),
        cost_estimate=pl.CostEstimate(
            flops=count * width * width, bytes_accessed=2 * count * width * width + 4 * slots * width * width, transcendentals=0
        ),
        name="sum_tiles",
    )(*(pltpu.with_memory_space_constraint(a, pltpu.HBM) for a in (src_block, dst_block, integrals)))


def split_kernel(half, mine, got, high, low):
    width = mine.shape[-1]

    def split(block, carry):
        for d in range(half):
            value = mine[block * half + d] + got[block * half + d]
            top = value.astype(jnp.bfloat16)
            rest = value - top.astype(jnp.float32)
            high[block, :, d * width : (d + 1) * width] = top
            low[block, :, d * width : (d + 1) * width] = rest.astype(jnp.bfloat16)
        return carry

    lax.fori_loop(0, got.shape[0] // half, split, 0)


def split_parts(mine, got, half):
    slots, width, _ = got.shape
    shape = pltpu.VMEM((slots // half, width, half * width), jnp.bfloat16)
    local = pl.BlockSpec(memory_space=pltpu.VMEM)
    high, low = pl.pallas_call(
        functools.partial(split_kernel, half),
        in_specs=[local, local],
        out_specs=[local, local],
        out_shape=[shape, shape],
        compiler_params=pltpu.CompilerParams(vmem_limit_bytes=24 * MIB),
        cost_estimate=pl.CostEstimate(flops=3 * got.size, bytes_accessed=12 * got.size, transcendentals=0),
        name="split_parts",
    )(*(pltpu.with_memory_space_constraint(a, pltpu.VMEM) for a in (mine, got)))
    return high.reshape(-1, half * width), low.reshape(-1, half * width)


def contract_kernel(by_core, across, *refs):
    mine, other, (high, low, out, rows) = refs[:4], refs[4:8], refs[8:]
    height, depth = mine[0].shape[-2:]
    core = lax.rem(lax.axis_index("grp"), NC)
    for away, pieces in enumerate((mine, other)):
        for part in range(PARTS):
            row_core = away if by_core else part ^ away
            half = part if by_core else (core if away == 0 else 1 - core)
            for (far, y, x), (piece, index) in PLACE.items():
                if x != across:
                    continue
                for near_z in range(NZ // 2):
                    z = far * (NZ // 2) + near_z
                    row = row_core * height
                    column = (z * NY + y) * PARTS * depth + half * depth
                    if not by_core:
                        column = pl.multiple_of(column, depth)
                    rows[row : row + height, pl.ds(column, depth)] = pieces[piece][index, near_z, part]
    total = jnp.dot(rows[...], high[...], preferred_element_type=jnp.float32)
    total += jnp.dot(rows[...], low[...], preferred_element_type=jnp.float32)
    for core in range(NC):
        out[core] = total[core * height : (core + 1) * height]


def contract(mine, other, high, low, by_core, across):
    height = mine[0].shape[-2]
    depth, columns = high.shape
    local = pl.BlockSpec(memory_space=pltpu.VMEM)
    return pl.pallas_call(
        functools.partial(contract_kernel, by_core, across),
        in_specs=[local] * 10,
        out_specs=local,
        out_shape=jax.ShapeDtypeStruct((NC, height, columns), jnp.float32),
        scratch_shapes=[pltpu.VMEM((NC * height, depth), jnp.bfloat16)],
        compiler_params=pltpu.CompilerParams(vmem_limit_bytes=24 * MIB),
        cost_estimate=pl.CostEstimate(
            flops=4 * NC * height * depth * columns, bytes_accessed=4 * depth * columns + 2 * NC * height * depth + 4 * NC * height * columns, transcendentals=0
        ),
        name="contract_sent" if across else "contract_kept",
    )(*mine, *other, high, low)


def on_device(amplitudes, driver, pair_energy, virt_energy, integrals, src_block, dst_block):
    tile_width = integrals.shape[1]
    local_blocks = virt_energy.shape[0] // tile_width
    blocks, half = NZ * NY * local_blocks, local_blocks // NC
    cut = half * tile_width

    def build():
        return sum_tiles(integrals, src_block, dst_block, local_blocks, blocks, amplitudes.shape[0])

    for iteration in range(ITERS):
        if iteration == 0:
            mine, (total, given, which) = gather_panel(over_z(amplitudes), parts_of, build)
            high, low = split_parts(total, over_core(given), half)
            lower = which == 0
            terms = jnp.stack([driver, virt_energy[None, :] - pair_energy[:, None]])
            kept_terms = jnp.where(lower, terms[..., :cut], terms[..., cut:])
            given_terms = jnp.where(lower, terms[..., cut:], terms[..., :cut])
            both_terms = jnp.stack([kept_terms, over_core(given_terms)], axis=1)
        else:
            mine, _ = gather_panel(over_z(shard), lambda parts: parts)
        other = tuple(over_core(piece) for piece in mine)
        sent = contract(mine, other, high, low, iteration == 0, 1)
        kept = contract(mine, other, high, low, iteration == 0, 0)
        if iteration < ITERS - 1:
            shard = ((both_terms[0] + (kept + over_x(sent))) / both_terms[1]).astype(jnp.bfloat16)
    here = kept[0] + over_x(sent[0])
    there = over_core(kept[1]) + over_diagonal(sent[1])
    ladder = jnp.concatenate([jnp.where(lower, here, there), jnp.where(lower, there, here)], axis=1)
    return ((driver + ladder) / (virt_energy[None, :] - pair_energy[:, None])).astype(jnp.bfloat16)


def solution(mesh):
    form = on_device if (mesh.shape["tile"], mesh.shape["grp"]) == (NZ * NY, NX * NC) else general_form
    return jax.shard_map(
        form,
        mesh=mesh,
        in_specs=(
            P("grp", "tile"),
            P("grp", "tile"),
            P("grp"),
            P("tile"),
            P(("tile", "grp"), None, None),
            P("tile"),
            P("tile"),
        ),
        out_specs=P("grp", "tile"),
        check_vma=False,
    )
```

```python
import functools
import math

import jax
import jax.numpy as jnp
from jax import lax
from jax.experimental import pallas as pl
from jax.experimental.pallas import tpu as pltpu
from jax.sharding import PartitionSpec as P

ITERS = 2
MIB = 1024 * 1024


def contract_blocks(amp_rows, tile_set, source, target, local_blocks):
    row_count = amp_rows.shape[0]
    tile_width = tile_set.shape[1]
    tile_count = tile_set.shape[0]
    group_size = math.gcd(tile_count, 48)
    turns = tile_count // group_size
    blocks = amp_rows.reshape(row_count, -1, tile_width)
    packed_tiles = tile_set.reshape(turns, group_size, tile_width, tile_width)
    packed_source = source.reshape(turns, group_size)
    packed_target = target.reshape(turns, group_size)

    def advance(total_sum, packed):
        picked = jnp.take(blocks, packed[1], axis=1)
        partial_value = jnp.einsum(
            "rgc,gcd->rgd", picked, packed[0], preferred_element_type=jnp.float32
        )
        pieces = []
        for block in range(local_blocks):
            chosen = (packed[2] == block)[None, :, None]
            pieces.append(jnp.sum(jnp.where(chosen, partial_value, 0.0), axis=1))
        return (total_sum + jnp.stack(pieces, axis=1), None)

    initial = jnp.zeros((row_count, local_blocks, tile_width), jnp.float32)
    total_sum, unused = lax.scan(advance, initial, (packed_tiles, packed_source, packed_target))
    return total_sum.reshape(row_count, local_blocks * tile_width)


def general_form(amplitudes, driver, pair_energy, virt_energy, integrals, src_block, dst_block):
    tile_width = integrals.shape[1]
    local_blocks = virt_energy.shape[0] // tile_width
    denominator = virt_energy[None, :] - pair_energy[:, None]
    current = amplitudes
    first_tile = lax.axis_index("grp") * integrals.shape[0]
    my_source = lax.dynamic_slice_in_dim(src_block, first_tile, integrals.shape[0])
    my_target = lax.dynamic_slice_in_dim(dst_block, first_tile, integrals.shape[0])
    for iteration in range(ITERS):
        all_pairs = lax.all_gather(current, "grp", axis=0, tiled=True)
        whole_panel = lax.all_gather(all_pairs, "tile", axis=1, tiled=True)
        partial_value = contract_blocks(whole_panel, integrals, my_source, my_target, local_blocks)
        ladder = lax.psum_scatter(partial_value, "grp", scatter_dimension=0, tiled=True)
        current = ((driver + ladder) / denominator).astype(jnp.bfloat16)
    return current


NZ, NY, NX, NC = 4, 2, 2, 2
PARTS = 2


def z_swap(away):
    return [(t, t ^ (away * NY)) for t in range(NZ * NY)]


Y_SWAP = [(t, t ^ 1) for t in range(NZ * NY)]
X_SWAP = [(g, g ^ 2) for g in range(NX * NC)]
XY_SWAP = [(d, d ^ (NX * NC + 2)) for d in range(NZ * NY * NX * NC)]
CORE_SWAP = [(g, g ^ 1) for g in range(NX * NC)]
DIAGONAL_SWAP = [(g, g ^ 3) for g in range(NX * NC)]


def over_y(value):
    return lax.ppermute(value, "tile", Y_SWAP)


def over_x(value):
    return lax.ppermute(value, "grp", X_SWAP)


def over_xy(value):
    return lax.ppermute(value, ("tile", "grp"), XY_SWAP)


def over_core(value):
    return lax.ppermute(value, "grp", CORE_SWAP)


def over_diagonal(value):
    return lax.ppermute(value, "grp", DIAGONAL_SWAP)


def parts_of(rows):
    return jnp.stack(jnp.split(rows, PARTS, axis=1))


def over_z(value):
    far = [lax.ppermute(value, "tile", z_swap(away)) for away in range(NZ // 2, NZ)]
    return [value] + [lax.ppermute(value, "tile", z_swap(away)) for away in range(1, NZ // 2)] + far


def gather_panel(shards, parts, build=None):
    built = () if build is None else build()
    if build is not None:
        shards, built = lax.optimization_barrier((shards, built))
    a = jnp.stack([parts(shard) for shard in shards[: NZ // 2]])
    b = jnp.stack([parts(shard) for shard in shards[NZ // 2 :]])
    here = jnp.stack([a, b])
    here_other = over_core(here)
    a_xy, a_x, a_y = over_xy(a), over_x(a), over_y(a)
    b_xy, b_x, b_y = over_xy(b), over_x(b), over_y(b)
    a_xy, a_x, a_y, b_xy, b_x = lax.optimization_barrier((a_xy, a_x, a_y, b_xy, b_x))
    here_other, b_y = lax.optimization_barrier((here_other, b_y))
    a_around, b_around = jnp.stack([a_xy, a_x, a_y]), jnp.stack([b_xy, b_x, b_y])
    return (here, a_around, b_around), (here_other, over_core(a_around), over_core(b_around)), built


PLACE = {(h, y, x): (h + 1, 2 - 2 * x + (x & ~y)) if y or x else (0, h) for h in range(2) for y in range(NY) for x in range(NX)}


def sum_kernel(chunk, local_blocks, src_any, dst_any, tiles_any, total, given, which, tiles, src, dst, list_sem, tile_sem):
    steps = tiles.shape[0] // chunk
    half = local_blocks // NC
    shift = half.bit_length() - 1
    slots = given.shape[0]
    lists = [pltpu.make_async_copy(a, b, list_sem.at[i]) for i, (a, b) in enumerate(((src_any, src), (dst_any, dst)))]
    for copy in lists:
        copy.start()

    def tile_copy(step):
        part = pl.ds(step * chunk, chunk)
        return pltpu.make_async_copy(tiles_any.at[part], tiles.at[part], tile_sem.at[step])

    for step in range(steps):
        tile_copy(step).start()

    def clear(slot, carry):
        total[slot] = jnp.zeros(total.shape[1:], jnp.float32)
        return carry

    lax.fori_loop(0, total.shape[0], clear, 0, unroll=4)
    for copy in lists:
        copy.wait()
    grp = lax.axis_index("grp")
    here = lax.axis_index("tile") * local_blocks
    core = lax.rem(grp, NC)
    which[...] = jnp.full(which.shape, core, jnp.int32)
    kept = core * half
    first = grp * tiles.shape[0]

    def run(step, carry):
        tile_copy(step).wait()

        def add(j, carry):
            k = step * chunk + j
            target = dst[first + k] ^ kept
            slot = (target >> shift) * slots + ((src[first + k] ^ here) << shift) + (target & (half - 1))
            total[slot] += tiles[k].astype(jnp.float32)
            return carry

        lax.fori_loop(0, chunk, add, 0, unroll=8)
        return carry

    lax.fori_loop(0, steps, run, 0)

    def give(slot, carry):
        given[slot] = total[slots + slot]
        return carry

    lax.fori_loop(0, slots, give, 0, unroll=4)


def sum_tiles(integrals, src_block, dst_block, local_blocks, blocks, rows):
    count, width, _ = integrals.shape
    slots = blocks * local_blocks // NC
    chunk = math.gcd(count, 24)
    outside = pl.BlockSpec(memory_space=pl.ANY)
    local = pl.BlockSpec(memory_space=pltpu.VMEM)
    return pl.pallas_call(
        functools.partial(sum_kernel, chunk, local_blocks),
        in_specs=[outside] * 3,
        out_specs=[local] * 3,
        out_shape=[
            pltpu.VMEM((NC * slots, width, width), jnp.float32),
            pltpu.VMEM((slots, width, width), jnp.float32),
            pltpu.VMEM((rows, local_blocks // NC * width), jnp.int32),
        ],
        scratch_shapes=[
            pltpu.VMEM(integrals.shape, jnp.bfloat16),
            pltpu.SMEM(src_block.shape, jnp.int32),
            pltpu.SMEM(dst_block.shape, jnp.int32),
            pltpu.SemaphoreType.DMA((2,)),
            pltpu.SemaphoreType.DMA((count // chunk,)),
        ],
        compiler_params=pltpu.CompilerParams(vmem_limit_bytes=24 * MIB),
        cost_estimate=pl.CostEstimate(
            flops=count * width * width, bytes_accessed=2 * count * width * width + 4 * slots * width * width, transcendentals=0
        ),
        name="sum_tiles",
    )(*(pltpu.with_memory_space_constraint(a, pltpu.HBM) for a in (src_block, dst_block, integrals)))


def split_kernel(half, mine, got, high, low):
    width = mine.shape[-1]

    def split(block, carry):
        for d in range(half):
            value = mine[block * half + d] + got[block * half + d]
            top = value.astype(jnp.bfloat16)
            rest = value - top.astype(jnp.float32)
            high[block, :, d * width : (d + 1) * width] = top
            low[block, :, d * width : (d + 1) * width] = rest.astype(jnp.bfloat16)
        return carry

    lax.fori_loop(0, got.shape[0] // half, split, 0)


def split_parts(mine, got, half):
    slots, width, _ = got.shape
    shape = pltpu.VMEM((slots // half, width, half * width), jnp.bfloat16)
    local = pl.BlockSpec(memory_space=pltpu.VMEM)
    high, low = pl.pallas_call(
        functools.partial(split_kernel, half),
        in_specs=[local, local],
        out_specs=[local, local],
        out_shape=[shape, shape],
        compiler_params=pltpu.CompilerParams(vmem_limit_bytes=24 * MIB),
        cost_estimate=pl.CostEstimate(flops=3 * got.size, bytes_accessed=12 * got.size, transcendentals=0),
        name="split_parts",
    )(*(pltpu.with_memory_space_constraint(a, pltpu.VMEM) for a in (mine, got)))
    return high.reshape(-1, half * width), low.reshape(-1, half * width)


def contract_kernel(by_core, across, *refs):
    mine, other, (high, low, out, rows) = refs[:3], refs[3:6], refs[6:]
    height, depth = mine[0].shape[-2:]
    core = lax.rem(lax.axis_index("grp"), NC)
    for away, pieces in enumerate((mine, other)):
        for part in range(PARTS):
            row_core = away if by_core else part ^ away
            half = part if by_core else (core if away == 0 else 1 - core)
            for (far, y, x), (piece, index) in PLACE.items():
                if x != across:
                    continue
                for near_z in range(NZ // 2):
                    z = far * (NZ // 2) + near_z
                    row = row_core * height
                    column = (z * NY + y) * PARTS * depth + half * depth
                    if not by_core:
                        column = pl.multiple_of(column, depth)
                    rows[row : row + height, pl.ds(column, depth)] = pieces[piece][index, near_z, part]
    total = jnp.dot(rows[...], high[...], preferred_element_type=jnp.float32)
    total += jnp.dot(rows[...], low[...], preferred_element_type=jnp.float32)
    for core in range(NC):
        out[core] = total[core * height : (core + 1) * height]


def contract(mine, other, high, low, by_core, across):
    height = mine[0].shape[-2]
    depth, columns = high.shape
    local = pl.BlockSpec(memory_space=pltpu.VMEM)
    return pl.pallas_call(
        functools.partial(contract_kernel, by_core, across),
        in_specs=[local] * 8,
        out_specs=local,
        out_shape=jax.ShapeDtypeStruct((NC, height, columns), jnp.float32),
        scratch_shapes=[pltpu.VMEM((NC * height, depth), jnp.bfloat16)],
        compiler_params=pltpu.CompilerParams(vmem_limit_bytes=24 * MIB),
        cost_estimate=pl.CostEstimate(
            flops=4 * NC * height * depth * columns, bytes_accessed=4 * depth * columns + 2 * NC * height * depth + 4 * NC * height * columns, transcendentals=0
        ),
        name="contract_sent" if across else "contract_kept",
    )(*mine, *other, high, low)


def on_device(amplitudes, driver, pair_energy, virt_energy, integrals, src_block, dst_block):
    tile_width = integrals.shape[1]
    local_blocks = virt_energy.shape[0] // tile_width
    blocks, half = NZ * NY * local_blocks, local_blocks // NC
    cut = half * tile_width

    def build():
        return sum_tiles(integrals, src_block, dst_block, local_blocks, blocks, amplitudes.shape[0])

    for iteration in range(ITERS):
        if iteration == 0:
            mine, other, (total, given, which) = gather_panel(over_z(amplitudes), parts_of, build)
            high, low = split_parts(total, over_core(given), half)
            lower = which == 0
            terms = jnp.stack([driver, virt_energy[None, :] - pair_energy[:, None]])
            kept_terms = jnp.where(lower, terms[..., :cut], terms[..., cut:])
            given_terms = jnp.where(lower, terms[..., cut:], terms[..., :cut])
            both_terms = jnp.stack([kept_terms, over_core(given_terms)], axis=1)
        else:
            mine, other, _ = gather_panel(over_z(shard), lambda parts: parts)
        sent = contract(mine, other, high, low, iteration == 0, 1)
        kept = contract(mine, other, high, low, iteration == 0, 0)
        if iteration < ITERS - 1:
            shard = ((both_terms[0] + (kept + over_x(sent))) / both_terms[1]).astype(jnp.bfloat16)
    here = kept[0] + over_x(sent[0])
    there = over_core(kept[1]) + over_diagonal(sent[1])
    ladder = jnp.concatenate([jnp.where(lower, here, there), jnp.where(lower, there, here)], axis=1)
    return ((driver + ladder) / (virt_energy[None, :] - pair_energy[:, None])).astype(jnp.bfloat16)


def solution(mesh):
    form = on_device if (mesh.shape["tile"], mesh.shape["grp"]) == (NZ * NY, NX * NC) else general_form
    return jax.shard_map(
        form,
        mesh=mesh,
        in_specs=(
            P("grp", "tile"),
            P("grp", "tile"),
            P("grp"),
            P("tile"),
            P(("tile", "grp"), None, None),
            P("tile"),
            P("tile"),
        ),
        out_specs=P("grp", "tile"),
        check_vma=False,
    )
```

```python
import functools
import math

import jax
import jax.numpy as jnp
from jax import lax
from jax.experimental import pallas as pl
from jax.experimental.pallas import tpu as pltpu
from jax.sharding import PartitionSpec as P

ITERS = 2
MIB = 1024 * 1024


def contract_blocks(amp_rows, tile_set, source, target, local_blocks):
    row_count = amp_rows.shape[0]
    tile_width = tile_set.shape[1]
    tile_count = tile_set.shape[0]
    group_size = math.gcd(tile_count, 48)
    turns = tile_count // group_size
    blocks = amp_rows.reshape(row_count, -1, tile_width)
    packed_tiles = tile_set.reshape(turns, group_size, tile_width, tile_width)
    packed_source = source.reshape(turns, group_size)
    packed_target = target.reshape(turns, group_size)

    def advance(total_sum, packed):
        picked = jnp.take(blocks, packed[1], axis=1)
        partial_value = jnp.einsum(
            "rgc,gcd->rgd", picked, packed[0], preferred_element_type=jnp.float32
        )
        pieces = []
        for block in range(local_blocks):
            chosen = (packed[2] == block)[None, :, None]
            pieces.append(jnp.sum(jnp.where(chosen, partial_value, 0.0), axis=1))
        return (total_sum + jnp.stack(pieces, axis=1), None)

    initial = jnp.zeros((row_count, local_blocks, tile_width), jnp.float32)
    total_sum, unused = lax.scan(advance, initial, (packed_tiles, packed_source, packed_target))
    return total_sum.reshape(row_count, local_blocks * tile_width)


def general_form(amplitudes, driver, pair_energy, virt_energy, integrals, src_block, dst_block):
    tile_width = integrals.shape[1]
    local_blocks = virt_energy.shape[0] // tile_width
    denominator = virt_energy[None, :] - pair_energy[:, None]
    current = amplitudes
    first_tile = lax.axis_index("grp") * integrals.shape[0]
    my_source = lax.dynamic_slice_in_dim(src_block, first_tile, integrals.shape[0])
    my_target = lax.dynamic_slice_in_dim(dst_block, first_tile, integrals.shape[0])
    for iteration in range(ITERS):
        all_pairs = lax.all_gather(current, "grp", axis=0, tiled=True)
        whole_panel = lax.all_gather(all_pairs, "tile", axis=1, tiled=True)
        partial_value = contract_blocks(whole_panel, integrals, my_source, my_target, local_blocks)
        ladder = lax.psum_scatter(partial_value, "grp", scatter_dimension=0, tiled=True)
        current = ((driver + ladder) / denominator).astype(jnp.bfloat16)
    return current


NZ, NY, NX, NC = 4, 2, 2, 2
PARTS = 2
CORE, X, Y, Z = 1, NC, NC * NX, NC * NX * NY


def swap(value, core_0, core_1=None):
    away = (core_0, core_0 if core_1 is None else core_1)
    return lax.ppermute(value, ("tile", "grp"), [(d, d ^ away[d % NC]) for d in range(NZ * NY * NX * NC)])


def parts_of(rows):
    return jnp.stack(jnp.split(rows, PARTS, axis=1))


def gather_panel(shard, parts, build=None):
    both = jnp.stack([parts(shard), parts(swap(shard, CORE))])
    built = () if build is None else build()
    near, far = swap(both, Z, 2 * Z), swap(both, 0, 3 * Z)
    if build is not None:
        near, far, built = lax.optimization_barrier((near, far, built))
    here = jnp.stack([far, near])
    first, second = swap(here, Y, X), swap(here, X, Y)
    return (here, first, second, swap(first, X, Y)), built


def sum_kernel(chunk, local_blocks, src_any, dst_any, tiles_any, total, given, which, tiles, src, dst, list_sem, tile_sem):
    steps = tiles.shape[0] // chunk
    half = local_blocks // NC
    shift = half.bit_length() - 1
    slots = given.shape[0]
    lists = [pltpu.make_async_copy(a, b, list_sem.at[i]) for i, (a, b) in enumerate(((src_any, src), (dst_any, dst)))]
    for copy in lists:
        copy.start()

    def tile_copy(step):
        part = pl.ds(step * chunk, chunk)
        return pltpu.make_async_copy(tiles_any.at[part], tiles.at[part], tile_sem.at[step])

    for step in range(steps):
        tile_copy(step).start()

    def clear(slot, carry):
        total[slot] = jnp.zeros(total.shape[1:], jnp.float32)
        return carry

    lax.fori_loop(0, total.shape[0], clear, 0, unroll=4)
    for copy in lists:
        copy.wait()
    grp = lax.axis_index("grp")
    here = lax.axis_index("tile") * local_blocks
    core = lax.rem(grp, NC)
    which[...] = jnp.full(which.shape, core, jnp.int32)
    kept = core * half
    first = grp * tiles.shape[0]

    def run(step, carry):
        tile_copy(step).wait()

        def add(j, carry):
            k = step * chunk + j
            target = dst[first + k] ^ kept
            slot = (target >> shift) * slots + ((src[first + k] ^ here) << shift) + (target & (half - 1))
            total[slot] += tiles[k].astype(jnp.float32)
            return carry

        lax.fori_loop(0, chunk, add, 0, unroll=8)
        return carry

    lax.fori_loop(0, steps, run, 0)

    def give(slot, carry):
        given[slot] = total[slots + slot]
        return carry

    lax.fori_loop(0, slots, give, 0, unroll=4)


def sum_tiles(integrals, src_block, dst_block, local_blocks, blocks, rows):
    count, width, _ = integrals.shape
    slots = blocks * local_blocks // NC
    chunk = math.gcd(count, 24)
    outside = pl.BlockSpec(memory_space=pl.ANY)
    local = pl.BlockSpec(memory_space=pltpu.VMEM)
    return pl.pallas_call(
        functools.partial(sum_kernel, chunk, local_blocks),
        in_specs=[outside] * 3,
        out_specs=[local] * 3,
        out_shape=[
            pltpu.VMEM((NC * slots, width, width), jnp.float32),
            pltpu.VMEM((slots, width, width), jnp.float32),
            pltpu.VMEM((rows, local_blocks // NC * width), jnp.int32),
        ],
        scratch_shapes=[
            pltpu.VMEM(integrals.shape, jnp.bfloat16),
            pltpu.SMEM(src_block.shape, jnp.int32),
            pltpu.SMEM(dst_block.shape, jnp.int32),
            pltpu.SemaphoreType.DMA((2,)),
            pltpu.SemaphoreType.DMA((count // chunk,)),
        ],
        compiler_params=pltpu.CompilerParams(vmem_limit_bytes=24 * MIB),
        cost_estimate=pl.CostEstimate(
            flops=count * width * width, bytes_accessed=2 * count * width * width + 4 * slots * width * width, transcendentals=0
        ),
        name="sum_tiles",
    )(*(pltpu.with_memory_space_constraint(a, pltpu.HBM) for a in (src_block, dst_block, integrals)))


def split_kernel(half, mine, got, high, low):
    width = mine.shape[-1]

    def split(block, carry):
        for d in range(half):
            value = mine[block * half + d] + got[block * half + d]
            top = value.astype(jnp.bfloat16)
            rest = value - top.astype(jnp.float32)
            high[block, :, d * width : (d + 1) * width] = top
            low[block, :, d * width : (d + 1) * width] = rest.astype(jnp.bfloat16)
        return carry

    lax.fori_loop(0, got.shape[0] // half, split, 0)


def split_parts(mine, got, half):
    slots, width, _ = got.shape
    shape = pltpu.VMEM((slots // half, width, half * width), jnp.bfloat16)
    local = pl.BlockSpec(memory_space=pltpu.VMEM)
    high, low = pl.pallas_call(
        functools.partial(split_kernel, half),
        in_specs=[local, local],
        out_specs=[local, local],
        out_shape=[shape, shape],
        compiler_params=pltpu.CompilerParams(vmem_limit_bytes=24 * MIB),
        cost_estimate=pl.CostEstimate(flops=3 * got.size, bytes_accessed=12 * got.size, transcendentals=0),
        name="split_parts",
    )(*(pltpu.with_memory_space_constraint(a, pltpu.VMEM) for a in (mine, got)))
    return high.reshape(-1, half * width), low.reshape(-1, half * width)


def contract_kernel(by_core, across, *refs):
    mine, other, (high, low, out, rows) = refs[:4], refs[4:8], refs[8:]
    height, depth = mine[0].shape[-2:]

    def assemble(core):
        for side, pieces in enumerate((mine, other)):
            carrier = core ^ side
            for step, piece in enumerate(pieces):
                x, y = (step // 2, step % 2) if carrier == 0 else (step % 2, step // 2)
                if x != across:
                    continue
                for slot in range(NZ // 2):
                    z = slot if carrier == 0 else NZ - 1 - slot
                    for holder in range(NC):
                        owner = side ^ holder
                        for part in range(PARTS):
                            row = (owner if by_core else owner ^ part) * height
                            half = part if by_core else core ^ owner
                            column = ((z * NY + y) * PARTS + half) * depth
                            rows[row : row + height, column : column + depth] = piece[slot, holder, part]

    for core in range(NC):
        pl.when(lax.rem(lax.axis_index("grp"), NC) == core)(functools.partial(assemble, core))
    total = jnp.dot(rows[...], high[...], preferred_element_type=jnp.float32)
    total += jnp.dot(rows[...], low[...], preferred_element_type=jnp.float32)
    for core in range(NC):
        out[core] = total[core * height : (core + 1) * height]


def contract(mine, other, high, low, by_core, across):
    height = mine[0].shape[-2]
    depth, columns = high.shape
    local = pl.BlockSpec(memory_space=pltpu.VMEM)
    return pl.pallas_call(
        functools.partial(contract_kernel, by_core, across),
        in_specs=[local] * 10,
        out_specs=local,
        out_shape=jax.ShapeDtypeStruct((NC, height, columns), jnp.float32),
        scratch_shapes=[pltpu.VMEM((NC * height, depth), jnp.bfloat16)],
        compiler_params=pltpu.CompilerParams(vmem_limit_bytes=24 * MIB),
        cost_estimate=pl.CostEstimate(
            flops=4 * NC * height * depth * columns, bytes_accessed=4 * depth * columns + 2 * NC * height * depth + 4 * NC * height * columns, transcendentals=0
        ),
        name="contract_sent" if across else "contract_kept",
    )(*mine, *other, high, low)


def on_device(amplitudes, driver, pair_energy, virt_energy, integrals, src_block, dst_block):
    tile_width = integrals.shape[1]
    local_blocks = virt_energy.shape[0] // tile_width
    blocks, half = NZ * NY * local_blocks, local_blocks // NC
    cut = half * tile_width

    def build():
        return sum_tiles(integrals, src_block, dst_block, local_blocks, blocks, amplitudes.shape[0])

    for iteration in range(ITERS):
        if iteration == 0:
            mine, (total, given, which) = gather_panel(amplitudes, parts_of, build)
            high, low = split_parts(total, swap(given, CORE), half)
            lower = which == 0
            terms = jnp.stack([driver, virt_energy[None, :] - pair_energy[:, None]])
            kept_terms = jnp.where(lower, terms[..., :cut], terms[..., cut:])
            given_terms = jnp.where(lower, terms[..., cut:], terms[..., :cut])
            both_terms = jnp.stack([kept_terms, swap(given_terms, CORE)], axis=1)
        else:
            mine, _ = gather_panel(shard, lambda parts: parts)
        other = tuple(swap(piece, CORE) for piece in mine)
        sent = contract(mine, other, high, low, iteration == 0, 1)
        kept = contract(mine, other, high, low, iteration == 0, 0)
        if iteration < ITERS - 1:
            shard = ((both_terms[0] + (kept + swap(sent, X))) / both_terms[1]).astype(jnp.bfloat16)
    here = kept[0] + swap(sent[0], X)
    there = swap(kept[1], CORE) + swap(sent[1], X + CORE)
    ladder = jnp.concatenate([jnp.where(lower, here, there), jnp.where(lower, there, here)], axis=1)
    return ((driver + ladder) / (virt_energy[None, :] - pair_energy[:, None])).astype(jnp.bfloat16)


def solution(mesh):
    form = on_device if (mesh.shape["tile"], mesh.shape["grp"]) == (NZ * NY, NX * NC) else general_form
    return jax.shard_map(
        form,
        mesh=mesh,
        in_specs=(
            P("grp", "tile"),
            P("grp", "tile"),
            P("grp"),
            P("tile"),
            P(("tile", "grp"), None, None),
            P("tile"),
            P("tile"),
        ),
        out_specs=P("grp", "tile"),
        check_vma=False,
    )
```

```python
import functools
import math

import jax
import jax.numpy as jnp
from jax import lax
from jax.experimental import pallas as pl
from jax.experimental.pallas import tpu as pltpu
from jax.sharding import PartitionSpec as P

ITERS = 2
MIB = 1024 * 1024


def contract_blocks(amp_rows, tile_set, source, target, local_blocks):
    row_count = amp_rows.shape[0]
    tile_width = tile_set.shape[1]
    tile_count = tile_set.shape[0]
    group_size = math.gcd(tile_count, 48)
    turns = tile_count // group_size
    blocks = amp_rows.reshape(row_count, -1, tile_width)
    packed_tiles = tile_set.reshape(turns, group_size, tile_width, tile_width)
    packed_source = source.reshape(turns, group_size)
    packed_target = target.reshape(turns, group_size)

    def advance(total_sum, packed):
        picked = jnp.take(blocks, packed[1], axis=1)
        partial_value = jnp.einsum(
            "rgc,gcd->rgd", picked, packed[0], preferred_element_type=jnp.float32
        )
        pieces = []
        for block in range(local_blocks):
            chosen = (packed[2] == block)[None, :, None]
            pieces.append(jnp.sum(jnp.where(chosen, partial_value, 0.0), axis=1))
        return (total_sum + jnp.stack(pieces, axis=1), None)

    initial = jnp.zeros((row_count, local_blocks, tile_width), jnp.float32)
    total_sum, unused = lax.scan(advance, initial, (packed_tiles, packed_source, packed_target))
    return total_sum.reshape(row_count, local_blocks * tile_width)


def general_form(amplitudes, driver, pair_energy, virt_energy, integrals, src_block, dst_block):
    tile_width = integrals.shape[1]
    local_blocks = virt_energy.shape[0] // tile_width
    denominator = virt_energy[None, :] - pair_energy[:, None]
    current = amplitudes
    first_tile = lax.axis_index("grp") * integrals.shape[0]
    my_source = lax.dynamic_slice_in_dim(src_block, first_tile, integrals.shape[0])
    my_target = lax.dynamic_slice_in_dim(dst_block, first_tile, integrals.shape[0])
    for iteration in range(ITERS):
        all_pairs = lax.all_gather(current, "grp", axis=0, tiled=True)
        whole_panel = lax.all_gather(all_pairs, "tile", axis=1, tiled=True)
        partial_value = contract_blocks(whole_panel, integrals, my_source, my_target, local_blocks)
        ladder = lax.psum_scatter(partial_value, "grp", scatter_dimension=0, tiled=True)
        current = ((driver + ladder) / denominator).astype(jnp.bfloat16)
    return current


NZ, NY, NX, NC = 4, 2, 2, 2
PARTS = 2


def z_swap(away):
    return [(t, t ^ (away * NY)) for t in range(NZ * NY)]


Y_SWAP = [(t, t ^ 1) for t in range(NZ * NY)]
X_SWAP = [(g, g ^ 2) for g in range(NX * NC)]
CORE_SWAP = [(g, g ^ 1) for g in range(NX * NC)]
DIAGONAL_SWAP = [(g, g ^ 3) for g in range(NX * NC)]


def over_y(value):
    return lax.ppermute(value, "tile", Y_SWAP)


def over_x(value):
    return lax.ppermute(value, "grp", X_SWAP)


def over_core(value):
    return lax.ppermute(value, "grp", CORE_SWAP)


def over_diagonal(value):
    return lax.ppermute(value, "grp", DIAGONAL_SWAP)


def parts_of(rows):
    return jnp.stack(jnp.split(rows, PARTS, axis=1))


def over_z(value):
    far = [lax.ppermute(value, "tile", z_swap(away)) for away in range(NZ // 2, NZ)]
    return [value] + [lax.ppermute(value, "tile", z_swap(away)) for away in range(1, NZ // 2)] + far


def gather_panel(shards, parts, build=None):
    built = [] if build is None else list(build())
    if build is not None:
        shards, built = lax.optimization_barrier((shards, built))
    a = jnp.stack([parts(shard) for shard in shards[: NZ // 2]])
    b = jnp.stack([parts(shard) for shard in shards[NZ // 2 :]])
    a_y, a_x = over_y(a), over_x(a)
    if build is not None:
        b_x, b_y, a_xy = over_x(b), over_y(b), over_x(a_y)
        a_x, a_xy = lax.optimization_barrier((a_x, a_xy))
        return [jnp.stack(pair) for pair in ((a, b), (a_y, b_x), (a_x, b_y), (a_xy, over_y(b_x)))], built
    b, a_y = lax.optimization_barrier((b, a_y))
    b_x, b_y, a_xy = over_x(b), over_y(b), over_x(a_y)
    b_x, a_x = lax.optimization_barrier((b_x, a_x))
    a_xy, b_xy, b_y = lax.optimization_barrier((a_xy, over_y(b_x), b_y))
    return [jnp.stack(group) for group in ((a, b, b_y), (a_y, a_x, b_x), (a_xy, b_xy))], built


PLACES = (
    {(0, 0, 0): (0, 0), (1, 0, 0): (0, 1), (0, 1, 0): (1, 0), (1, 0, 1): (1, 1), (0, 0, 1): (2, 0), (1, 1, 0): (2, 1), (0, 1, 1): (3, 0), (1, 1, 1): (3, 1)},
    {(0, 0, 0): (0, 0), (1, 0, 0): (0, 1), (1, 1, 0): (0, 2), (0, 1, 0): (1, 0), (0, 0, 1): (1, 1), (1, 0, 1): (1, 2), (0, 1, 1): (2, 0), (1, 1, 1): (2, 1)},
)


def sum_kernel(chunk, local_blocks, src_any, dst_any, tiles_any, total, given, which, tiles, src, dst, list_sem, tile_sem):
    steps = tiles.shape[0] // chunk
    half = local_blocks // NC
    shift = half.bit_length() - 1
    slots = given.shape[0]
    lists = [pltpu.make_async_copy(a, b, list_sem.at[i]) for i, (a, b) in enumerate(((src_any, src), (dst_any, dst)))]
    for copy in lists:
        copy.start()

    def tile_copy(step):
        part = pl.ds(step * chunk, chunk)
        return pltpu.make_async_copy(tiles_any.at[part], tiles.at[part], tile_sem.at[step])

    for step in range(steps):
        tile_copy(step).start()

    def clear(slot, carry):
        total[slot] = jnp.zeros(total.shape[1:], jnp.float32)
        return carry

    lax.fori_loop(0, total.shape[0], clear, 0, unroll=4)
    for copy in lists:
        copy.wait()
    grp = lax.axis_index("grp")
    here = lax.axis_index("tile") * local_blocks
    core = lax.rem(grp, NC)
    which[...] = jnp.full(which.shape, core, jnp.int32)
    kept = core * half
    first = grp * tiles.shape[0]

    def run(step, carry):
        tile_copy(step).wait()

        def add(j, carry):
            k = step * chunk + j
            target = dst[first + k] ^ kept
            slot = (target >> shift) * slots + ((src[first + k] ^ here) << shift) + (target & (half - 1))
            total[slot] += tiles[k].astype(jnp.float32)
            return carry

        lax.fori_loop(0, chunk, add, 0, unroll=8)
        return carry

    lax.fori_loop(0, steps, run, 0)

    def give(slot, carry):
        given[slot] = total[slots + slot]
        return carry

    lax.fori_loop(0, slots, give, 0, unroll=4)


def sum_tiles(integrals, src_block, dst_block, local_blocks, blocks, rows):
    count, width, _ = integrals.shape
    slots = blocks * local_blocks // NC
    chunk = math.gcd(count, 24)
    outside = pl.BlockSpec(memory_space=pl.ANY)
    local = pl.BlockSpec(memory_space=pltpu.VMEM)
    return pl.pallas_call(
        functools.partial(sum_kernel, chunk, local_blocks),
        in_specs=[outside] * 3,
        out_specs=[local] * 3,
        out_shape=[
            pltpu.VMEM((NC * slots, width, width), jnp.float32),
            pltpu.VMEM((slots, width, width), jnp.float32),
            pltpu.VMEM((rows, local_blocks // NC * width), jnp.int32),
        ],
        scratch_shapes=[
            pltpu.VMEM(integrals.shape, jnp.bfloat16),
            pltpu.SMEM(src_block.shape, jnp.int32),
            pltpu.SMEM(dst_block.shape, jnp.int32),
            pltpu.SemaphoreType.DMA((2,)),
            pltpu.SemaphoreType.DMA((count // chunk,)),
        ],
        compiler_params=pltpu.CompilerParams(vmem_limit_bytes=24 * MIB),
        cost_estimate=pl.CostEstimate(
            flops=count * width * width, bytes_accessed=2 * count * width * width + 4 * slots * width * width, transcendentals=0
        ),
        name="sum_tiles",
    )(*(pltpu.with_memory_space_constraint(a, pltpu.HBM) for a in (src_block, dst_block, integrals)))


def split_kernel(half, mine, got, high, low):
    width = mine.shape[-1]

    def split(block, carry):
        for d in range(half):
            value = mine[block * half + d] + got[block * half + d]
            top = value.astype(jnp.bfloat16)
            rest = value - top.astype(jnp.float32)
            high[block, :, d * width : (d + 1) * width] = top
            low[block, :, d * width : (d + 1) * width] = rest.astype(jnp.bfloat16)
        return carry

    lax.fori_loop(0, got.shape[0] // half, split, 0)


def split_parts(mine, got, half):
    slots, width, _ = got.shape
    shape = pltpu.VMEM((slots // half, width, half * width), jnp.bfloat16)
    local = pl.BlockSpec(memory_space=pltpu.VMEM)
    high, low = pl.pallas_call(
        functools.partial(split_kernel, half),
        in_specs=[local, local],
        out_specs=[local, local],
        out_shape=[shape, shape],
        compiler_params=pltpu.CompilerParams(vmem_limit_bytes=24 * MIB),
        cost_estimate=pl.CostEstimate(flops=3 * got.size, bytes_accessed=12 * got.size, transcendentals=0),
        name="split_parts",
    )(*(pltpu.with_memory_space_constraint(a, pltpu.VMEM) for a in (mine, got)))
    return high.reshape(-1, half * width), low.reshape(-1, half * width)


def contract_kernel(by_core, across, along, used, *refs):
    mine, other = (dict(zip(used, part)) for part in (refs[: len(used)], refs[len(used) : 2 * len(used)]))
    high, low, *before, out, rows = refs[2 * len(used) :]
    height, depth = next(iter(mine.values())).shape[-2:]
    wide = PARTS * depth
    core = lax.rem(lax.axis_index("grp"), NC)
    spans = [(z, y) for z in range(NZ) for y in along]
    for away, pieces in enumerate((mine, other)):
        for part in range(PARTS):
            row = (away if by_core else part ^ away) * height
            half = part if by_core else (core if away == 0 else 1 - core)
            for span, (z, y) in enumerate(spans):
                piece, index = PLACES[not by_core][z // (NZ // 2), y, across]
                column = span * wide + half * depth
                if not by_core:
                    column = pl.multiple_of(column, depth)
                rows[row : row + height, pl.ds(column, depth)] = pieces[piece][index, z % (NZ // 2), part]
    total = sum(ref[...].reshape(NC * height, -1) for ref in before)
    if len(along) == NY:
        chunks = [(rows[...], slice(None))]
    else:
        chunks = [(rows[:, i * wide : (i + 1) * wide], pl.ds((z * NY + y) * wide, wide)) for i, (z, y) in enumerate(spans)]
    for left, right in chunks:
        for matrix in (high, low):
            total += jnp.dot(left, matrix[right, :], preferred_element_type=jnp.float32)
    for core in range(NC):
        out[core] = total[core * height : (core + 1) * height]


def contract(mine, other, high, low, by_core, across, along=range(NY), before=()):
    used = sorted({PLACES[not by_core][half, y, across][0] for half in range(2) for y in along})
    height = mine[0].shape[-2]
    depth, columns = high.shape
    depth = depth // NY * len(along)
    local = pl.BlockSpec(memory_space=pltpu.VMEM)
    return pl.pallas_call(
        functools.partial(contract_kernel, by_core, across, tuple(along), used),
        in_specs=[local] * (2 * len(used) + 2 + len(before)),
        out_specs=local,
        out_shape=jax.ShapeDtypeStruct((NC, height, columns), jnp.float32),
        scratch_shapes=[pltpu.VMEM((NC * height, depth), jnp.bfloat16)],
        compiler_params=pltpu.CompilerParams(vmem_limit_bytes=24 * MIB),
        cost_estimate=pl.CostEstimate(
            flops=4 * NC * height * depth * columns, bytes_accessed=4 * depth * columns + 2 * NC * height * depth + 4 * NC * height * columns, transcendentals=0
        ),
        name=f"contract_{'sent' if across else 'kept'}_{len(before)}",
    )(*(mine[i] for i in used), *(other[i] for i in used), high, low, *before)


def on_device(amplitudes, driver, pair_energy, virt_energy, integrals, src_block, dst_block):
    tile_width = integrals.shape[1]
    local_blocks = virt_energy.shape[0] // tile_width
    blocks, half = NZ * NY * local_blocks, local_blocks // NC
    cut = half * tile_width

    def build():
        return sum_tiles(integrals, src_block, dst_block, local_blocks, blocks, amplitudes.shape[0])

    for iteration in range(ITERS):
        if iteration == 0:
            mine, (total, given, which) = gather_panel(over_z(amplitudes), parts_of, build)
            high, low = split_parts(total, over_core(given), half)
            lower = which == 0
            terms = jnp.stack([driver, virt_energy[None, :] - pair_energy[:, None]])
            kept_terms = jnp.where(lower, terms[..., :cut], terms[..., cut:])
            given_terms = jnp.where(lower, terms[..., cut:], terms[..., :cut])
            both_terms = jnp.stack([kept_terms, over_core(given_terms)], axis=1)
        else:
            mine, _ = gather_panel(over_z(shard), lambda parts: parts)
        *early, last = mine
        other = [over_core(piece) for piece in early]
        begun = contract(early, other, high, low, iteration == 0, 1, [0])
        mine, other = [*early, last], [*other, over_core(last)]
        sent = contract(mine, other, high, low, iteration == 0, 1, [1], [begun])
        kept = contract(mine, other, high, low, iteration == 0, 0)
        if iteration < ITERS - 1:
            shard = ((both_terms[0] + (kept + over_x(sent))) / both_terms[1]).astype(jnp.bfloat16)
    there = over_diagonal(sent[1])
    here, there = lax.optimization_barrier((kept[0] + over_x(sent[0]), over_core(kept[1]) + there))
    ladder = jnp.concatenate([jnp.where(lower, here, there), jnp.where(lower, there, here)], axis=1)
    return ((driver + ladder) / (virt_energy[None, :] - pair_energy[:, None])).astype(jnp.bfloat16)


def solution(mesh):
    form = on_device if (mesh.shape["tile"], mesh.shape["grp"]) == (NZ * NY, NX * NC) else general_form
    return jax.shard_map(
        form,
        mesh=mesh,
        in_specs=(
            P("grp", "tile"),
            P("grp", "tile"),
            P("grp"),
            P("tile"),
            P(("tile", "grp"), None, None),
            P("tile"),
            P("tile"),
        ),
        out_specs=P("grp", "tile"),
        check_vma=False,
    )
```

```python
import functools
import math

import jax
import jax.numpy as jnp
from jax import lax
from jax.experimental import pallas as pl
from jax.experimental.pallas import tpu as pltpu
from jax.sharding import PartitionSpec as P

ITERS = 2
MIB = 1024 * 1024


def contract_blocks(amp_rows, tile_set, source, target, local_blocks):
    row_count = amp_rows.shape[0]
    tile_width = tile_set.shape[1]
    tile_count = tile_set.shape[0]
    group_size = math.gcd(tile_count, 48)
    turns = tile_count // group_size
    blocks = amp_rows.reshape(row_count, -1, tile_width)
    packed_tiles = tile_set.reshape(turns, group_size, tile_width, tile_width)
    packed_source = source.reshape(turns, group_size)
    packed_target = target.reshape(turns, group_size)

    def advance(total_sum, packed):
        picked = jnp.take(blocks, packed[1], axis=1)
        partial_value = jnp.einsum(
            "rgc,gcd->rgd", picked, packed[0], preferred_element_type=jnp.float32
        )
        pieces = []
        for block in range(local_blocks):
            chosen = (packed[2] == block)[None, :, None]
            pieces.append(jnp.sum(jnp.where(chosen, partial_value, 0.0), axis=1))
        return (total_sum + jnp.stack(pieces, axis=1), None)

    initial = jnp.zeros((row_count, local_blocks, tile_width), jnp.float32)
    total_sum, unused = lax.scan(advance, initial, (packed_tiles, packed_source, packed_target))
    return total_sum.reshape(row_count, local_blocks * tile_width)


def general_form(amplitudes, driver, pair_energy, virt_energy, integrals, src_block, dst_block):
    tile_width = integrals.shape[1]
    local_blocks = virt_energy.shape[0] // tile_width
    denominator = virt_energy[None, :] - pair_energy[:, None]
    current = amplitudes
    first_tile = lax.axis_index("grp") * integrals.shape[0]
    my_source = lax.dynamic_slice_in_dim(src_block, first_tile, integrals.shape[0])
    my_target = lax.dynamic_slice_in_dim(dst_block, first_tile, integrals.shape[0])
    for iteration in range(ITERS):
        all_pairs = lax.all_gather(current, "grp", axis=0, tiled=True)
        whole_panel = lax.all_gather(all_pairs, "tile", axis=1, tiled=True)
        partial_value = contract_blocks(whole_panel, integrals, my_source, my_target, local_blocks)
        ladder = lax.psum_scatter(partial_value, "grp", scatter_dimension=0, tiled=True)
        current = ((driver + ladder) / denominator).astype(jnp.bfloat16)
    return current


NZ, NY, NX, NC = 4, 2, 2, 2
PARTS = 2
SCALED = 14
EXTRA = 16


def z_swap(away):
    return [(t, t ^ (away * NY)) for t in range(NZ * NY)]


Y_SWAP = [(t, t ^ 1) for t in range(NZ * NY)]
X_SWAP = [(g, g ^ 2) for g in range(NX * NC)]
CORE_SWAP = [(g, g ^ 1) for g in range(NX * NC)]
DIAGONAL_SWAP = [(g, g ^ 3) for g in range(NX * NC)]


def over_y(value):
    return lax.ppermute(value, "tile", Y_SWAP)


def over_x(value):
    return lax.ppermute(value, "grp", X_SWAP)


def over_core(value):
    return lax.ppermute(value, "grp", CORE_SWAP)


def over_diagonal(value):
    return lax.ppermute(value, "grp", DIAGONAL_SWAP)


def parts_of(rows):
    return jnp.stack(jnp.split(rows, PARTS, axis=1))


def over_z(value):
    far = [lax.ppermute(value, "tile", z_swap(away)) for away in range(NZ // 2, NZ)]
    return [value] + [lax.ppermute(value, "tile", z_swap(away)) for away in range(1, NZ // 2)] + far


def gather_panel(shards, parts, build=None):
    built = [] if build is None else list(build())
    if build is not None:
        shards, built = lax.optimization_barrier((shards, built))
    a = jnp.stack([parts(shard) for shard in shards[: NZ // 2]])
    b = jnp.stack([parts(shard) for shard in shards[NZ // 2 :]])
    a_y, a_x = over_y(a), over_x(a)
    if build is not None:
        b_x, b_y, a_xy = over_x(b), over_y(b), over_x(a_y)
        a_x, a_xy = lax.optimization_barrier((a_x, a_xy))
        return [jnp.stack(pair) for pair in ((a, b), (a_y, b_x), (a_x, b_y), (a_xy, over_y(b_x)))], built
    b, a_y = lax.optimization_barrier((b, a_y))
    b_x, b_y, a_xy = over_x(b), over_y(b), over_x(a_y)
    b_x, a_x = lax.optimization_barrier((b_x, a_x))
    a_xy, b_xy, b_y = lax.optimization_barrier((a_xy, over_y(b_x), b_y))
    return [jnp.stack(group) for group in ((a, b, b_y), (a_y, a_x, b_x), (a_xy, b_xy))], built


PLACES = (
    {(0, 0, 0): (0, 0), (1, 0, 0): (0, 1), (0, 1, 0): (1, 0), (1, 0, 1): (1, 1), (0, 0, 1): (2, 0), (1, 1, 0): (2, 1), (0, 1, 1): (3, 0), (1, 1, 1): (3, 1)},
    {(0, 0, 0): (0, 0), (1, 0, 0): (0, 1), (1, 1, 0): (0, 2), (0, 1, 0): (1, 0), (0, 0, 1): (1, 1), (1, 0, 1): (1, 2), (0, 1, 1): (2, 0), (1, 1, 1): (2, 1)},
)


def sum_kernel(chunk, local_blocks, src_any, dst_any, tiles_any, total, given, which, tiles, src, dst, list_sem, tile_sem):
    steps = tiles.shape[0] // chunk
    half = local_blocks // NC
    shift = half.bit_length() - 1
    slots = given.shape[0]
    lists = [pltpu.make_async_copy(a, b, list_sem.at[i]) for i, (a, b) in enumerate(((src_any, src), (dst_any, dst)))]
    for copy in lists:
        copy.start()

    def tile_copy(step):
        part = pl.ds(step * chunk, chunk)
        return pltpu.make_async_copy(tiles_any.at[part], tiles.at[part], tile_sem.at[step])

    for step in range(steps):
        tile_copy(step).start()

    def clear(slot, carry):
        total[slot] = jnp.zeros(total.shape[1:], jnp.float32)
        return carry

    lax.fori_loop(0, total.shape[0], clear, 0, unroll=4)
    for copy in lists:
        copy.wait()
    grp = lax.axis_index("grp")
    here = lax.axis_index("tile") * local_blocks
    core = lax.rem(grp, NC)
    which[...] = jnp.full(which.shape, core, jnp.int32)
    kept = core * half
    first = grp * tiles.shape[0]

    def run(step, carry):
        tile_copy(step).wait()

        def add(j, carry):
            k = step * chunk + j
            target = dst[first + k] ^ kept
            slot = (target >> shift) * slots + ((src[first + k] ^ here) << shift) + (target & (half - 1))
            total[slot] += tiles[k].astype(jnp.float32)
            return carry

        lax.fori_loop(0, chunk, add, 0, unroll=8)
        return carry

    lax.fori_loop(0, steps, run, 0)

    def give(slot, carry):
        given[slot] = total[slots + slot]
        return carry

    lax.fori_loop(0, slots, give, 0, unroll=4)


def sum_tiles(integrals, src_block, dst_block, local_blocks, blocks, rows):
    count, width, _ = integrals.shape
    slots = blocks * local_blocks // NC
    chunk = math.gcd(count, 24)
    outside = pl.BlockSpec(memory_space=pl.ANY)
    local = pl.BlockSpec(memory_space=pltpu.VMEM)
    return pl.pallas_call(
        functools.partial(sum_kernel, chunk, local_blocks),
        in_specs=[outside] * 3,
        out_specs=[local] * 3,
        out_shape=[
            pltpu.VMEM((NC * slots, width, width), jnp.float32),
            pltpu.VMEM((slots, width, width), jnp.float32),
            pltpu.VMEM((rows, local_blocks // NC * width), jnp.int32),
        ],
        scratch_shapes=[
            pltpu.VMEM(integrals.shape, jnp.bfloat16),
            pltpu.SMEM(src_block.shape, jnp.int32),
            pltpu.SMEM(dst_block.shape, jnp.int32),
            pltpu.SemaphoreType.DMA((2,)),
            pltpu.SemaphoreType.DMA((count // chunk,)),
        ],
        compiler_params=pltpu.CompilerParams(vmem_limit_bytes=24 * MIB),
        cost_estimate=pl.CostEstimate(
            flops=count * width * width, bytes_accessed=2 * count * width * width + 4 * slots * width * width, transcendentals=0
        ),
        name="sum_tiles",
    )(*(pltpu.with_memory_space_constraint(a, pltpu.HBM) for a in (src_block, dst_block, integrals)))


def split_kernel(half, mine, got, high, low):
    width = mine.shape[-1]

    def split(block, carry):
        for d in range(half):
            value = mine[block * half + d] + got[block * half + d]
            top = value.astype(jnp.bfloat16)
            rest = value - top.astype(jnp.float32)
            high[block, :, d * width : (d + 1) * width] = top
            low[block, :, d * width : (d + 1) * width] = rest.astype(jnp.bfloat16)
        return carry

    lax.fori_loop(0, got.shape[0] // half, split, 0)


def split_parts(mine, got, half):
    slots, width, _ = got.shape
    shape = pltpu.VMEM((slots // half, width, half * width), jnp.bfloat16)
    local = pl.BlockSpec(memory_space=pltpu.VMEM)
    high, low = pl.pallas_call(
        functools.partial(split_kernel, half),
        in_specs=[local, local],
        out_specs=[local, local],
        out_shape=[shape, shape],
        compiler_params=pltpu.CompilerParams(vmem_limit_bytes=24 * MIB),
        cost_estimate=pl.CostEstimate(flops=3 * got.size, bytes_accessed=12 * got.size, transcendentals=0),
        name="split_parts",
    )(*(pltpu.with_memory_space_constraint(a, pltpu.VMEM) for a in (mine, got)))
    return high.reshape(-1, half * width), low.reshape(-1, half * width)


def contract_kernel(by_core, across, along, used, *refs):
    mine, other = (dict(zip(used, part)) for part in (refs[: len(used)], refs[len(used) : 2 * len(used)]))
    high, low, *before, out, rows = refs[2 * len(used) :]
    height, depth = next(iter(mine.values())).shape[-2:]
    wide = PARTS * depth
    core = lax.rem(lax.axis_index("grp"), NC)
    spans = [(z, y) for z in range(NZ) for y in along]
    for away, pieces in enumerate((mine, other)):
        for part in range(PARTS):
            row = (away if by_core else part ^ away) * height
            half = part if by_core else (core if away == 0 else 1 - core)
            for span, (z, y) in enumerate(spans):
                piece, index = PLACES[not by_core][z // (NZ // 2), y, across]
                column = span * wide + half * depth
                if not by_core:
                    column = pl.multiple_of(column, depth)
                rows[row : row + height, pl.ds(column, depth)] = pieces[piece][index, z % (NZ // 2), part]
    total = sum(ref[...].reshape(NC * height, -1) for ref in before)
    if len(along) == NY:
        chunks = [(rows[...], slice(None))]
    else:
        chunks = [(rows[:, i * wide : (i + 1) * wide], pl.ds((z * NY + y) * wide, wide)) for i, (z, y) in enumerate(spans)]
    for left, right in chunks:
        for matrix in (high, low):
            total += jnp.dot(left, matrix[right, :], preferred_element_type=jnp.float32)
    if out.shape[1] > height:
        most = jnp.clip(jnp.max(jnp.abs(total), keepdims=True), 1e-30, 1e30)
        exponent = jnp.ceil(jnp.log2(most))
        total *= jnp.exp2(SCALED - exponent)
        for core in range(NC):
            out[core, height:] = jnp.broadcast_to(exponent, (out.shape[1] - height, total.shape[1]))
    for core in range(NC):
        out[core, :height] = total[core * height : (core + 1) * height]


def send_sums(sums, across):
    got = across(sums.astype(jnp.float16)).astype(jnp.float32)
    rows = got.shape[-2] - EXTRA
    return got[..., :rows, :] * jnp.exp2(got[..., rows : rows + 1, :] - SCALED)


def contract(mine, other, high, low, by_core, across, along=range(NY), before=(), scaled=False):
    used = sorted({PLACES[not by_core][half, y, across][0] for half in range(2) for y in along})
    height = mine[0].shape[-2]
    depth, columns = high.shape
    depth = depth // NY * len(along)
    local = pl.BlockSpec(memory_space=pltpu.VMEM)
    return pl.pallas_call(
        functools.partial(contract_kernel, by_core, across, tuple(along), used),
        in_specs=[local] * (2 * len(used) + 2 + len(before)),
        out_specs=local,
        out_shape=jax.ShapeDtypeStruct((NC, height + EXTRA * scaled, columns), jnp.float32),
        scratch_shapes=[pltpu.VMEM((NC * height, depth), jnp.bfloat16)],
        compiler_params=pltpu.CompilerParams(vmem_limit_bytes=24 * MIB),
        cost_estimate=pl.CostEstimate(
            flops=4 * NC * height * depth * columns, bytes_accessed=4 * depth * columns + 2 * NC * height * depth + 4 * NC * height * columns, transcendentals=0
        ),
        name=f"contract_{'sent' if across else 'kept'}_{len(before)}",
    )(*(mine[i] for i in used), *(other[i] for i in used), high, low, *before)


def on_device(amplitudes, driver, pair_energy, virt_energy, integrals, src_block, dst_block):
    tile_width = integrals.shape[1]
    local_blocks = virt_energy.shape[0] // tile_width
    blocks, half = NZ * NY * local_blocks, local_blocks // NC
    cut = half * tile_width

    def build():
        return sum_tiles(integrals, src_block, dst_block, local_blocks, blocks, amplitudes.shape[0])

    for iteration in range(ITERS):
        if iteration == 0:
            mine, (total, given, which) = gather_panel(over_z(amplitudes), parts_of, build)
            high, low = split_parts(total, over_core(given), half)
            lower = which == 0
            terms = jnp.stack([driver, virt_energy[None, :] - pair_energy[:, None]])
            kept_terms = jnp.where(lower, terms[..., :cut], terms[..., cut:])
            given_terms = jnp.where(lower, terms[..., cut:], terms[..., :cut])
            both_terms = jnp.stack([kept_terms, over_core(given_terms)], axis=1)
        else:
            mine, _ = gather_panel(over_z(shard), lambda parts: parts)
        *early, last = mine
        other = [over_core(piece) for piece in early]
        begun = contract(early, other, high, low, iteration == 0, 1, [0])
        mine, other = [*early, last], [*other, over_core(last)]
        sent = contract(mine, other, high, low, iteration == 0, 1, [1], [begun], True)
        kept = contract(mine, other, high, low, iteration == 0, 0)
        if iteration < ITERS - 1:
            shard = ((both_terms[0] + (kept + send_sums(sent, over_x))) / both_terms[1]).astype(jnp.bfloat16)
    there = send_sums(sent[1], over_diagonal)
    here, there = lax.optimization_barrier((kept[0] + send_sums(sent[0], over_x), over_core(kept[1]) + there))
    ladder = jnp.concatenate([jnp.where(lower, here, there), jnp.where(lower, there, here)], axis=1)
    return ((driver + ladder) / (virt_energy[None, :] - pair_energy[:, None])).astype(jnp.bfloat16)


def solution(mesh):
    form = on_device if (mesh.shape["tile"], mesh.shape["grp"]) == (NZ * NY, NX * NC) else general_form
    return jax.shard_map(
        form,
        mesh=mesh,
        in_specs=(
            P("grp", "tile"),
            P("grp", "tile"),
            P("grp"),
            P("tile"),
            P(("tile", "grp"), None, None),
            P("tile"),
            P("tile"),
        ),
        out_specs=P("grp", "tile"),
        check_vma=False,
    )
```

```python
import functools
import math

import jax
import jax.numpy as jnp
from jax import lax
from jax.experimental import pallas as pl
from jax.experimental.pallas import tpu as pltpu
from jax.sharding import PartitionSpec as P

ITERS = 2
MIB = 1024 * 1024


def contract_blocks(amp_rows, tile_set, source, target, local_blocks):
    row_count = amp_rows.shape[0]
    tile_width = tile_set.shape[1]
    tile_count = tile_set.shape[0]
    group_size = math.gcd(tile_count, 48)
    turns = tile_count // group_size
    blocks = amp_rows.reshape(row_count, -1, tile_width)
    packed_tiles = tile_set.reshape(turns, group_size, tile_width, tile_width)
    packed_source = source.reshape(turns, group_size)
    packed_target = target.reshape(turns, group_size)

    def advance(total_sum, packed):
        picked = jnp.take(blocks, packed[1], axis=1)
        partial_value = jnp.einsum(
            "rgc,gcd->rgd", picked, packed[0], preferred_element_type=jnp.float32
        )
        pieces = []
        for block in range(local_blocks):
            chosen = (packed[2] == block)[None, :, None]
            pieces.append(jnp.sum(jnp.where(chosen, partial_value, 0.0), axis=1))
        return (total_sum + jnp.stack(pieces, axis=1), None)

    initial = jnp.zeros((row_count, local_blocks, tile_width), jnp.float32)
    total_sum, unused = lax.scan(advance, initial, (packed_tiles, packed_source, packed_target))
    return total_sum.reshape(row_count, local_blocks * tile_width)


def general_form(amplitudes, driver, pair_energy, virt_energy, integrals, src_block, dst_block):
    tile_width = integrals.shape[1]
    local_blocks = virt_energy.shape[0] // tile_width
    denominator = virt_energy[None, :] - pair_energy[:, None]
    current = amplitudes
    first_tile = lax.axis_index("grp") * integrals.shape[0]
    my_source = lax.dynamic_slice_in_dim(src_block, first_tile, integrals.shape[0])
    my_target = lax.dynamic_slice_in_dim(dst_block, first_tile, integrals.shape[0])
    for iteration in range(ITERS):
        all_pairs = lax.all_gather(current, "grp", axis=0, tiled=True)
        whole_panel = lax.all_gather(all_pairs, "tile", axis=1, tiled=True)
        partial_value = contract_blocks(whole_panel, integrals, my_source, my_target, local_blocks)
        ladder = lax.psum_scatter(partial_value, "grp", scatter_dimension=0, tiled=True)
        current = ((driver + ladder) / denominator).astype(jnp.bfloat16)
    return current


NZ, NY, NX, NC = 4, 2, 2, 2
PARTS = 2
SCALED = 14
EXTRA = 16


def z_swap(away):
    return [(t, t ^ (away * NY)) for t in range(NZ * NY)]


Y_SWAP = [(t, t ^ 1) for t in range(NZ * NY)]
X_SWAP = [(g, g ^ 2) for g in range(NX * NC)]
CORE_SWAP = [(g, g ^ 1) for g in range(NX * NC)]
DIAGONAL_SWAP = [(g, g ^ 3) for g in range(NX * NC)]


def over_y(value):
    return lax.ppermute(value, "tile", Y_SWAP)


def over_x(value):
    return lax.ppermute(value, "grp", X_SWAP)


def over_core(value):
    return lax.ppermute(value, "grp", CORE_SWAP)


def over_diagonal(value):
    return lax.ppermute(value, "grp", DIAGONAL_SWAP)


def parts_of(rows):
    return jnp.stack(jnp.split(rows, PARTS, axis=1))


def over_z(value):
    far = [lax.ppermute(value, "tile", z_swap(away)) for away in range(NZ // 2, NZ)]
    return [value] + [lax.ppermute(value, "tile", z_swap(away)) for away in range(1, NZ // 2)] + far


def gather_panel(shards, parts, build=None):
    built = [] if build is None else list(build())
    if build is not None:
        shards, built = lax.optimization_barrier((shards, built))
    a = jnp.stack([parts(shard) for shard in shards[: NZ // 2]])
    b = jnp.stack([parts(shard) for shard in shards[NZ // 2 :]])
    a_y, a_x = over_y(a), over_x(a)
    if build is not None:
        b_x, b_y, a_xy = over_x(b), over_y(b), over_x(a_y)
        b_xy = over_y(b_x)
        a_x, a_xy = lax.optimization_barrier((a_x, a_xy))
        b_y, b_xy = lax.optimization_barrier((b_y, b_xy))
        return [jnp.stack(pair) for pair in ((a, b), (a_y, b_x), (a_x, b_y), (a_xy, b_xy))], built
    b, a_y = lax.optimization_barrier((b, a_y))
    b_x, b_y, a_xy = over_x(b), over_y(b), over_x(a_y)
    b_x, a_x = lax.optimization_barrier((b_x, a_x))
    a_xy, b_xy, b_y = lax.optimization_barrier((a_xy, over_y(b_x), b_y))
    return [jnp.stack(group) for group in ((a, b, b_y), (a_y, a_x, b_x), (a_xy, b_xy))], built


PLACES = (
    {(0, 0, 0): (0, 0), (1, 0, 0): (0, 1), (0, 1, 0): (1, 0), (1, 0, 1): (1, 1), (0, 0, 1): (2, 0), (1, 1, 0): (2, 1), (0, 1, 1): (3, 0), (1, 1, 1): (3, 1)},
    {(0, 0, 0): (0, 0), (1, 0, 0): (0, 1), (1, 1, 0): (0, 2), (0, 1, 0): (1, 0), (0, 0, 1): (1, 1), (1, 0, 1): (1, 2), (0, 1, 1): (2, 0), (1, 1, 1): (2, 1)},
)


def sum_kernel(chunk, local_blocks, src_any, dst_any, tiles_any, total, given, which, tiles, src, dst, list_sem, tile_sem):
    steps = tiles.shape[0] // chunk
    half = local_blocks // NC
    shift = half.bit_length() - 1
    slots = given.shape[0]
    lists = [pltpu.make_async_copy(a, b, list_sem.at[i]) for i, (a, b) in enumerate(((src_any, src), (dst_any, dst)))]
    for copy in lists:
        copy.start()

    def tile_copy(step):
        part = pl.ds(step * chunk, chunk)
        return pltpu.make_async_copy(tiles_any.at[part], tiles.at[part], tile_sem.at[step])

    for step in range(steps):
        tile_copy(step).start()

    def clear(slot, carry):
        total[slot] = jnp.zeros(total.shape[1:], jnp.float32)
        return carry

    lax.fori_loop(0, total.shape[0], clear, 0, unroll=4)
    for copy in lists:
        copy.wait()
    grp = lax.axis_index("grp")
    here = lax.axis_index("tile") * local_blocks
    core = lax.rem(grp, NC)
    which[...] = jnp.full(which.shape, core, jnp.int32)
    kept = core * half
    first = grp * tiles.shape[0]

    def run(step, carry):
        tile_copy(step).wait()

        def add(j, carry):
            k = step * chunk + j
            target = dst[first + k] ^ kept
            slot = (target >> shift) * slots + ((src[first + k] ^ here) << shift) + (target & (half - 1))
            total[slot] += tiles[k].astype(jnp.float32)
            return carry

        lax.fori_loop(0, chunk, add, 0, unroll=8)
        return carry

    lax.fori_loop(0, steps, run, 0)

    def give(slot, carry):
        given[slot] = total[slots + slot]
        return carry

    lax.fori_loop(0, slots, give, 0, unroll=4)


def sum_tiles(integrals, src_block, dst_block, local_blocks, blocks, rows):
    count, width, _ = integrals.shape
    slots = blocks * local_blocks // NC
    chunk = math.gcd(count, 24)
    outside = pl.BlockSpec(memory_space=pl.ANY)
    local = pl.BlockSpec(memory_space=pltpu.VMEM)
    return pl.pallas_call(
        functools.partial(sum_kernel, chunk, local_blocks),
        in_specs=[outside] * 3,
        out_specs=[local] * 3,
        out_shape=[
            pltpu.VMEM((NC * slots, width, width), jnp.float32),
            pltpu.VMEM((slots, width, width), jnp.float32),
            pltpu.VMEM((rows, local_blocks // NC * width), jnp.int32),
        ],
        scratch_shapes=[
            pltpu.VMEM(integrals.shape, jnp.bfloat16),
            pltpu.SMEM(src_block.shape, jnp.int32),
            pltpu.SMEM(dst_block.shape, jnp.int32),
            pltpu.SemaphoreType.DMA((2,)),
            pltpu.SemaphoreType.DMA((count // chunk,)),
        ],
        compiler_params=pltpu.CompilerParams(vmem_limit_bytes=24 * MIB),
        cost_estimate=pl.CostEstimate(
            flops=count * width * width, bytes_accessed=2 * count * width * width + 4 * slots * width * width, transcendentals=0
        ),
        name="sum_tiles",
    )(*(pltpu.with_memory_space_constraint(a, pltpu.HBM) for a in (src_block, dst_block, integrals)))


def split_kernel(half, mine, got, high, low):
    width = mine.shape[-1]

    def split(block, carry):
        for d in range(half):
            value = mine[block * half + d] + got[block * half + d]
            top = value.astype(jnp.bfloat16)
            rest = value - top.astype(jnp.float32)
            high[block, :, d * width : (d + 1) * width] = top
            low[block, :, d * width : (d + 1) * width] = rest.astype(jnp.bfloat16)
        return carry

    lax.fori_loop(0, got.shape[0] // half, split, 0)


def split_parts(mine, got, half):
    slots, width, _ = got.shape
    shape = pltpu.VMEM((slots // half, width, half * width), jnp.bfloat16)
    local = pl.BlockSpec(memory_space=pltpu.VMEM)
    high, low = pl.pallas_call(
        functools.partial(split_kernel, half),
        in_specs=[local, local],
        out_specs=[local, local],
        out_shape=[shape, shape],
        compiler_params=pltpu.CompilerParams(vmem_limit_bytes=24 * MIB),
        cost_estimate=pl.CostEstimate(flops=3 * got.size, bytes_accessed=12 * got.size, transcendentals=0),
        name="split_parts",
    )(*(pltpu.with_memory_space_constraint(a, pltpu.VMEM) for a in (mine, got)))
    return high.reshape(-1, half * width), low.reshape(-1, half * width)


def contract_kernel(by_core, across, along, used, *refs):
    mine, other = (dict(zip(used, part)) for part in (refs[: len(used)], refs[len(used) : 2 * len(used)]))
    high, low, *before, out, rows = refs[2 * len(used) :]
    height, depth = next(iter(mine.values())).shape[-2:]
    wide = PARTS * depth
    core = lax.rem(lax.axis_index("grp"), NC)
    spans = [(z, y) for z in range(NZ) for y in along]
    for away, pieces in enumerate((mine, other)):
        for part in range(PARTS):
            row = (away if by_core else part ^ away) * height
            half = part if by_core else (core if away == 0 else 1 - core)
            for span, (z, y) in enumerate(spans):
                piece, index = PLACES[not by_core][z // (NZ // 2), y, across]
                column = span * wide + half * depth
                if not by_core:
                    column = pl.multiple_of(column, depth)
                rows[row : row + height, pl.ds(column, depth)] = pieces[piece][index, z % (NZ // 2), part]
    total = sum(ref[...].reshape(NC * height, -1) for ref in before)
    if len(along) == NY:
        chunks = [(rows[...], slice(None))]
    else:
        chunks = [(rows[:, i * wide : (i + 1) * wide], pl.ds((z * NY + y) * wide, wide)) for i, (z, y) in enumerate(spans)]
    for left, right in chunks:
        for matrix in (high, low):
            total += jnp.dot(left, matrix[right, :], preferred_element_type=jnp.float32)
    if out.shape[1] > height:
        most = jnp.clip(jnp.max(jnp.abs(total), keepdims=True), 1e-30, 1e30)
        exponent = jnp.ceil(jnp.log2(most))
        total *= jnp.exp2(SCALED - exponent)
        for core in range(NC):
            out[core, height:] = jnp.broadcast_to(exponent, (out.shape[1] - height, total.shape[1]))
    for core in range(NC):
        out[core, :height] = total[core * height : (core + 1) * height]


def sums_of(got):
    got = got.astype(jnp.float32)
    rows = got.shape[-2] - EXTRA
    return got[..., :rows, :] * jnp.exp2(got[..., rows : rows + 1, :] - SCALED)


def contract(mine, other, high, low, by_core, across, along=range(NY), before=(), scaled=False):
    used = sorted({PLACES[not by_core][half, y, across][0] for half in range(2) for y in along})
    height = mine[0].shape[-2]
    depth, columns = high.shape
    depth = depth // NY * len(along)
    local = pl.BlockSpec(memory_space=pltpu.VMEM)
    return pl.pallas_call(
        functools.partial(contract_kernel, by_core, across, tuple(along), used),
        in_specs=[local] * (2 * len(used) + 2 + len(before)),
        out_specs=local,
        out_shape=jax.ShapeDtypeStruct((NC, height + EXTRA * scaled, columns), jnp.float32),
        scratch_shapes=[pltpu.VMEM((NC * height, depth), jnp.bfloat16)],
        compiler_params=pltpu.CompilerParams(vmem_limit_bytes=24 * MIB),
        cost_estimate=pl.CostEstimate(
            flops=4 * NC * height * depth * columns, bytes_accessed=4 * depth * columns + 2 * NC * height * depth + 4 * NC * height * columns, transcendentals=0
        ),
        name=f"contract_{'sent' if across else 'kept'}_{len(before)}",
    )(*(mine[i] for i in used), *(other[i] for i in used), high, low, *before)


def on_device(amplitudes, driver, pair_energy, virt_energy, integrals, src_block, dst_block):
    tile_width = integrals.shape[1]
    local_blocks = virt_energy.shape[0] // tile_width
    blocks, half = NZ * NY * local_blocks, local_blocks // NC
    cut = half * tile_width

    def build():
        return sum_tiles(integrals, src_block, dst_block, local_blocks, blocks, amplitudes.shape[0])

    for iteration in range(ITERS):
        if iteration == 0:
            mine, (total, given, which) = gather_panel(over_z(amplitudes), parts_of, build)
            high, low = split_parts(total, over_core(given), half)
            lower = which == 0
            terms = jnp.stack([driver, virt_energy[None, :] - pair_energy[:, None]])
            kept_terms = jnp.where(lower, terms[..., :cut], terms[..., cut:])
            given_terms = jnp.where(lower, terms[..., cut:], terms[..., :cut])
            both_terms = jnp.stack([kept_terms, over_core(given_terms)], axis=1)
        else:
            mine, _ = gather_panel(over_z(shard), lambda parts: parts)
        *early, last = mine
        other = [over_core(piece) for piece in early]
        begun = contract(early, other, high, low, iteration == 0, 1, [0])
        mine, other = [*early, last], [*other, over_core(last)]
        sent = contract(mine, other, high, low, iteration == 0, 1, [1], [begun], True)
        kept = contract(mine, other, high, low, iteration == 0, 0)
        if iteration < ITERS - 1:
            shard = ((both_terms[0] + (kept + sums_of(over_x(sent.astype(jnp.float16))))) / both_terms[1]).astype(jnp.bfloat16)
    sent = sent.astype(jnp.float16)
    got_there, got_here = over_diagonal(sent[1]), over_x(sent[0])
    got_there, kept = lax.optimization_barrier((got_there, kept))
    got_here, kept_there = lax.optimization_barrier((got_here, over_core(kept[1])))
    here, there = kept[0] + sums_of(got_here), kept_there + sums_of(got_there)
    ladder = jnp.concatenate([jnp.where(lower, here, there), jnp.where(lower, there, here)], axis=1)
    return ((driver + ladder) / (virt_energy[None, :] - pair_energy[:, None])).astype(jnp.bfloat16)


def solution(mesh):
    form = on_device if (mesh.shape["tile"], mesh.shape["grp"]) == (NZ * NY, NX * NC) else general_form
    return jax.shard_map(
        form,
        mesh=mesh,
        in_specs=(
            P("grp", "tile"),
            P("grp", "tile"),
            P("grp"),
            P("tile"),
            P(("tile", "grp"), None, None),
            P("tile"),
            P("tile"),
        ),
        out_specs=P("grp", "tile"),
        check_vma=False,
    )
```

```python
import functools
import math

import jax
import jax.numpy as jnp
from jax import lax
from jax.experimental import pallas as pl
from jax.experimental.pallas import tpu as pltpu
from jax.sharding import PartitionSpec as P

ITERS = 2
MIB = 1024 * 1024


def contract_blocks(amp_rows, tile_set, source, target, local_blocks):
    row_count = amp_rows.shape[0]
    tile_width = tile_set.shape[1]
    tile_count = tile_set.shape[0]
    group_size = math.gcd(tile_count, 48)
    turns = tile_count // group_size
    blocks = amp_rows.reshape(row_count, -1, tile_width)
    packed_tiles = tile_set.reshape(turns, group_size, tile_width, tile_width)
    packed_source = source.reshape(turns, group_size)
    packed_target = target.reshape(turns, group_size)

    def advance(total_sum, packed):
        picked = jnp.take(blocks, packed[1], axis=1)
        partial_value = jnp.einsum(
            "rgc,gcd->rgd", picked, packed[0], preferred_element_type=jnp.float32
        )
        pieces = []
        for block in range(local_blocks):
            chosen = (packed[2] == block)[None, :, None]
            pieces.append(jnp.sum(jnp.where(chosen, partial_value, 0.0), axis=1))
        return (total_sum + jnp.stack(pieces, axis=1), None)

    initial = jnp.zeros((row_count, local_blocks, tile_width), jnp.float32)
    total_sum, unused = lax.scan(advance, initial, (packed_tiles, packed_source, packed_target))
    return total_sum.reshape(row_count, local_blocks * tile_width)


def general_form(amplitudes, driver, pair_energy, virt_energy, integrals, src_block, dst_block):
    tile_width = integrals.shape[1]
    local_blocks = virt_energy.shape[0] // tile_width
    denominator = virt_energy[None, :] - pair_energy[:, None]
    current = amplitudes
    first_tile = lax.axis_index("grp") * integrals.shape[0]
    my_source = lax.dynamic_slice_in_dim(src_block, first_tile, integrals.shape[0])
    my_target = lax.dynamic_slice_in_dim(dst_block, first_tile, integrals.shape[0])
    for iteration in range(ITERS):
        all_pairs = lax.all_gather(current, "grp", axis=0, tiled=True)
        whole_panel = lax.all_gather(all_pairs, "tile", axis=1, tiled=True)
        partial_value = contract_blocks(whole_panel, integrals, my_source, my_target, local_blocks)
        ladder = lax.psum_scatter(partial_value, "grp", scatter_dimension=0, tiled=True)
        current = ((driver + ladder) / denominator).astype(jnp.bfloat16)
    return current


NZ, NY, NX, NC = 4, 2, 2, 2
PARTS = 2
SCALED = 14
EXTRA = 16


def z_swap(away):
    return [(t, t ^ (away * NY)) for t in range(NZ * NY)]


Y_SWAP = [(t, t ^ 1) for t in range(NZ * NY)]
X_SWAP = [(g, g ^ 2) for g in range(NX * NC)]
CORE_SWAP = [(g, g ^ 1) for g in range(NX * NC)]
DIAGONAL_SWAP = [(g, g ^ 3) for g in range(NX * NC)]


def over_y(value):
    return lax.ppermute(value, "tile", Y_SWAP)


def over_x(value):
    return lax.ppermute(value, "grp", X_SWAP)


def over_core(value):
    return lax.ppermute(value, "grp", CORE_SWAP)


def over_diagonal(value):
    return lax.ppermute(value, "grp", DIAGONAL_SWAP)


def parts_of(rows):
    return jnp.stack(jnp.split(rows, PARTS, axis=1))


def over_z(value):
    far = [lax.ppermute(value, "tile", z_swap(away)) for away in range(NZ // 2, NZ)]
    return [value] + [lax.ppermute(value, "tile", z_swap(away)) for away in range(1, NZ // 2)] + far


def gather_panel(shards, parts, build=None):
    built = [] if build is None else list(build())
    if build is not None:
        shards, built = lax.optimization_barrier((shards, built))
    a = jnp.stack([parts(shard) for shard in shards[: NZ // 2]])
    b = jnp.stack([parts(shard) for shard in shards[NZ // 2 :]])
    a_y, a_x = over_y(a), over_x(a)
    if build is not None:
        b_x, b_y, a_xy = over_x(b), over_y(b), over_x(a_y)
        b_xy = over_y(b_x)
        a_x, a_xy = lax.optimization_barrier((a_x, a_xy))
        b_y, b_xy = lax.optimization_barrier((b_y, b_xy))
        return [jnp.stack(pair) for pair in ((a, b), (a_y, b_x), (a_x, b_y), (a_xy, b_xy))], built
    late_b, a_y, a_x = lax.optimization_barrier((b, a_y, a_x))
    b_x, b_y, a_xy = over_x(b), over_y(late_b), over_x(a_y)
    b_xy = over_y(b_x)
    a_xy, b_xy, b_y = lax.optimization_barrier((a_xy, b_xy, b_y))
    return [jnp.stack(group) for group in ((a, b, b_y), (a_y, a_x, b_x), (a_xy, b_xy))], built


PLACES = (
    {(0, 0, 0): (0, 0), (1, 0, 0): (0, 1), (0, 1, 0): (1, 0), (1, 0, 1): (1, 1), (0, 0, 1): (2, 0), (1, 1, 0): (2, 1), (0, 1, 1): (3, 0), (1, 1, 1): (3, 1)},
    {(0, 0, 0): (0, 0), (1, 0, 0): (0, 1), (1, 1, 0): (0, 2), (0, 1, 0): (1, 0), (0, 0, 1): (1, 1), (1, 0, 1): (1, 2), (0, 1, 1): (2, 0), (1, 1, 1): (2, 1)},
)


def sum_kernel(chunk, local_blocks, src_any, dst_any, tiles_any, total, given, which, tiles, src, dst, list_sem, tile_sem):
    steps = tiles.shape[0] // chunk
    half = local_blocks // NC
    shift = half.bit_length() - 1
    slots = given.shape[0]
    lists = [pltpu.make_async_copy(a, b, list_sem.at[i]) for i, (a, b) in enumerate(((src_any, src), (dst_any, dst)))]
    for copy in lists:
        copy.start()

    def tile_copy(step):
        part = pl.ds(step * chunk, chunk)
        return pltpu.make_async_copy(tiles_any.at[part], tiles.at[part], tile_sem.at[step])

    for step in range(steps):
        tile_copy(step).start()

    def clear(slot, carry):
        total[slot] = jnp.zeros(total.shape[1:], jnp.float32)
        return carry

    lax.fori_loop(0, total.shape[0], clear, 0, unroll=4)
    for copy in lists:
        copy.wait()
    grp = lax.axis_index("grp")
    here = lax.axis_index("tile") * local_blocks
    core = lax.rem(grp, NC)
    which[...] = jnp.full(which.shape, core, jnp.int32)
    kept = core * half
    first = grp * tiles.shape[0]

    def run(step, carry):
        tile_copy(step).wait()

        def add(j, carry):
            k = step * chunk + j
            target = dst[first + k] ^ kept
            slot = (target >> shift) * slots + ((src[first + k] ^ here) << shift) + (target & (half - 1))
            total[slot] += tiles[k].astype(jnp.float32)
            return carry

        lax.fori_loop(0, chunk, add, 0, unroll=8)
        return carry

    lax.fori_loop(0, steps, run, 0)

    def give(slot, carry):
        given[slot] = total[slots + slot]
        return carry

    lax.fori_loop(0, slots, give, 0, unroll=4)


def sum_tiles(integrals, src_block, dst_block, local_blocks, blocks, rows):
    count, width, _ = integrals.shape
    slots = blocks * local_blocks // NC
    chunk = math.gcd(count, 24)
    outside = pl.BlockSpec(memory_space=pl.ANY)
    local = pl.BlockSpec(memory_space=pltpu.VMEM)
    return pl.pallas_call(
        functools.partial(sum_kernel, chunk, local_blocks),
        in_specs=[outside] * 3,
        out_specs=[local] * 3,
        out_shape=[
            pltpu.VMEM((NC * slots, width, width), jnp.float32),
            pltpu.VMEM((slots, width, width), jnp.float32),
            pltpu.VMEM((rows, local_blocks // NC * width), jnp.int32),
        ],
        scratch_shapes=[
            pltpu.VMEM(integrals.shape, jnp.bfloat16),
            pltpu.SMEM(src_block.shape, jnp.int32),
            pltpu.SMEM(dst_block.shape, jnp.int32),
            pltpu.SemaphoreType.DMA((2,)),
            pltpu.SemaphoreType.DMA((count // chunk,)),
        ],
        compiler_params=pltpu.CompilerParams(vmem_limit_bytes=24 * MIB),
        cost_estimate=pl.CostEstimate(
            flops=count * width * width, bytes_accessed=2 * count * width * width + 4 * slots * width * width, transcendentals=0
        ),
        name="sum_tiles",
    )(*(pltpu.with_memory_space_constraint(a, pltpu.HBM) for a in (src_block, dst_block, integrals)))


def split_kernel(half, mine, got, high, low):
    width = mine.shape[-1]

    def split(block, carry):
        for d in range(half):
            value = mine[block * half + d] + got[block * half + d]
            top = value.astype(jnp.bfloat16)
            rest = value - top.astype(jnp.float32)
            high[block, :, d * width : (d + 1) * width] = top
            low[block, :, d * width : (d + 1) * width] = rest.astype(jnp.bfloat16)
        return carry

    lax.fori_loop(0, got.shape[0] // half, split, 0)


def split_parts(mine, got, half):
    slots, width, _ = got.shape
    shape = pltpu.VMEM((slots // half, width, half * width), jnp.bfloat16)
    local = pl.BlockSpec(memory_space=pltpu.VMEM)
    high, low = pl.pallas_call(
        functools.partial(split_kernel, half),
        in_specs=[local, local],
        out_specs=[local, local],
        out_shape=[shape, shape],
        compiler_params=pltpu.CompilerParams(vmem_limit_bytes=24 * MIB),
        cost_estimate=pl.CostEstimate(flops=3 * got.size, bytes_accessed=12 * got.size, transcendentals=0),
        name="split_parts",
    )(*(pltpu.with_memory_space_constraint(a, pltpu.VMEM) for a in (mine, got)))
    return high.reshape(-1, half * width), low.reshape(-1, half * width)


def contract_kernel(by_core, across, along, used, *refs):
    mine, other = (dict(zip(used, part)) for part in (refs[: len(used)], refs[len(used) : 2 * len(used)]))
    high, low, *before, out, rows = refs[2 * len(used) :]
    height, depth = next(iter(mine.values())).shape[-2:]
    wide = PARTS * depth
    core = lax.rem(lax.axis_index("grp"), NC)
    spans = [(z, y) for z in range(NZ) for y in along]
    for away, pieces in enumerate((mine, other)):
        for part in range(PARTS):
            row = (away if by_core else part ^ away) * height
            half = part if by_core else (core if away == 0 else 1 - core)
            for span, (z, y) in enumerate(spans):
                piece, index = PLACES[not by_core][z // (NZ // 2), y, across]
                column = span * wide + half * depth
                if not by_core:
                    column = pl.multiple_of(column, depth)
                rows[row : row + height, pl.ds(column, depth)] = pieces[piece][index, z % (NZ // 2), part]
    total = sum(ref[...].reshape(NC * height, -1) for ref in before)
    if len(along) == NY:
        chunks = [(rows[...], slice(None))]
    else:
        chunks = [(rows[:, i * wide : (i + 1) * wide], pl.ds((z * NY + y) * wide, wide)) for i, (z, y) in enumerate(spans)]
    for left, right in chunks:
        for matrix in (high, low):
            total += jnp.dot(left, matrix[right, :], preferred_element_type=jnp.float32)
    if out.shape[1] > height:
        most = jnp.clip(jnp.max(jnp.abs(total), keepdims=True), 1e-30, 1e30)
        exponent = jnp.ceil(jnp.log2(most))
        total *= jnp.exp2(SCALED - exponent)
        for core in range(NC):
            out[core, height:] = jnp.broadcast_to(exponent, (out.shape[1] - height, total.shape[1]))
    for core in range(NC):
        out[core, :height] = total[core * height : (core + 1) * height]


def sums_of(got):
    got = got.astype(jnp.float32)
    rows = got.shape[-2] - EXTRA
    return got[..., :rows, :] * jnp.exp2(got[..., rows : rows + 1, :] - SCALED)


def contract(mine, other, high, low, by_core, across, along=range(NY), before=(), scaled=False):
    used = sorted({PLACES[not by_core][half, y, across][0] for half in range(2) for y in along})
    height = mine[0].shape[-2]
    depth, columns = high.shape
    depth = depth // NY * len(along)
    local = pl.BlockSpec(memory_space=pltpu.VMEM)
    return pl.pallas_call(
        functools.partial(contract_kernel, by_core, across, tuple(along), used),
        in_specs=[local] * (2 * len(used) + 2 + len(before)),
        out_specs=local,
        out_shape=jax.ShapeDtypeStruct((NC, height + EXTRA * scaled, columns), jnp.float32),
        scratch_shapes=[pltpu.VMEM((NC * height, depth), jnp.bfloat16)],
        compiler_params=pltpu.CompilerParams(vmem_limit_bytes=24 * MIB),
        cost_estimate=pl.CostEstimate(
            flops=4 * NC * height * depth * columns, bytes_accessed=4 * depth * columns + 2 * NC * height * depth + 4 * NC * height * columns, transcendentals=0
        ),
        name=f"contract_{'sent' if across else 'kept'}_{len(before)}",
    )(*(mine[i] for i in used), *(other[i] for i in used), high, low, *before)


def on_device(amplitudes, driver, pair_energy, virt_energy, integrals, src_block, dst_block):
    tile_width = integrals.shape[1]
    local_blocks = virt_energy.shape[0] // tile_width
    blocks, half = NZ * NY * local_blocks, local_blocks // NC
    cut = half * tile_width

    def build():
        return sum_tiles(integrals, src_block, dst_block, local_blocks, blocks, amplitudes.shape[0])

    for iteration in range(ITERS):
        if iteration == 0:
            mine, (total, given, which) = gather_panel(over_z(amplitudes), parts_of, build)
            high, low = split_parts(total, over_core(given), half)
            lower = which == 0
            terms = jnp.stack([driver, virt_energy[None, :] - pair_energy[:, None]])
            kept_terms = jnp.where(lower, terms[..., :cut], terms[..., cut:])
            given_terms = jnp.where(lower, terms[..., cut:], terms[..., :cut])
            both_terms = jnp.stack([kept_terms, over_core(given_terms)], axis=1)
        else:
            mine, _ = gather_panel(over_z(shard), lambda parts: parts)
        *early, last = mine
        other = [over_core(piece) for piece in early]
        begun = contract(early, other, high, low, iteration == 0, 1, [0])
        mine, other = [*early, last], [*other, over_core(last)]
        sent = contract(mine, other, high, low, iteration == 0, 1, [1], [begun], True)
        kept = contract(mine, other, high, low, iteration == 0, 0)
        if iteration < ITERS - 1:
            shard = ((both_terms[0] + (kept + sums_of(over_x(sent.astype(jnp.float16))))) / both_terms[1]).astype(jnp.bfloat16)
    sent = sent.astype(jnp.float16)
    got_there, got_here = over_diagonal(sent[1]), over_x(sent[0])
    got_there, kept = lax.optimization_barrier((got_there, kept))
    got_here, kept_there = lax.optimization_barrier((got_here, over_core(kept[1])))
    here, there = kept[0] + sums_of(got_here), kept_there + sums_of(got_there)
    ladder = jnp.concatenate([jnp.where(lower, here, there), jnp.where(lower, there, here)], axis=1)
    return ((driver + ladder) / (virt_energy[None, :] - pair_energy[:, None])).astype(jnp.bfloat16)


def solution(mesh):
    form = on_device if (mesh.shape["tile"], mesh.shape["grp"]) == (NZ * NY, NX * NC) else general_form
    return jax.shard_map(
        form,
        mesh=mesh,
        in_specs=(
            P("grp", "tile"),
            P("grp", "tile"),
            P("grp"),
            P("tile"),
            P(("tile", "grp"), None, None),
            P("tile"),
            P("tile"),
        ),
        out_specs=P("grp", "tile"),
        check_vma=False,
    )
```

```python
import functools
import math

import jax
import jax.numpy as jnp
from jax import lax
from jax.experimental import pallas as pl
from jax.experimental.pallas import tpu as pltpu
from jax.sharding import PartitionSpec as P

ITERS = 2
MIB = 1024 * 1024


def contract_blocks(amp_rows, tile_set, source, target, local_blocks):
    row_count = amp_rows.shape[0]
    tile_width = tile_set.shape[1]
    tile_count = tile_set.shape[0]
    group_size = math.gcd(tile_count, 48)
    turns = tile_count // group_size
    blocks = amp_rows.reshape(row_count, -1, tile_width)
    packed_tiles = tile_set.reshape(turns, group_size, tile_width, tile_width)
    packed_source = source.reshape(turns, group_size)
    packed_target = target.reshape(turns, group_size)

    def advance(total_sum, packed):
        picked = jnp.take(blocks, packed[1], axis=1)
        partial_value = jnp.einsum(
            "rgc,gcd->rgd", picked, packed[0], preferred_element_type=jnp.float32
        )
        pieces = []
        for block in range(local_blocks):
            chosen = (packed[2] == block)[None, :, None]
            pieces.append(jnp.sum(jnp.where(chosen, partial_value, 0.0), axis=1))
        return (total_sum + jnp.stack(pieces, axis=1), None)

    initial = jnp.zeros((row_count, local_blocks, tile_width), jnp.float32)
    total_sum, unused = lax.scan(advance, initial, (packed_tiles, packed_source, packed_target))
    return total_sum.reshape(row_count, local_blocks * tile_width)


def general_form(amplitudes, driver, pair_energy, virt_energy, integrals, src_block, dst_block):
    tile_width = integrals.shape[1]
    local_blocks = virt_energy.shape[0] // tile_width
    denominator = virt_energy[None, :] - pair_energy[:, None]
    current = amplitudes
    first_tile = lax.axis_index("grp") * integrals.shape[0]
    my_source = lax.dynamic_slice_in_dim(src_block, first_tile, integrals.shape[0])
    my_target = lax.dynamic_slice_in_dim(dst_block, first_tile, integrals.shape[0])
    for iteration in range(ITERS):
        all_pairs = lax.all_gather(current, "grp", axis=0, tiled=True)
        whole_panel = lax.all_gather(all_pairs, "tile", axis=1, tiled=True)
        partial_value = contract_blocks(whole_panel, integrals, my_source, my_target, local_blocks)
        ladder = lax.psum_scatter(partial_value, "grp", scatter_dimension=0, tiled=True)
        current = ((driver + ladder) / denominator).astype(jnp.bfloat16)
    return current


NZ, NY, NX, NC = 4, 2, 2, 2
PARTS = 2
SCALED = 14
EXTRA = 16


def z_swap(away):
    return [(t, t ^ (away * NY)) for t in range(NZ * NY)]


Y_SWAP = [(t, t ^ 1) for t in range(NZ * NY)]
X_SWAP = [(g, g ^ 2) for g in range(NX * NC)]
CORE_SWAP = [(g, g ^ 1) for g in range(NX * NC)]
DIAGONAL_SWAP = [(g, g ^ 3) for g in range(NX * NC)]


def over_y(value):
    return lax.ppermute(value, "tile", Y_SWAP)


def over_x(value):
    return lax.ppermute(value, "grp", X_SWAP)


def over_core(value):
    return lax.ppermute(value, "grp", CORE_SWAP)


def over_diagonal(value):
    return lax.ppermute(value, "grp", DIAGONAL_SWAP)


def parts_of(rows):
    return jnp.stack(jnp.split(rows, PARTS, axis=1))


def over_z(value):
    far = [lax.ppermute(value, "tile", z_swap(away)) for away in range(NZ // 2, NZ)]
    return [value] + [lax.ppermute(value, "tile", z_swap(away)) for away in range(1, NZ // 2)] + far


def gather_panel(shards, parts, build=None):
    built = [] if build is None else list(build())
    if build is not None:
        shards, built = lax.optimization_barrier((shards, built))
    a = jnp.stack([parts(shard) for shard in shards[: NZ // 2]])
    b = jnp.stack([parts(shard) for shard in shards[NZ // 2 :]])
    a_y, a_x = over_y(a), over_x(a)
    if build is not None:
        b_x, b_y, a_xy = over_x(b), over_y(b), over_x(a_y)
        b_xy = over_y(b_x)
        a_x, a_xy = lax.optimization_barrier((a_x, a_xy))
        b_y, b_xy = lax.optimization_barrier((b_y, b_xy))
        return [jnp.stack(pair) for pair in ((a, b), (a_y, b_x), (a_x, b_y), (a_xy, b_xy))], built
    b, a_y = lax.optimization_barrier((b, a_y))
    b_x, b_y, a_xy = over_diagonal(b), over_y(b), over_x(a_y)
    b_x, a_x = lax.optimization_barrier((b_x, a_x))
    a_xy, b_xy, b_y = lax.optimization_barrier((a_xy, over_y(b_x), b_y))
    return [jnp.stack(group) for group in ((a, b, b_y), (a_y, a_x, b_x), (a_xy, b_xy))], built


PLACES = (
    {(0, 0, 0): (0, 0), (1, 0, 0): (0, 1), (0, 1, 0): (1, 0), (1, 0, 1): (1, 1), (0, 0, 1): (2, 0), (1, 1, 0): (2, 1), (0, 1, 1): (3, 0), (1, 1, 1): (3, 1)},
    {(0, 0, 0): (0, 0), (1, 0, 0): (0, 1), (1, 1, 0): (0, 2), (0, 1, 0): (1, 0), (0, 0, 1): (1, 1), (1, 0, 1): (1, 2), (0, 1, 1): (2, 0), (1, 1, 1): (2, 1)},
)


def sum_kernel(chunk, local_blocks, src_any, dst_any, tiles_any, total, given, which, tiles, src, dst, list_sem, tile_sem):
    steps = tiles.shape[0] // chunk
    half = local_blocks // NC
    shift = half.bit_length() - 1
    slots = given.shape[0]
    lists = [pltpu.make_async_copy(a, b, list_sem.at[i]) for i, (a, b) in enumerate(((src_any, src), (dst_any, dst)))]
    for copy in lists:
        copy.start()

    def tile_copy(step):
        part = pl.ds(step * chunk, chunk)
        return pltpu.make_async_copy(tiles_any.at[part], tiles.at[part], tile_sem.at[step])

    for step in range(steps):
        tile_copy(step).start()

    def clear(slot, carry):
        total[slot] = jnp.zeros(total.shape[1:], jnp.float32)
        return carry

    lax.fori_loop(0, total.shape[0], clear, 0, unroll=4)
    for copy in lists:
        copy.wait()
    grp = lax.axis_index("grp")
    here = lax.axis_index("tile") * local_blocks
    core = lax.rem(grp, NC)
    which[...] = jnp.full(which.shape, core, jnp.int32)
    kept = core * half
    first = grp * tiles.shape[0]

    def run(step, carry):
        tile_copy(step).wait()

        def add(j, carry):
            k = step * chunk + j
            target = dst[first + k] ^ kept
            slot = (target >> shift) * slots + ((src[first + k] ^ here) << shift) + (target & (half - 1))
            total[slot] += tiles[k].astype(jnp.float32)
            return carry

        lax.fori_loop(0, chunk, add, 0, unroll=8)
        return carry

    lax.fori_loop(0, steps, run, 0)

    def give(slot, carry):
        given[slot] = total[slots + slot]
        return carry

    lax.fori_loop(0, slots, give, 0, unroll=4)


def sum_tiles(integrals, src_block, dst_block, local_blocks, blocks, rows):
    count, width, _ = integrals.shape
    slots = blocks * local_blocks // NC
    chunk = math.gcd(count, 24)
    outside = pl.BlockSpec(memory_space=pl.ANY)
    local = pl.BlockSpec(memory_space=pltpu.VMEM)
    return pl.pallas_call(
        functools.partial(sum_kernel, chunk, local_blocks),
        in_specs=[outside] * 3,
        out_specs=[local] * 3,
        out_shape=[
            pltpu.VMEM((NC * slots, width, width), jnp.float32),
            pltpu.VMEM((slots, width, width), jnp.float32),
            pltpu.VMEM((rows, local_blocks // NC * width), jnp.int32),
        ],
        scratch_shapes=[
            pltpu.VMEM(integrals.shape, jnp.bfloat16),
            pltpu.SMEM(src_block.shape, jnp.int32),
            pltpu.SMEM(dst_block.shape, jnp.int32),
            pltpu.SemaphoreType.DMA((2,)),
            pltpu.SemaphoreType.DMA((count // chunk,)),
        ],
        compiler_params=pltpu.CompilerParams(vmem_limit_bytes=24 * MIB),
        cost_estimate=pl.CostEstimate(
            flops=count * width * width, bytes_accessed=2 * count * width * width + 4 * slots * width * width, transcendentals=0
        ),
        name="sum_tiles",
    )(*(pltpu.with_memory_space_constraint(a, pltpu.HBM) for a in (src_block, dst_block, integrals)))


def split_kernel(half, mine, got, high, low):
    width = mine.shape[-1]

    def split(block, carry):
        for d in range(half):
            value = mine[block * half + d] + got[block * half + d]
            top = value.astype(jnp.bfloat16)
            rest = value - top.astype(jnp.float32)
            high[block, :, d * width : (d + 1) * width] = top
            low[block, :, d * width : (d + 1) * width] = rest.astype(jnp.bfloat16)
        return carry

    lax.fori_loop(0, got.shape[0] // half, split, 0)


def split_parts(mine, got, half):
    slots, width, _ = got.shape
    shape = pltpu.VMEM((slots // half, width, half * width), jnp.bfloat16)
    local = pl.BlockSpec(memory_space=pltpu.VMEM)
    high, low = pl.pallas_call(
        functools.partial(split_kernel, half),
        in_specs=[local, local],
        out_specs=[local, local],
        out_shape=[shape, shape],
        compiler_params=pltpu.CompilerParams(vmem_limit_bytes=24 * MIB),
        cost_estimate=pl.CostEstimate(flops=3 * got.size, bytes_accessed=12 * got.size, transcendentals=0),
        name="split_parts",
    )(*(pltpu.with_memory_space_constraint(a, pltpu.VMEM) for a in (mine, got)))
    return high.reshape(-1, half * width), low.reshape(-1, half * width)


def contract_kernel(by_core, across, along, used, *refs):
    mine, other = (dict(zip(used, part)) for part in (refs[: len(used)], refs[len(used) : 2 * len(used)]))
    high, low, *before, out, rows = refs[2 * len(used) :]
    height, depth = next(iter(mine.values())).shape[-2:]
    wide = PARTS * depth
    core = lax.rem(lax.axis_index("grp"), NC)
    spans = [(z, y) for z in range(NZ) for y in along]
    for away, pieces in enumerate((mine, other)):
        for part in range(PARTS):
            for span, (z, y) in enumerate(spans):
                far = z // (NZ // 2)
                piece, index = PLACES[not by_core][far, y, across]
                owner = away if by_core else away ^ (far & across)
                row = (owner if by_core else part ^ owner) * height
                half = part if by_core else (core if owner == 0 else 1 - core)
                column = span * wide + half * depth
                if not by_core:
                    column = pl.multiple_of(column, depth)
                rows[row : row + height, pl.ds(column, depth)] = pieces[piece][index, z % (NZ // 2), part]
    total = sum(ref[...].reshape(NC * height, -1) for ref in before)
    if len(along) == NY:
        chunks = [(rows[...], slice(None))]
    else:
        chunks = [(rows[:, i * wide : (i + 1) * wide], pl.ds((z * NY + y) * wide, wide)) for i, (z, y) in enumerate(spans)]
    for left, right in chunks:
        for matrix in (high, low):
            total += jnp.dot(left, matrix[right, :], preferred_element_type=jnp.float32)
    if out.shape[1] > height:
        most = jnp.clip(jnp.max(jnp.abs(total), keepdims=True), 1e-30, 1e30)
        exponent = jnp.ceil(jnp.log2(most))
        total *= jnp.exp2(SCALED - exponent)
        for core in range(NC):
            out[core, height:] = jnp.broadcast_to(exponent, (out.shape[1] - height, total.shape[1]))
    for core in range(NC):
        out[core, :height] = total[core * height : (core + 1) * height]


def sums_of(got):
    got = got.astype(jnp.float32)
    rows = got.shape[-2] - EXTRA
    return got[..., :rows, :] * jnp.exp2(got[..., rows : rows + 1, :] - SCALED)


def contract(mine, other, high, low, by_core, across, along=range(NY), before=(), scaled=False):
    used = sorted({PLACES[not by_core][half, y, across][0] for half in range(2) for y in along})
    height = mine[0].shape[-2]
    depth, columns = high.shape
    depth = depth // NY * len(along)
    local = pl.BlockSpec(memory_space=pltpu.VMEM)
    return pl.pallas_call(
        functools.partial(contract_kernel, by_core, across, tuple(along), used),
        in_specs=[local] * (2 * len(used) + 2 + len(before)),
        out_specs=local,
        out_shape=jax.ShapeDtypeStruct((NC, height + EXTRA * scaled, columns), jnp.float32),
        scratch_shapes=[pltpu.VMEM((NC * height, depth), jnp.bfloat16)],
        compiler_params=pltpu.CompilerParams(vmem_limit_bytes=24 * MIB),
        cost_estimate=pl.CostEstimate(
            flops=4 * NC * height * depth * columns, bytes_accessed=4 * depth * columns + 2 * NC * height * depth + 4 * NC * height * columns, transcendentals=0
        ),
        name=f"contract_{'sent' if across else 'kept'}_{len(before)}",
    )(*(mine[i] for i in used), *(other[i] for i in used), high, low, *before)


def on_device(amplitudes, driver, pair_energy, virt_energy, integrals, src_block, dst_block):
    tile_width = integrals.shape[1]
    local_blocks = virt_energy.shape[0] // tile_width
    blocks, half = NZ * NY * local_blocks, local_blocks // NC
    cut = half * tile_width

    def build():
        return sum_tiles(integrals, src_block, dst_block, local_blocks, blocks, amplitudes.shape[0])

    for iteration in range(ITERS):
        if iteration == 0:
            mine, (total, given, which) = gather_panel(over_z(amplitudes), parts_of, build)
            high, low = split_parts(total, over_core(given), half)
            lower = which == 0
            terms = jnp.stack([driver, virt_energy[None, :] - pair_energy[:, None]])
            kept_terms = jnp.where(lower, terms[..., :cut], terms[..., cut:])
            given_terms = jnp.where(lower, terms[..., cut:], terms[..., :cut])
            both_terms = jnp.stack([kept_terms, over_core(given_terms)], axis=1)
        else:
            mine, _ = gather_panel(over_z(shard), lambda parts: parts)
        *early, last = mine
        other = [over_core(piece) for piece in early]
        begun = contract(early, other, high, low, iteration == 0, 1, [0])
        mine, other = [*early, last], [*other, over_core(last)]
        sent = contract(mine, other, high, low, iteration == 0, 1, [1], [begun], True)
        kept = contract(mine, other, high, low, iteration == 0, 0)
        if iteration < ITERS - 1:
            shard = ((both_terms[0] + (kept + sums_of(over_x(sent.astype(jnp.float16))))) / both_terms[1]).astype(jnp.bfloat16)
    sent = sent.astype(jnp.float16)
    got_there, got_here = over_diagonal(sent[1]), over_x(sent[0])
    got_there, kept = lax.optimization_barrier((got_there, kept))
    got_here, kept_there = lax.optimization_barrier((got_here, over_core(kept[1])))
    here, there = kept[0] + sums_of(got_here), kept_there + sums_of(got_there)
    ladder = jnp.concatenate([jnp.where(lower, here, there), jnp.where(lower, there, here)], axis=1)
    return ((driver + ladder) / (virt_energy[None, :] - pair_energy[:, None])).astype(jnp.bfloat16)


def solution(mesh):
    form = on_device if (mesh.shape["tile"], mesh.shape["grp"]) == (NZ * NY, NX * NC) else general_form
    return jax.shard_map(
        form,
        mesh=mesh,
        in_specs=(
            P("grp", "tile"),
            P("grp", "tile"),
            P("grp"),
            P("tile"),
            P(("tile", "grp"), None, None),
            P("tile"),
            P("tile"),
        ),
        out_specs=P("grp", "tile"),
        check_vma=False,
    )
```

```python
import functools
import math

import jax
import jax.numpy as jnp
from jax import lax
from jax.experimental import pallas as pl
from jax.experimental.pallas import tpu as pltpu
from jax.sharding import PartitionSpec as P

ITERS = 2
MIB = 1024 * 1024


def contract_blocks(amp_rows, tile_set, source, target, local_blocks):
    row_count = amp_rows.shape[0]
    tile_width = tile_set.shape[1]
    tile_count = tile_set.shape[0]
    group_size = math.gcd(tile_count, 48)
    turns = tile_count // group_size
    blocks = amp_rows.reshape(row_count, -1, tile_width)
    packed_tiles = tile_set.reshape(turns, group_size, tile_width, tile_width)
    packed_source = source.reshape(turns, group_size)
    packed_target = target.reshape(turns, group_size)

    def advance(total_sum, packed):
        picked = jnp.take(blocks, packed[1], axis=1)
        partial_value = jnp.einsum(
            "rgc,gcd->rgd", picked, packed[0], preferred_element_type=jnp.float32
        )
        pieces = []
        for block in range(local_blocks):
            chosen = (packed[2] == block)[None, :, None]
            pieces.append(jnp.sum(jnp.where(chosen, partial_value, 0.0), axis=1))
        return (total_sum + jnp.stack(pieces, axis=1), None)

    initial = jnp.zeros((row_count, local_blocks, tile_width), jnp.float32)
    total_sum, unused = lax.scan(advance, initial, (packed_tiles, packed_source, packed_target))
    return total_sum.reshape(row_count, local_blocks * tile_width)


def general_form(amplitudes, driver, pair_energy, virt_energy, integrals, src_block, dst_block):
    tile_width = integrals.shape[1]
    local_blocks = virt_energy.shape[0] // tile_width
    denominator = virt_energy[None, :] - pair_energy[:, None]
    current = amplitudes
    first_tile = lax.axis_index("grp") * integrals.shape[0]
    my_source = lax.dynamic_slice_in_dim(src_block, first_tile, integrals.shape[0])
    my_target = lax.dynamic_slice_in_dim(dst_block, first_tile, integrals.shape[0])
    for iteration in range(ITERS):
        all_pairs = lax.all_gather(current, "grp", axis=0, tiled=True)
        whole_panel = lax.all_gather(all_pairs, "tile", axis=1, tiled=True)
        partial_value = contract_blocks(whole_panel, integrals, my_source, my_target, local_blocks)
        ladder = lax.psum_scatter(partial_value, "grp", scatter_dimension=0, tiled=True)
        current = ((driver + ladder) / denominator).astype(jnp.bfloat16)
    return current


NZ, NY, NX, NC = 4, 2, 2, 2
PARTS = 2
SCALED = 14
EXTRA = 16


def z_swap(away):
    return [(t, t ^ (away * NY)) for t in range(NZ * NY)]


Y_SWAP = [(t, t ^ 1) for t in range(NZ * NY)]
X_SWAP = [(g, g ^ 2) for g in range(NX * NC)]
CORE_SWAP = [(g, g ^ 1) for g in range(NX * NC)]
DIAGONAL_SWAP = [(g, g ^ 3) for g in range(NX * NC)]


def over_y(value):
    return lax.ppermute(value, "tile", Y_SWAP)


def over_x(value):
    return lax.ppermute(value, "grp", X_SWAP)


def over_core(value):
    return lax.ppermute(value, "grp", CORE_SWAP)


def over_diagonal(value):
    return lax.ppermute(value, "grp", DIAGONAL_SWAP)


def parts_of(rows):
    return jnp.stack(jnp.split(rows, PARTS, axis=1))


def over_z(value):
    far = [lax.ppermute(value, "tile", z_swap(away)) for away in range(NZ // 2, NZ)]
    return [value] + [lax.ppermute(value, "tile", z_swap(away)) for away in range(1, NZ // 2)] + far


def gather_panel(shards, parts, build=None):
    built = [] if build is None else list(build())
    if build is not None:
        shards, built = lax.optimization_barrier((shards, built))
    a = jnp.stack([parts(shard) for shard in shards[: NZ // 2]])
    b = jnp.stack([parts(shard) for shard in shards[NZ // 2 :]])
    a_y, a_x = over_y(a), over_x(a)
    if build is not None:
        b_x, b_y, a_xy = over_x(b), over_y(b), over_x(a_y)
        b_xy = over_y(b_x)
        a_x, a_xy = lax.optimization_barrier((a_x, a_xy))
        b_y, b_xy = lax.optimization_barrier((b_y, b_xy))
        return [jnp.stack(pair) for pair in ((a, b), (a_y, b_x), (a_x, b_y), (a_xy, b_xy))], built
    b, a_y = lax.optimization_barrier((b, a_y))
    b_x, b_y, a_xy = over_x(b), over_y(b), over_x(a_y)
    b_x, a_x = lax.optimization_barrier((b_x, a_x))
    a_xy, b_xy, b_y = lax.optimization_barrier((a_xy, over_y(b_x), b_y))
    return [jnp.stack(group) for group in ((a, b, b_y), (a_y, a_x, b_x), (a_xy, b_xy))], built


PLACES = (
    {(0, 0, 0): (0, 0), (1, 0, 0): (0, 1), (0, 1, 0): (1, 0), (1, 0, 1): (1, 1), (0, 0, 1): (2, 0), (1, 1, 0): (2, 1), (0, 1, 1): (3, 0), (1, 1, 1): (3, 1)},
    {(0, 0, 0): (0, 0), (1, 0, 0): (0, 1), (1, 1, 0): (0, 2), (0, 1, 0): (1, 0), (0, 0, 1): (1, 1), (1, 0, 1): (1, 2), (0, 1, 1): (2, 0), (1, 1, 1): (2, 1)},
)


def sum_kernel(chunk, local_blocks, src_any, dst_any, tiles_any, total, given, which, tiles, src, dst, list_sem, tile_sem):
    steps = tiles.shape[0] // chunk
    half = local_blocks // NC
    shift = half.bit_length() - 1
    slots = given.shape[0]
    lists = [pltpu.make_async_copy(a, b, list_sem.at[i]) for i, (a, b) in enumerate(((src_any, src), (dst_any, dst)))]
    for copy in lists:
        copy.start()

    def tile_copy(step):
        part = pl.ds(step * chunk, chunk)
        return pltpu.make_async_copy(tiles_any.at[part], tiles.at[part], tile_sem.at[step])

    for step in range(steps):
        tile_copy(step).start()

    def clear(slot, carry):
        total[slot] = jnp.zeros(total.shape[1:], jnp.float32)
        return carry

    lax.fori_loop(0, total.shape[0], clear, 0, unroll=4)
    for copy in lists:
        copy.wait()
    grp = lax.axis_index("grp")
    here = lax.axis_index("tile") * local_blocks
    core = lax.rem(grp, NC)
    which[...] = jnp.full(which.shape, core, jnp.int32)
    kept = core * half
    first = grp * tiles.shape[0]

    def run(step, carry):
        tile_copy(step).wait()

        def add(j, carry):
            k = step * chunk + j
            target = dst[first + k] ^ kept
            slot = (target >> shift) * slots + ((src[first + k] ^ here) << shift) + (target & (half - 1))
            total[slot] += tiles[k].astype(jnp.float32)
            return carry

        lax.fori_loop(0, chunk, add, 0, unroll=8)
        return carry

    lax.fori_loop(0, steps, run, 0)

    def give(slot, carry):
        given[slot] = total[slots + slot]
        return carry

    lax.fori_loop(0, slots, give, 0, unroll=4)


def sum_tiles(integrals, src_block, dst_block, local_blocks, blocks, rows):
    count, width, _ = integrals.shape
    slots = blocks * local_blocks // NC
    chunk = math.gcd(count, 24)
    outside = pl.BlockSpec(memory_space=pl.ANY)
    local = pl.BlockSpec(memory_space=pltpu.VMEM)
    return pl.pallas_call(
        functools.partial(sum_kernel, chunk, local_blocks),
        in_specs=[outside] * 3,
        out_specs=[local] * 3,
        out_shape=[
            pltpu.VMEM((NC * slots, width, width), jnp.float32),
            pltpu.VMEM((slots, width, width), jnp.float32),
            pltpu.VMEM((rows, local_blocks // NC * width), jnp.int32),
        ],
        scratch_shapes=[
            pltpu.VMEM(integrals.shape, jnp.bfloat16),
            pltpu.SMEM(src_block.shape, jnp.int32),
            pltpu.SMEM(dst_block.shape, jnp.int32),
            pltpu.SemaphoreType.DMA((2,)),
            pltpu.SemaphoreType.DMA((count // chunk,)),
        ],
        compiler_params=pltpu.CompilerParams(vmem_limit_bytes=24 * MIB),
        cost_estimate=pl.CostEstimate(
            flops=count * width * width, bytes_accessed=2 * count * width * width + 4 * slots * width * width, transcendentals=0
        ),
        name="sum_tiles",
    )(*(pltpu.with_memory_space_constraint(a, pltpu.HBM) for a in (src_block, dst_block, integrals)))


def split_kernel(half, mine, got, high, low):
    width = mine.shape[-1]

    def split(block, carry):
        for d in range(half):
            value = mine[block * half + d] + got[block * half + d]
            top = value.astype(jnp.bfloat16)
            rest = value - top.astype(jnp.float32)
            high[block, :, d * width : (d + 1) * width] = top
            low[block, :, d * width : (d + 1) * width] = rest.astype(jnp.bfloat16)
        return carry

    lax.fori_loop(0, got.shape[0] // half, split, 0)


def split_parts(mine, got, half):
    slots, width, _ = got.shape
    shape = pltpu.VMEM((slots // half, width, half * width), jnp.bfloat16)
    local = pl.BlockSpec(memory_space=pltpu.VMEM)
    high, low = pl.pallas_call(
        functools.partial(split_kernel, half),
        in_specs=[local, local],
        out_specs=[local, local],
        out_shape=[shape, shape],
        compiler_params=pltpu.CompilerParams(vmem_limit_bytes=24 * MIB),
        cost_estimate=pl.CostEstimate(flops=3 * got.size, bytes_accessed=12 * got.size, transcendentals=0),
        name="split_parts",
    )(*(pltpu.with_memory_space_constraint(a, pltpu.VMEM) for a in (mine, got)))
    return high.reshape(-1, half * width), low.reshape(-1, half * width)


def contract_kernel(by_core, across, along, used, scaled, *refs):
    mine, other = (dict(zip(used, part)) for part in (refs[: len(used)], refs[len(used) : 2 * len(used)]))
    high, low, *before, out, rows = refs[2 * len(used) :]
    height, depth = next(iter(mine.values())).shape[-2:]
    wide = PARTS * depth
    core = lax.rem(lax.axis_index("grp"), NC)
    spans = [(z, y) for z in range(NZ) for y in along]
    for away, pieces in enumerate((mine, other)):
        for part in range(PARTS):
            row = (away if by_core else part ^ away) * height
            half = part if by_core else (core if away == 0 else 1 - core)
            for span, (z, y) in enumerate(spans):
                piece, index = PLACES[not by_core][z // (NZ // 2), y, across]
                column = span * wide + half * depth
                if not by_core:
                    column = pl.multiple_of(column, depth)
                rows[row : row + height, pl.ds(column, depth)] = pieces[piece][index, z % (NZ // 2), part]
    total = sum(ref[...].reshape(NC * height, -1) for ref in before)
    if len(along) == NY:
        chunks = [(rows[...], slice(None))]
    else:
        chunks = [(rows[:, i * wide : (i + 1) * wide], pl.ds((z * NY + y) * wide, wide)) for i, (z, y) in enumerate(spans)]
    for left, right in chunks:
        for matrix in (high, low):
            total += jnp.dot(left, matrix[right, :], preferred_element_type=jnp.float32)
    if scaled:
        most = jnp.clip(jnp.max(jnp.abs(total), keepdims=True), 1e-30, 1e30)
        exponent = jnp.ceil(jnp.log2(most))
        total *= jnp.exp2(SCALED - exponent)
        exponents = jnp.broadcast_to(exponent, (EXTRA, total.shape[1]))
        if len(out.shape) == 2:
            out[: NC * height] = total
            out[NC * height :] = exponents
        else:
            for core in range(NC):
                out[core, :height] = total[core * height : (core + 1) * height]
                out[core, height:] = exponents
    else:
        for core in range(NC):
            out[core] = total[core * height : (core + 1) * height]


def sums_of(got):
    got = got.astype(jnp.float32)
    rows = got.shape[-2] - EXTRA
    return got[..., :rows, :] * jnp.exp2(got[..., rows : rows + 1, :] - SCALED)


def contract(mine, other, high, low, by_core, across, along=range(NY), before=(), scaled=0):
    used = sorted({PLACES[not by_core][half, y, across][0] for half in range(2) for y in along})
    height = mine[0].shape[-2]
    depth, columns = high.shape
    depth = depth // NY * len(along)
    shape = {0: (NC, height, columns), 1: (NC * height + EXTRA, columns), 2: (NC, height + EXTRA, columns)}[scaled]
    local = pl.BlockSpec(memory_space=pltpu.VMEM)
    return pl.pallas_call(
        functools.partial(contract_kernel, by_core, across, tuple(along), used, scaled),
        in_specs=[local] * (2 * len(used) + 2 + len(before)),
        out_specs=local,
        out_shape=jax.ShapeDtypeStruct(shape, jnp.float32),
        scratch_shapes=[pltpu.VMEM((NC * height, depth), jnp.bfloat16)],
        compiler_params=pltpu.CompilerParams(vmem_limit_bytes=24 * MIB),
        cost_estimate=pl.CostEstimate(
            flops=4 * NC * height * depth * columns, bytes_accessed=4 * depth * columns + 2 * NC * height * depth + 4 * NC * height * columns, transcendentals=0
        ),
        name=f"contract_{'sent' if across else 'kept'}_{len(before)}",
    )(*(mine[i] for i in used), *(other[i] for i in used), high, low, *before)


def on_device(amplitudes, driver, pair_energy, virt_energy, integrals, src_block, dst_block):
    tile_width = integrals.shape[1]
    local_blocks = virt_energy.shape[0] // tile_width
    blocks, half = NZ * NY * local_blocks, local_blocks // NC
    cut = half * tile_width

    def build():
        return sum_tiles(integrals, src_block, dst_block, local_blocks, blocks, amplitudes.shape[0])

    for iteration in range(ITERS):
        if iteration == 0:
            mine, (total, given, which) = gather_panel(over_z(amplitudes), parts_of, build)
            high, low = split_parts(total, over_core(given), half)
            lower = which == 0
            terms = jnp.stack([driver, virt_energy[None, :] - pair_energy[:, None]])
            kept_terms = jnp.where(lower, terms[..., :cut], terms[..., cut:])
            given_terms = jnp.where(lower, terms[..., cut:], terms[..., :cut])
            both_terms = jnp.stack([kept_terms, over_core(given_terms)], axis=1)
        else:
            mine, _ = gather_panel(over_z(shard), lambda parts: parts)
        *early, last = mine
        other = [over_core(piece) for piece in early]
        begun = contract(early, other, high, low, iteration == 0, 1, [0])
        mine, other = [*early, last], [*other, over_core(last)]
        sent = contract(mine, other, high, low, iteration == 0, 1, [1], [begun], 1 + iteration)
        kept = contract(mine, other, high, low, iteration == 0, 0)
        if iteration < ITERS - 1:
            shard = ((both_terms[0] + (kept + sums_of(over_x(sent.astype(jnp.float16))).reshape(kept.shape))) / both_terms[1]).astype(jnp.bfloat16)
    sent = sent.astype(jnp.float16)
    got_here, got_there = over_x(sent[0]), over_diagonal(sent[1])
    got_here, kept = lax.optimization_barrier((got_here, kept))
    got_there, kept_there = lax.optimization_barrier((got_there, over_core(kept[1])))
    here, there = kept[0] + sums_of(got_here), kept_there + sums_of(got_there)
    ladder = jnp.concatenate([jnp.where(lower, here, there), jnp.where(lower, there, here)], axis=1)
    return ((driver + ladder) / (virt_energy[None, :] - pair_energy[:, None])).astype(jnp.bfloat16)


def solution(mesh):
    form = on_device if (mesh.shape["tile"], mesh.shape["grp"]) == (NZ * NY, NX * NC) else general_form
    return jax.shard_map(
        form,
        mesh=mesh,
        in_specs=(
            P("grp", "tile"),
            P("grp", "tile"),
            P("grp"),
            P("tile"),
            P(("tile", "grp"), None, None),
            P("tile"),
            P("tile"),
        ),
        out_specs=P("grp", "tile"),
        check_vma=False,
    )
```

```python
import functools
import math

import jax
import jax.numpy as jnp
from jax import lax
from jax.experimental import pallas as pl
from jax.experimental.pallas import tpu as pltpu
from jax.sharding import PartitionSpec as P

ITERS = 2
MIB = 1024 * 1024


def contract_blocks(amp_rows, tile_set, source, target, local_blocks):
    row_count = amp_rows.shape[0]
    tile_width = tile_set.shape[1]
    tile_count = tile_set.shape[0]
    group_size = math.gcd(tile_count, 48)
    turns = tile_count // group_size
    blocks = amp_rows.reshape(row_count, -1, tile_width)
    packed_tiles = tile_set.reshape(turns, group_size, tile_width, tile_width)
    packed_source = source.reshape(turns, group_size)
    packed_target = target.reshape(turns, group_size)

    def advance(total_sum, packed):
        picked = jnp.take(blocks, packed[1], axis=1)
        partial_value = jnp.einsum(
            "rgc,gcd->rgd", picked, packed[0], preferred_element_type=jnp.float32
        )
        pieces = []
        for block in range(local_blocks):
            chosen = (packed[2] == block)[None, :, None]
            pieces.append(jnp.sum(jnp.where(chosen, partial_value, 0.0), axis=1))
        return (total_sum + jnp.stack(pieces, axis=1), None)

    initial = jnp.zeros((row_count, local_blocks, tile_width), jnp.float32)
    total_sum, unused = lax.scan(advance, initial, (packed_tiles, packed_source, packed_target))
    return total_sum.reshape(row_count, local_blocks * tile_width)


def general_form(amplitudes, driver, pair_energy, virt_energy, integrals, src_block, dst_block):
    tile_width = integrals.shape[1]
    local_blocks = virt_energy.shape[0] // tile_width
    denominator = virt_energy[None, :] - pair_energy[:, None]
    current = amplitudes
    first_tile = lax.axis_index("grp") * integrals.shape[0]
    my_source = lax.dynamic_slice_in_dim(src_block, first_tile, integrals.shape[0])
    my_target = lax.dynamic_slice_in_dim(dst_block, first_tile, integrals.shape[0])
    for iteration in range(ITERS):
        all_pairs = lax.all_gather(current, "grp", axis=0, tiled=True)
        whole_panel = lax.all_gather(all_pairs, "tile", axis=1, tiled=True)
        partial_value = contract_blocks(whole_panel, integrals, my_source, my_target, local_blocks)
        ladder = lax.psum_scatter(partial_value, "grp", scatter_dimension=0, tiled=True)
        current = ((driver + ladder) / denominator).astype(jnp.bfloat16)
    return current


NZ, NY, NX, NC = 4, 2, 2, 2
PARTS = 2
SCALED = 14
EXTRA = 16


def z_swap(away):
    return [(t, t ^ (away * NY)) for t in range(NZ * NY)]


Y_SWAP = [(t, t ^ 1) for t in range(NZ * NY)]
X_SWAP = [(g, g ^ 2) for g in range(NX * NC)]
CORE_SWAP = [(g, g ^ 1) for g in range(NX * NC)]
DIAGONAL_SWAP = [(g, g ^ 3) for g in range(NX * NC)]


def over_y(value):
    return lax.ppermute(value, "tile", Y_SWAP)


def over_x(value):
    return lax.ppermute(value, "grp", X_SWAP)


def over_core(value):
    return lax.ppermute(value, "grp", CORE_SWAP)


def over_diagonal(value):
    return lax.ppermute(value, "grp", DIAGONAL_SWAP)


def parts_of(rows):
    return jnp.stack(jnp.split(rows, PARTS, axis=1))


def over_z(value):
    far = [lax.ppermute(value, "tile", z_swap(away)) for away in range(NZ - 1, NZ // 2 - 1, -1)]
    return [value] + [lax.ppermute(value, "tile", z_swap(away)) for away in range(1, NZ // 2)] + far


def gather_panel(shards, parts, build=None):
    built = [] if build is None else list(build())
    if build is not None:
        shards, built = lax.optimization_barrier((shards, built))
    a = jnp.stack([parts(shard) for shard in shards[: NZ // 2]])
    b = jnp.stack([parts(shard) for shard in shards[NZ // 2 :]])
    a_y, a_x = over_y(a), over_x(a)
    if build is not None:
        b_x, b_y, a_xy = over_x(b), over_y(b), over_x(a_y)
        b_xy = over_y(b_x)
        a_x, a_xy = lax.optimization_barrier((a_x, a_xy))
        b_y, b_xy = lax.optimization_barrier((b_y, b_xy))
        return [jnp.stack(pair) for pair in ((a, b), (a_y, b_x), (a_x, b_y), (a_xy, b_xy))], built
    b, a_y = lax.optimization_barrier((b, a_y))
    b_x, b_y, a_xy = over_x(b), over_y(b), over_x(a_y)
    b_x, a_x = lax.optimization_barrier((b_x, a_x))
    a_xy, b_xy, b_y = lax.optimization_barrier((a_xy, over_y(b_x), b_y))
    return [jnp.stack(group) for group in ((a, b, b_y), (a_y, a_x, b_x), (a_xy, b_xy))], built


PLACES = (
    {(0, 0, 0): (0, 0), (1, 0, 0): (0, 1), (0, 1, 0): (1, 0), (1, 0, 1): (1, 1), (0, 0, 1): (2, 0), (1, 1, 0): (2, 1), (0, 1, 1): (3, 0), (1, 1, 1): (3, 1)},
    {(0, 0, 0): (0, 0), (1, 0, 0): (0, 1), (1, 1, 0): (0, 2), (0, 1, 0): (1, 0), (0, 0, 1): (1, 1), (1, 0, 1): (1, 2), (0, 1, 1): (2, 0), (1, 1, 1): (2, 1)},
)


def sum_kernel(chunk, local_blocks, src_any, dst_any, tiles_any, total, given, which, tiles, src, dst, list_sem, tile_sem):
    steps = tiles.shape[0] // chunk
    half = local_blocks // NC
    shift = half.bit_length() - 1
    slots = given.shape[0]
    lists = [pltpu.make_async_copy(a, b, list_sem.at[i]) for i, (a, b) in enumerate(((src_any, src), (dst_any, dst)))]
    for copy in lists:
        copy.start()

    def tile_copy(step):
        part = pl.ds(step * chunk, chunk)
        return pltpu.make_async_copy(tiles_any.at[part], tiles.at[part], tile_sem.at[step])

    for step in range(steps):
        tile_copy(step).start()

    def clear(slot, carry):
        total[slot] = jnp.zeros(total.shape[1:], jnp.float32)
        return carry

    lax.fori_loop(0, total.shape[0], clear, 0, unroll=4)
    for copy in lists:
        copy.wait()
    grp = lax.axis_index("grp")
    here = lax.axis_index("tile") * local_blocks
    core = lax.rem(grp, NC)
    which[...] = jnp.full(which.shape, core, jnp.int32)
    kept = core * half
    first = grp * tiles.shape[0]

    def run(step, carry):
        tile_copy(step).wait()

        def add(j, carry):
            k = step * chunk + j
            target = dst[first + k] ^ kept
            slot = (target >> shift) * slots + ((src[first + k] ^ here) << shift) + (target & (half - 1))
            total[slot] += tiles[k].astype(jnp.float32)
            return carry

        lax.fori_loop(0, chunk, add, 0, unroll=8)
        return carry

    lax.fori_loop(0, steps, run, 0)

    def give(slot, carry):
        given[slot] = total[slots + slot]
        return carry

    lax.fori_loop(0, slots, give, 0, unroll=4)


def sum_tiles(integrals, src_block, dst_block, local_blocks, blocks, rows):
    count, width, _ = integrals.shape
    slots = blocks * local_blocks // NC
    chunk = math.gcd(count, 24)
    outside = pl.BlockSpec(memory_space=pl.ANY)
    local = pl.BlockSpec(memory_space=pltpu.VMEM)
    return pl.pallas_call(
        functools.partial(sum_kernel, chunk, local_blocks),
        in_specs=[outside] * 3,
        out_specs=[local] * 3,
        out_shape=[
            pltpu.VMEM((NC * slots, width, width), jnp.float32),
            pltpu.VMEM((slots, width, width), jnp.float32),
            pltpu.VMEM((rows, local_blocks // NC * width), jnp.int32),
        ],
        scratch_shapes=[
            pltpu.VMEM(integrals.shape, jnp.bfloat16),
            pltpu.SMEM(src_block.shape, jnp.int32),
            pltpu.SMEM(dst_block.shape, jnp.int32),
            pltpu.SemaphoreType.DMA((2,)),
            pltpu.SemaphoreType.DMA((count // chunk,)),
        ],
        compiler_params=pltpu.CompilerParams(vmem_limit_bytes=24 * MIB),
        cost_estimate=pl.CostEstimate(
            flops=count * width * width, bytes_accessed=2 * count * width * width + 4 * slots * width * width, transcendentals=0
        ),
        name="sum_tiles",
    )(*(pltpu.with_memory_space_constraint(a, pltpu.HBM) for a in (src_block, dst_block, integrals)))


def split_kernel(half, mine, got, high, low):
    width = mine.shape[-1]

    def split(block, carry):
        for d in range(half):
            value = mine[block * half + d] + got[block * half + d]
            top = value.astype(jnp.bfloat16)
            rest = value - top.astype(jnp.float32)
            high[block, :, d * width : (d + 1) * width] = top
            low[block, :, d * width : (d + 1) * width] = rest.astype(jnp.bfloat16)
        return carry

    lax.fori_loop(0, got.shape[0] // half, split, 0)


def split_parts(mine, got, half):
    slots, width, _ = got.shape
    shape = pltpu.VMEM((slots // half, width, half * width), jnp.bfloat16)
    local = pl.BlockSpec(memory_space=pltpu.VMEM)
    high, low = pl.pallas_call(
        functools.partial(split_kernel, half),
        in_specs=[local, local],
        out_specs=[local, local],
        out_shape=[shape, shape],
        compiler_params=pltpu.CompilerParams(vmem_limit_bytes=24 * MIB),
        cost_estimate=pl.CostEstimate(flops=3 * got.size, bytes_accessed=12 * got.size, transcendentals=0),
        name="split_parts",
    )(*(pltpu.with_memory_space_constraint(a, pltpu.VMEM) for a in (mine, got)))
    return high.reshape(-1, half * width), low.reshape(-1, half * width)


def contract_kernel(by_core, across, along, used, *refs):
    mine, other = (dict(zip(used, part)) for part in (refs[: len(used)], refs[len(used) : 2 * len(used)]))
    high, low, *before, out, rows = refs[2 * len(used) :]
    height, depth = next(iter(mine.values())).shape[-2:]
    wide = PARTS * depth
    core = lax.rem(lax.axis_index("grp"), NC)
    spans = [(z, y) for z in range(NZ) for y in along]
    for away, pieces in enumerate((mine, other)):
        for part in range(PARTS):
            row = (away if by_core else part ^ away) * height
            half = part if by_core else (core if away == 0 else 1 - core)
            for span, (z, y) in enumerate(spans):
                piece, index = PLACES[not by_core][z // (NZ // 2), y, across]
                column = span * wide + half * depth
                if not by_core:
                    column = pl.multiple_of(column, depth)
                rows[row : row + height, pl.ds(column, depth)] = pieces[piece][index, (z ^ z // (NZ // 2)) % (NZ // 2), part]
    total = sum(ref[...].reshape(NC * height, -1) for ref in before)
    if len(along) == NY:
        chunks = [(rows[...], slice(None))]
    else:
        chunks = [(rows[:, i * wide : (i + 1) * wide], pl.ds((z * NY + y) * wide, wide)) for i, (z, y) in enumerate(spans)]
    for left, right in chunks:
        for matrix in (high, low):
            total += jnp.dot(left, matrix[right, :], preferred_element_type=jnp.float32)
    if out.shape[1] > height:
        most = jnp.clip(jnp.max(jnp.abs(total), keepdims=True), 1e-30, 1e30)
        exponent = jnp.ceil(jnp.log2(most))
        total *= jnp.exp2(SCALED - exponent)
        for core in range(NC):
            out[core, height:] = jnp.broadcast_to(exponent, (out.shape[1] - height, total.shape[1]))
    for core in range(NC):
        out[core, :height] = total[core * height : (core + 1) * height]


def sums_of(got):
    got = got.astype(jnp.float32)
    rows = got.shape[-2] - EXTRA
    return got[..., :rows, :] * jnp.exp2(got[..., rows : rows + 1, :] - SCALED)


def contract(mine, other, high, low, by_core, across, along=range(NY), before=(), scaled=False):
    used = sorted({PLACES[not by_core][half, y, across][0] for half in range(2) for y in along})
    height = mine[0].shape[-2]
    depth, columns = high.shape
    depth = depth // NY * len(along)
    local = pl.BlockSpec(memory_space=pltpu.VMEM)
    return pl.pallas_call(
        functools.partial(contract_kernel, by_core, across, tuple(along), used),
        in_specs=[local] * (2 * len(used) + 2 + len(before)),
        out_specs=local,
        out_shape=jax.ShapeDtypeStruct((NC, height + EXTRA * scaled, columns), jnp.float32),
        scratch_shapes=[pltpu.VMEM((NC * height, depth), jnp.bfloat16)],
        compiler_params=pltpu.CompilerParams(vmem_limit_bytes=24 * MIB),
        cost_estimate=pl.CostEstimate(
            flops=4 * NC * height * depth * columns, bytes_accessed=4 * depth * columns + 2 * NC * height * depth + 4 * NC * height * columns, transcendentals=0
        ),
        name=f"contract_{'sent' if across else 'kept'}_{len(before)}",
    )(*(mine[i] for i in used), *(other[i] for i in used), high, low, *before)


def on_device(amplitudes, driver, pair_energy, virt_energy, integrals, src_block, dst_block):
    tile_width = integrals.shape[1]
    local_blocks = virt_energy.shape[0] // tile_width
    blocks, half = NZ * NY * local_blocks, local_blocks // NC
    cut = half * tile_width

    def build():
        return sum_tiles(integrals, src_block, dst_block, local_blocks, blocks, amplitudes.shape[0])

    for iteration in range(ITERS):
        if iteration == 0:
            mine, (total, given, which) = gather_panel(over_z(amplitudes), parts_of, build)
            high, low = split_parts(total, over_core(given), half)
            lower = which == 0
            terms = jnp.stack([driver, virt_energy[None, :] - pair_energy[:, None]])
            kept_terms = jnp.where(lower, terms[..., :cut], terms[..., cut:])
            given_terms = jnp.where(lower, terms[..., cut:], terms[..., :cut])
            both_terms = jnp.stack([kept_terms, over_core(given_terms)], axis=1)
        else:
            mine, _ = gather_panel(over_z(shard), lambda parts: parts)
        *early, last = mine
        other = [over_core(piece) for piece in early]
        begun = contract(early, other, high, low, iteration == 0, 1, [0])
        mine, other = [*early, last], [*other, over_core(last)]
        sent = contract(mine, other, high, low, iteration == 0, 1, [1], [begun], True)
        kept = contract(mine, other, high, low, iteration == 0, 0)
        if iteration < ITERS - 1:
            shard = ((both_terms[0] + (kept + sums_of(over_x(sent.astype(jnp.float16))))) / both_terms[1]).astype(jnp.bfloat16)
    sent = sent.astype(jnp.float16)
    got_there, got_here = over_diagonal(sent[1]), over_x(sent[0])
    got_there, kept = lax.optimization_barrier((got_there, kept))
    got_here, kept_there = lax.optimization_barrier((got_here, over_core(kept[1])))
    here, there = kept[0] + sums_of(got_here), kept_there + sums_of(got_there)
    ladder = jnp.concatenate([jnp.where(lower, here, there), jnp.where(lower, there, here)], axis=1)
    return ((driver + ladder) / (virt_energy[None, :] - pair_energy[:, None])).astype(jnp.bfloat16)


def solution(mesh):
    form = on_device if (mesh.shape["tile"], mesh.shape["grp"]) == (NZ * NY, NX * NC) else general_form
    return jax.shard_map(
        form,
        mesh=mesh,
        in_specs=(
            P("grp", "tile"),
            P("grp", "tile"),
            P("grp"),
            P("tile"),
            P(("tile", "grp"), None, None),
            P("tile"),
            P("tile"),
        ),
        out_specs=P("grp", "tile"),
        check_vma=False,
    )
```

```python
import functools
import math

import jax
import jax.numpy as jnp
from jax import lax
from jax.experimental import pallas as pl
from jax.experimental.pallas import tpu as pltpu
from jax.sharding import PartitionSpec as P

ITERS = 2
MIB = 1024 * 1024


def contract_blocks(amp_rows, tile_set, source, target, local_blocks):
    row_count = amp_rows.shape[0]
    tile_width = tile_set.shape[1]
    tile_count = tile_set.shape[0]
    group_size = math.gcd(tile_count, 48)
    turns = tile_count // group_size
    blocks = amp_rows.reshape(row_count, -1, tile_width)
    packed_tiles = tile_set.reshape(turns, group_size, tile_width, tile_width)
    packed_source = source.reshape(turns, group_size)
    packed_target = target.reshape(turns, group_size)

    def advance(total_sum, packed):
        picked = jnp.take(blocks, packed[1], axis=1)
        partial_value = jnp.einsum(
            "rgc,gcd->rgd", picked, packed[0], preferred_element_type=jnp.float32
        )
        pieces = []
        for block in range(local_blocks):
            chosen = (packed[2] == block)[None, :, None]
            pieces.append(jnp.sum(jnp.where(chosen, partial_value, 0.0), axis=1))
        return (total_sum + jnp.stack(pieces, axis=1), None)

    initial = jnp.zeros((row_count, local_blocks, tile_width), jnp.float32)
    total_sum, unused = lax.scan(advance, initial, (packed_tiles, packed_source, packed_target))
    return total_sum.reshape(row_count, local_blocks * tile_width)


def general_form(amplitudes, driver, pair_energy, virt_energy, integrals, src_block, dst_block):
    tile_width = integrals.shape[1]
    local_blocks = virt_energy.shape[0] // tile_width
    denominator = virt_energy[None, :] - pair_energy[:, None]
    current = amplitudes
    first_tile = lax.axis_index("grp") * integrals.shape[0]
    my_source = lax.dynamic_slice_in_dim(src_block, first_tile, integrals.shape[0])
    my_target = lax.dynamic_slice_in_dim(dst_block, first_tile, integrals.shape[0])
    for iteration in range(ITERS):
        all_pairs = lax.all_gather(current, "grp", axis=0, tiled=True)
        whole_panel = lax.all_gather(all_pairs, "tile", axis=1, tiled=True)
        partial_value = contract_blocks(whole_panel, integrals, my_source, my_target, local_blocks)
        ladder = lax.psum_scatter(partial_value, "grp", scatter_dimension=0, tiled=True)
        current = ((driver + ladder) / denominator).astype(jnp.bfloat16)
    return current


NZ, NY, NX, NC = 4, 2, 2, 2
PARTS = 2
SCALED = 14
EXTRA = 16


def z_swap(away):
    return [(t, t ^ (away * NY)) for t in range(NZ * NY)]


Y_SWAP = [(t, t ^ 1) for t in range(NZ * NY)]
X_SWAP = [(g, g ^ 2) for g in range(NX * NC)]
CORE_SWAP = [(g, g ^ 1) for g in range(NX * NC)]
DIAGONAL_SWAP = [(g, g ^ 3) for g in range(NX * NC)]


def over_y(value):
    return lax.ppermute(value, "tile", Y_SWAP)


def over_x(value):
    return lax.ppermute(value, "grp", X_SWAP)


def over_core(value):
    return lax.ppermute(value, "grp", CORE_SWAP)


def over_diagonal(value):
    return lax.ppermute(value, "grp", DIAGONAL_SWAP)


def parts_of(rows):
    return jnp.stack(jnp.split(rows, PARTS, axis=1))


def over_z(value):
    far = [lax.ppermute(value, "tile", z_swap(away)) for away in range(NZ // 2, NZ)]
    return [value] + [lax.ppermute(value, "tile", z_swap(away)) for away in range(1, NZ // 2)] + far


def gather_panel(shards, parts, build=None):
    built = [] if build is None else list(build())
    if build is not None:
        shards, built = lax.optimization_barrier((shards, built))
    a = jnp.stack([parts(shard) for shard in shards[: NZ // 2]])
    b = jnp.stack([parts(shard) for shard in shards[NZ // 2 :]])
    a_y, a_x = over_y(a), over_x(a)
    if build is not None:
        b_x, b_y, a_xy = over_x(b), over_y(b), over_x(a_y)
        b_xy = over_y(b_x)
        a_x, a_xy = lax.optimization_barrier((a_x, a_xy))
        b_y, b_xy = lax.optimization_barrier((b_y, b_xy))
        return [jnp.stack(pair) for pair in ((a, b), (a_y, b_x), (a_x, b_y), (a_xy, b_xy))], built
    b, a_y = lax.optimization_barrier((b, a_y))
    b_x, b_y, a_xy = over_x(b), over_y(b), over_x(a_y)
    b_x, a_x = lax.optimization_barrier((b_x, a_x))
    a_xy, b_xy, b_y = lax.optimization_barrier((a_xy, over_y(b_x), b_y))
    return [jnp.stack(group) for group in ((a, b, b_y), (a_y, a_x, b_x), (a_xy, b_xy))], built


PLACES = (
    {(0, 0, 0): (0, 0), (1, 0, 0): (0, 1), (0, 1, 0): (1, 0), (1, 0, 1): (1, 1), (0, 0, 1): (2, 0), (1, 1, 0): (2, 1), (0, 1, 1): (3, 0), (1, 1, 1): (3, 1)},
    {(0, 0, 0): (0, 0), (1, 0, 0): (0, 1), (1, 1, 0): (0, 2), (0, 1, 0): (1, 0), (0, 0, 1): (1, 1), (1, 0, 1): (1, 2), (0, 1, 1): (2, 0), (1, 1, 1): (2, 1)},
)


def sum_kernel(chunk, local_blocks, src_any, dst_any, tiles_any, total, given, which, tiles, src, dst, list_sem, tile_sem):
    steps = tiles.shape[0] // chunk
    half = local_blocks // NC
    shift = half.bit_length() - 1
    slots = given.shape[0]
    lists = [pltpu.make_async_copy(a, b, list_sem.at[i]) for i, (a, b) in enumerate(((src_any, src), (dst_any, dst)))]
    for copy in lists:
        copy.start()

    def tile_copy(step):
        part = pl.ds(step * chunk, chunk)
        return pltpu.make_async_copy(tiles_any.at[part], tiles.at[part], tile_sem.at[step])

    for step in range(steps):
        tile_copy(step).start()

    def clear(slot, carry):
        total[slot] = jnp.zeros(total.shape[1:], jnp.float32)
        return carry

    lax.fori_loop(0, total.shape[0], clear, 0, unroll=4)
    for copy in lists:
        copy.wait()
    grp = lax.axis_index("grp")
    here = lax.axis_index("tile") * local_blocks
    core = lax.rem(grp, NC)
    which[...] = jnp.full(which.shape, core, jnp.int32)
    kept = core * half
    first = grp * tiles.shape[0]

    def run(step, carry):
        tile_copy(step).wait()

        def add(j, carry):
            k = step * chunk + j
            target = dst[first + k] ^ kept
            slot = (target >> shift) * slots + ((src[first + k] ^ here) << shift) + (target & (half - 1))
            total[slot] += tiles[k].astype(jnp.float32)
            return carry

        lax.fori_loop(0, chunk, add, 0, unroll=8)
        return carry

    lax.fori_loop(0, steps, run, 0)

    def give(slot, carry):
        given[slot] = total[slots + slot]
        return carry

    lax.fori_loop(0, slots, give, 0, unroll=4)


def sum_tiles(integrals, src_block, dst_block, local_blocks, blocks, rows):
    count, width, _ = integrals.shape
    slots = blocks * local_blocks // NC
    chunk = math.gcd(count, 24)
    outside = pl.BlockSpec(memory_space=pl.ANY)
    local = pl.BlockSpec(memory_space=pltpu.VMEM)
    return pl.pallas_call(
        functools.partial(sum_kernel, chunk, local_blocks),
        in_specs=[outside] * 3,
        out_specs=[local] * 3,
        out_shape=[
            pltpu.VMEM((NC * slots, width, width), jnp.float32),
            pltpu.VMEM((slots, width, width), jnp.float32),
            pltpu.VMEM((rows, local_blocks // NC * width), jnp.int32),
        ],
        scratch_shapes=[
            pltpu.VMEM(integrals.shape, jnp.bfloat16),
            pltpu.SMEM(src_block.shape, jnp.int32),
            pltpu.SMEM(dst_block.shape, jnp.int32),
            pltpu.SemaphoreType.DMA((2,)),
            pltpu.SemaphoreType.DMA((count // chunk,)),
        ],
        compiler_params=pltpu.CompilerParams(vmem_limit_bytes=24 * MIB),
        cost_estimate=pl.CostEstimate(
            flops=count * width * width, bytes_accessed=2 * count * width * width + 4 * slots * width * width, transcendentals=0
        ),
        name="sum_tiles",
    )(*(pltpu.with_memory_space_constraint(a, pltpu.HBM) for a in (src_block, dst_block, integrals)))


def split_kernel(half, mine, got, high, low):
    width = mine.shape[-1]

    def split(block, carry):
        for d in range(half):
            value = mine[block * half + d] + got[block * half + d]
            top = value.astype(jnp.bfloat16)
            rest = value - top.astype(jnp.float32)
            high[block, :, d * width : (d + 1) * width] = top
            low[block, :, d * width : (d + 1) * width] = rest.astype(jnp.bfloat16)
        return carry

    lax.fori_loop(0, got.shape[0] // half, split, 0)


def split_parts(mine, got, half):
    slots, width, _ = got.shape
    shape = pltpu.VMEM((slots // half, width, half * width), jnp.bfloat16)
    local = pl.BlockSpec(memory_space=pltpu.VMEM)
    high, low = pl.pallas_call(
        functools.partial(split_kernel, half),
        in_specs=[local, local],
        out_specs=[local, local],
        out_shape=[shape, shape],
        compiler_params=pltpu.CompilerParams(vmem_limit_bytes=24 * MIB),
        cost_estimate=pl.CostEstimate(flops=3 * got.size, bytes_accessed=12 * got.size, transcendentals=0),
        name="split_parts",
    )(*(pltpu.with_memory_space_constraint(a, pltpu.VMEM) for a in (mine, got)))
    return high.reshape(-1, half * width), low.reshape(-1, half * width)


def contract_kernel(by_core, across, along, used, scaled, *refs):
    mine, other = (dict(zip(used, part)) for part in (refs[: len(used)], refs[len(used) : 2 * len(used)]))
    high, low, *before, out, rows = refs[2 * len(used) :]
    height, depth = next(iter(mine.values())).shape[-2:]
    wide = PARTS * depth
    core = lax.rem(lax.axis_index("grp"), NC)
    spans = [(z, y) for z in range(NZ) for y in along]
    for away, pieces in enumerate((mine, other)):
        for part in range(PARTS):
            row = (away if by_core else part ^ away) * height
            half = part if by_core else (core if away == 0 else 1 - core)
            for span, (z, y) in enumerate(spans):
                piece, index = PLACES[not by_core][z // (NZ // 2), y, across]
                column = span * wide + half * depth
                if not by_core:
                    column = pl.multiple_of(column, depth)
                rows[row : row + height, pl.ds(column, depth)] = pieces[piece][index, z % (NZ // 2), part]
    total = sum(ref[...].reshape(NC * height, -1) for ref in before)
    if len(along) == NY:
        chunks = [(rows[...], slice(None))]
    else:
        chunks = [(rows[:, i * wide : (i + 1) * wide], pl.ds((z * NY + y) * wide, wide)) for i, (z, y) in enumerate(spans)]
    for left, right in chunks:
        for matrix in (high, low):
            total += jnp.dot(left, matrix[right, :], preferred_element_type=jnp.float32)
    if scaled:
        most = jnp.clip(jnp.max(jnp.abs(total), keepdims=True), 1e-30, 1e30)
        exponent = jnp.ceil(jnp.log2(most))
        total *= jnp.exp2(SCALED - exponent)
        exponents = jnp.broadcast_to(exponent, (EXTRA, total.shape[1]))
        if len(out.shape) == 2:
            out[: NC * height] = total
            out[NC * height :] = exponents
        else:
            for core in range(NC):
                out[core, :height] = total[core * height : (core + 1) * height]
                out[core, height:] = exponents
    else:
        for core in range(NC):
            out[core] = total[core * height : (core + 1) * height]


def sums_of(got):
    got = got.astype(jnp.float32)
    rows = got.shape[-2] - EXTRA
    return got[..., :rows, :] * jnp.exp2(got[..., rows : rows + 1, :] - SCALED)


def contract(mine, other, high, low, by_core, across, along=range(NY), before=(), scaled=0):
    used = sorted({PLACES[not by_core][half, y, across][0] for half in range(2) for y in along})
    height = mine[0].shape[-2]
    depth, columns = high.shape
    depth = depth // NY * len(along)
    shape = {0: (NC, height, columns), 1: (NC * height + EXTRA, columns), 2: (NC, height + EXTRA, columns)}[scaled]
    local = pl.BlockSpec(memory_space=pltpu.VMEM)
    return pl.pallas_call(
        functools.partial(contract_kernel, by_core, across, tuple(along), used, scaled),
        in_specs=[local] * (2 * len(used) + 2 + len(before)),
        out_specs=local,
        out_shape=jax.ShapeDtypeStruct(shape, jnp.float32),
        scratch_shapes=[pltpu.VMEM((NC * height, depth), jnp.bfloat16)],
        compiler_params=pltpu.CompilerParams(vmem_limit_bytes=24 * MIB),
        cost_estimate=pl.CostEstimate(
            flops=4 * NC * height * depth * columns, bytes_accessed=4 * depth * columns + 2 * NC * height * depth + 4 * NC * height * columns, transcendentals=0
        ),
        name=f"contract_{'sent' if across else 'kept'}_{len(before)}",
    )(*(mine[i] for i in used), *(other[i] for i in used), high, low, *before)


def on_device(amplitudes, driver, pair_energy, virt_energy, integrals, src_block, dst_block):
    tile_width = integrals.shape[1]
    local_blocks = virt_energy.shape[0] // tile_width
    blocks, half = NZ * NY * local_blocks, local_blocks // NC
    cut = half * tile_width

    def build():
        return sum_tiles(integrals, src_block, dst_block, local_blocks, blocks, amplitudes.shape[0])

    for iteration in range(ITERS):
        if iteration == 0:
            mine, (total, given, which) = gather_panel(over_z(amplitudes), parts_of, build)
            high, low = split_parts(total, over_core(given), half)
            lower = which == 0
            terms = jnp.stack([driver, virt_energy[None, :] - pair_energy[:, None]])
            kept_terms = jnp.where(lower, terms[..., :cut], terms[..., cut:])
            given_terms = jnp.where(lower, terms[..., cut:], terms[..., :cut])
            both_terms = jnp.stack([kept_terms, over_core(given_terms)], axis=1)
        else:
            mine, _ = gather_panel(over_z(shard), lambda parts: parts)
        *early, last = mine
        other = [over_core(piece) for piece in early]
        begun = contract(early, other, high, low, iteration == 0, 1, [0])
        mine, other = [*early, last], [*other, over_core(last)]
        sent = contract(mine, other, high, low, iteration == 0, 1, [1], [begun], 1 + iteration)
        kept = contract(mine, other, high, low, iteration == 0, 0)
        if iteration < ITERS - 1:
            shard = ((both_terms[0] + (kept + sums_of(over_x(sent.astype(jnp.float16))).reshape(kept.shape))) / both_terms[1]).astype(jnp.bfloat16)
    sent = sent.astype(jnp.float16)
    got_there, got_here = over_diagonal(sent[1]), over_x(sent[0])
    got_there, kept = lax.optimization_barrier((got_there, kept))
    got_here, kept_there = lax.optimization_barrier((got_here, over_core(kept[1])))
    here, there = kept[0] + sums_of(got_here), kept_there + sums_of(got_there)
    ladder = jnp.concatenate([jnp.where(lower, here, there), jnp.where(lower, there, here)], axis=1)
    return ((driver + ladder) / (virt_energy[None, :] - pair_energy[:, None])).astype(jnp.bfloat16)


def solution(mesh):
    form = on_device if (mesh.shape["tile"], mesh.shape["grp"]) == (NZ * NY, NX * NC) else general_form
    return jax.shard_map(
        form,
        mesh=mesh,
        in_specs=(
            P("grp", "tile"),
            P("grp", "tile"),
            P("grp"),
            P("tile"),
            P(("tile", "grp"), None, None),
            P("tile"),
            P("tile"),
        ),
        out_specs=P("grp", "tile"),
        check_vma=False,
    )
```
